256 devices in a mesh: clus: 4 (over x), trip: 32 (over y, z), mode: 2 (over core).
Axes of the slice: x: 4, y: 4, z: 8, core: 2. Of those that a mesh axis runs over, the one named last changes fastest.
Arguments:
- force_third: bfloat16 [8, 90, 8100], P('clus', 'mode'), may hold values from -0.0234375 to 0.0234375
- phase_angle: bfloat16 [8, 128], P('clus', 'trip'), may hold values from -3.140625 to 3.140625
- eigenvectors: bfloat16 [256, 90, 180], P('trip'), may hold values from -0.4375 to 0.4375
- frequencies: bfloat16 [256, 90], P('trip'), may hold values from 0.5 to 2
- deviation: bfloat16 [256, 90], P('trip'), may hold values from 0.5 to 2
- send_rows: int32 [32, 32], P('trip'), may hold values from 0 to 7
- trip_table: int32 [128, 3], P('trip'), may hold values from 0 to 31
- irreducible: int32 [128], P('trip'), may hold values from 0 to 31
- multiplicity: int32 [128], P('trip'), may hold values from 1 to 8
- drive_term: float32 [32, 90], P('trip', 'mode'), may hold values from -120 to 120
- boundary: float32 [32, 90], P('trip', 'mode'), may hold values from 5 to 40
Outputs:
- gamma_total: float32 [32, 90], P('trip', 'mode')
- new_deviation: float32 [32, 90], P('trip', 'mode')
The draws below stay inside these ranges and needn't reach their ends.
All inputs are finite; a program needn't handle non-finite values.
Results may differ from the reference program's by a relative error of at most 0.00095.
Values may be sent and summed in bfloat16 or wider, within the bound.
No kernel may reach another device: no remote copies, remote signals or barrier semaphores. Data moves between devices by JAX's collectives and lax.ppermute only.
A program may use at most 64 MiB of HBM per device.

```python
import math
import jax
import jax.numpy as jnp
from jax import lax

M = 90
CL_DEV = 2
G_DEV = 8
RECV = 32
NR = 8
TT = 4
TRIPLETS = 128
NG = 256
NQ = 32
SLOT = 1
N_CLUS = 4
N_TRIP = 32


def with_ends(values, rng, smallest, top_value):
    dims = values.shape
    index_at = [jax.random.randint(jax.random.fold_in(rng, axis), (), 0, dims[axis]) for axis in range(len(dims))]
    values = values.at[tuple(index_at)].set(smallest)
    longest = dims.index(max(dims))
    index_at[longest] = (index_at[longest] + 1) % dims[longest]
    return values.at[tuple(index_at)].set(top_value)


def levels(own_key, extent, pieces, least, largest):
    def one(position, blocks):
        draws = jax.random.uniform(jax.random.fold_in(jax.random.fold_in(own_key, 6), position), (blocks,), jnp.float32, least / len(pieces), largest / len(pieces))
        return jnp.repeat(jnp.exp(draws), extent[position] // blocks).reshape((-1,) + (1,) * (len(extent) - position - 1))

    factor_of = one(*pieces[0])
    for cut in pieces[1:]:
        factor_of = factor_of * one(*cut)
    return factor_of


def bell_draw(key, extent, scale, bound, cuts=(), kind=jnp.bfloat16):
    result = jax.random.normal(key, extent, jnp.float32) * scale
    if len(cuts) > 0:
        result = levels(key, extent, cuts, -0.22, 0.18) * result
    return jnp.clip(result, min=-bound, max=bound).astype(kind)


def setup_inputs(seed: int = 0) -> dict:
    seeds = jax.random.split(jax.random.key(seed), 12)
    force_third = bell_draw(seeds[0], (NR, M, M * M), (M * M * NR) ** -0.5, 0.0234375, ((0, 4), (1, 2)))
    phase_angle = jnp.clip(jax.random.uniform(seeds[1], (NR, TRIPLETS), jnp.float32, -3.140625, 3.140625), -3.140625, 3.140625).astype(jnp.bfloat16)
    eigenvectors = bell_draw(seeds[2], (NG, M, 2 * M), (2 * M) ** -0.5, 0.4375, ((0, 32),))
    frequencies = jnp.clip(jnp.exp(math.log(2.0) - 1.3862944 * jax.random.uniform(seeds[3], (NG, M), jnp.float32) ** levels(seeds[3], (NG, M), ((0, 32),), -0.2, 0.2)), 0.5, 2.0).astype(jnp.bfloat16)
    deviation = jnp.clip(0.5 + 1.5 * jax.random.uniform(seeds[4], (NG, M), jnp.float32) ** levels(seeds[4], (NG, M), ((0, 32),), -0.2, 0.2), 0.5, 2.0).astype(jnp.bfloat16)
    send_rows = with_ends(jax.random.randint(seeds[5], (N_TRIP, RECV), 0, G_DEV), jax.random.fold_in(seeds[5], 1), 0, G_DEV - 1).astype(jnp.int32)
    trip_table = with_ends(jax.random.randint(seeds[6], (TRIPLETS, 3), 0, RECV), jax.random.fold_in(seeds[6], 1), 0, RECV - 1).astype(jnp.int32)
    irreducible = with_ends(jax.random.randint(seeds[7], (TRIPLETS,), 0, NQ), jax.random.fold_in(seeds[7], 1), 0, NQ - 1).astype(jnp.int32)
    multiplicity = with_ends(jax.random.randint(seeds[8], (TRIPLETS,), 1, 9), jax.random.fold_in(seeds[8], 1), 1, 8).astype(jnp.int32)
    drive_term = bell_draw(seeds[9], (NQ, M), 20.0, 120.0, ((0, 32), (1, 2)), jnp.float32)
    boundary = jnp.clip(jnp.exp(math.log(40.0) - 2.0794415 * jax.random.uniform(seeds[10], (NQ, M), jnp.float32) ** levels(seeds[10], (NQ, M), ((0, 32), (1, 2)), -0.2, 0.2)), 5.0, 40.0)
    return dict(force_third=force_third, phase_angle=phase_angle, eigenvectors=eigenvectors, frequencies=frequencies, deviation=deviation, send_rows=send_rows, trip_table=trip_table, irreducible=irreducible, multiplicity=multiplicity, drive_term=drive_term, boundary=boundary)


smearing = 0.3
highest = lax.Precision.HIGHEST


def rounded(values):
    return lax.optimization_barrier(values.astype(jnp.bfloat16)).astype(jnp.float32)


def gaussian_weights(freq_zero, freq_one, freq_two):
    decays = freq_zero - freq_one - freq_two
    merges = freq_zero + freq_one - freq_two
    scaled = 0.5 / (smearing * smearing)
    return (jnp.exp(-scaled * decays * decays) + jnp.exp(-scaled * merges * merges)) / (freq_zero * freq_one * freq_two)


def combine(by_real, by_imag, mode_count):
    return jnp.concatenate([by_real[..., :mode_count] - by_imag[..., mode_count:], by_real[..., mode_count:] + by_imag[..., :mode_count]], axis=-1)


def interaction(transform, vectors):
    mode_count = vectors.shape[1]
    real_part = transform[0].reshape(-1, mode_count)
    imag_part = transform[1].reshape(-1, mode_count)
    last_vec = vectors[2]
    flipped = jnp.concatenate([-last_vec[:, mode_count:], last_vec[:, :mode_count]], axis=1)
    section_one = jnp.dot(real_part, last_vec, precision=highest) + jnp.dot(imag_part, flipped, precision=highest)
    section_one = rounded(section_one).reshape(mode_count, mode_count, 2 * mode_count)
    middle = vectors[1]
    section_two = rounded(combine(jnp.einsum("abk,bj->ajk", section_one, middle[:, :mode_count], precision=highest), jnp.einsum("abk,bj->ajk", section_one, middle[:, mode_count:], precision=highest), mode_count))
    leading = vectors[0]
    return combine(jnp.einsum("as,ajk->sjk", leading[:, :mode_count], section_two, precision=highest), jnp.einsum("as,ajk->sjk", leading[:, mode_count:], section_two, precision=highest), mode_count)


def reference(force_third, phase_angle, eigenvectors, frequencies, deviation, send_rows, trip_table, irreducible, multiplicity, drive_term, boundary):
    clusters = force_third.astype(jnp.float32).reshape(N_CLUS, CL_DEV, M * M * M)
    triplets = jnp.arange(TRIPLETS, dtype=jnp.int32)
    owners = triplets // TT
    sources = trip_table // SLOT
    within = trip_table % SLOT
    grid_points = sources * G_DEV + send_rows[sources, owners[:, None] * SLOT + within]
    vectors_all = eigenvectors.astype(jnp.float32)
    freq_all = frequencies.astype(jnp.float32)
    occupied_all = deviation.astype(jnp.float32)

    def one_triplet(triplet):
        angles = phase_angle[:, triplet].astype(jnp.float32).reshape(N_CLUS, CL_DEV)
        cosines = rounded(jnp.cos(angles))
        sines = rounded(jnp.sin(angles))
        real_sum = rounded(jnp.sum(rounded(jnp.einsum("gr,grx->gx", cosines, clusters, precision=highest)), axis=0))
        imag_sum = rounded(jnp.sum(rounded(jnp.einsum("gr,grx->gx", sines, clusters, precision=highest)), axis=0))
        transform = jnp.stack([real_sum, imag_sum]).reshape(2, M, M * M)
        members = grid_points[triplet]
        amplitude = interaction(transform, vectors_all[members])
        squared = amplitude[..., :M] ** 2 + amplitude[..., M:] ** 2
        rates = freq_all[members]
        weights = squared * gaussian_weights(rates[0][:, None, None], rates[1][None, :, None], rates[2][None, None, :]) * multiplicity[triplet].astype(jnp.float32)
        occupied = occupied_all[members]
        totals = jnp.sum(weights, axis=(1, 2))
        couples = jnp.einsum("sjk,j->s", weights, occupied[1], precision=highest) + jnp.einsum("sjk,k->s", weights, occupied[2], precision=highest)
        return totals, couples

    totals, couples = lax.map(one_triplet, triplets)
    onehot = (irreducible[:, None] == jnp.arange(NQ, dtype=jnp.int32)[None, :]).astype(jnp.float32)
    rate = jnp.dot(onehot.T, totals, precision=highest)
    coupled = jnp.dot(onehot.T, couples, precision=highest)
    gamma_total = rate + boundary
    return gamma_total, (drive_term + coupled) / gamma_total
```

```python
import jax
import jax.numpy as jnp
from jax import lax
from jax.experimental import pallas as pl
from jax.experimental.pallas import tpu as pltpu
from jax.sharding import PartitionSpec as P

smearing = 0.3
SPLIT = 4096
LANES = 256
RING_Y = 4
RING_Z = 8
PAD = 48
WIDE = 96


def send_kernel(rows_ref, share_ref, out_ref):
    for target in range(out_ref.shape[0]):
        out_ref[target] = share_ref[rows_ref[0, target]]


def pick_kernel(table_ref, arrived_ref, phase_ref, out_ref):
    for triplet in range(4):
        for member in range(3):
            block = arrived_ref[table_ref[triplet, member]]
            out_ref[2 * triplet, member] = block
            out_ref[2 * triplet + 1, member] = block
        out_ref[2 * triplet, 3] = phase_ref[triplet]
        out_ref[2 * triplet + 1, 3] = phase_ref[triplet]


def transform_kernel(where_ref, trig_ref, own_ref, *refs):
    out_ref = refs[-1]
    rank = where_ref[0]
    color = where_ref[1]
    pieces = [
        (3, True, refs[0], refs[1]),
        (1, True, refs[2], refs[3]),
        (3, False, refs[4], refs[5]),
        (1, False, refs[6], refs[7]),
        (2, True, refs[8], refs[9]),
        (2, False, refs[10], refs[11]),
    ]
    factors = []
    for offset, same, _, _ in pieces:
        which = color if same else 1 - color
        at = 2 * (2 * ((rank + offset) & 3) + which)
        factors.append((trig_ref[at], trig_ref[at + 1]))
    own = [(trig_ref[4 * rank + 2 * r], trig_ref[4 * rank + 2 * r + 1]) for r in range(2)]
    out_ref[:, 45:PAD, :] = jnp.zeros((2, PAD - 45, out_ref.shape[2]), out_ref.dtype)

    def chunk(half, start, width):
        whole = start + half * SPLIT
        if not isinstance(start, int):
            whole = pl.multiple_of(whole, LANES)
            start = pl.multiple_of(start, LANES)
        real = imag = None
        for r in range(2):
            values = own_ref[r, :, pl.ds(whole, width)].astype(jnp.float32)
            real = own[r][0] * values if real is None else real + own[r][0] * values
            imag = own[r][1] * values if imag is None else imag + own[r][1] * values
        for (cosine, sine), piece in zip(factors, pieces):
            values = piece[2 + half][:, pl.ds(start, width)].astype(jnp.float32)
            real = real + cosine * values
            imag = imag + sine * values
        out_ref[0, 0:45, pl.ds(whole, width)] = real.astype(out_ref.dtype)
        out_ref[1, 0:45, pl.ds(whole, width)] = imag.astype(out_ref.dtype)

    total = own_ref.shape[2]
    for half, length in ((0, SPLIT), (1, total - SPLIT)):
        count = length // LANES

        @pl.loop(0, count)
        def _(i, half=half):
            chunk(half, i * LANES, LANES)

        if length % LANES:
            chunk(half, count * LANES, length % LANES)


def interaction_kernel(
    scalars_ref,
    lead_ref,
    middle_ref,
    last_ref,
    tables_ref,
    mine_ref,
    other_ref,
    out_ref,
    flat,
    windows,
    mid_real,
    mid_imag,
    rate_acc,
    couple_acc,
):
    total = mine_ref.shape[2]
    flat[:, 8064:8320] = jnp.zeros((2 * PAD, 256), flat.dtype)
    for start in range(0, total, 1024):
        width = min(1024, total - start)
        cols = pl.ds(start, width)
        stacked = jnp.concatenate(
            [mine_ref[0, :, cols], mine_ref[1, :, cols], other_ref[0, :, cols], other_ref[1, :, cols]],
            axis=0,
        )
        flat[:, cols] = jnp.dot(
            lead_ref[...], stacked, preferred_element_type=jnp.float32
        ).astype(flat.dtype)
    for b in range(90):
        tile, shift = divmod(90 * b, 128)
        pair = flat[:, tile * 128 : tile * 128 + 256]
        window = pair[:, shift : shift + 128]
        windows[b * PAD : (b + 1) * PAD, 0:128] = window[0:PAD]
        windows[b * PAD : (b + 1) * PAD, 128:256] = window[PAD:]
    zeros = jnp.zeros((PAD, 128), jnp.float32)
    for b in range(90, WIDE):
        mid_real[pl.ds(b, PAD, stride=WIDE), :] = zeros
        mid_imag[pl.ds(b, PAD, stride=WIDE), :] = zeros
    for group in range(9):
        product = jnp.dot(
            windows[group * 480 : (group + 1) * 480, :],
            last_ref[...],
            preferred_element_type=jnp.float32,
        )
        for i in range(10):
            rows = pl.ds(group * 10 + i, PAD, stride=WIDE)
            mid_real[rows, :] = product[i * PAD : (i + 1) * PAD, 0:128]
            mid_imag[rows, :] = product[i * PAD : (i + 1) * PAD, 128:256]

    scaled = 0.5 / (smearing * smearing)
    tail = jnp.zeros((8 * (PAD - 45), 128), jnp.float32)
    rate_acc[8 * 45 :, :] = tail
    couple_acc[8 * 45 :, :] = tail

    def one_mode(s):
        rows = pl.ds(pl.multiple_of(s * WIDE, WIDE), WIDE)
        operand = jnp.concatenate([mid_real[rows, :], mid_imag[rows, :]], axis=0)
        value = jnp.dot(
            middle_ref[...], operand.astype(jnp.bfloat16), preferred_element_type=jnp.float32
        )
        real = value[0:WIDE]
        imag = value[WIDE:]
        freq = scalars_ref[0, s]
        decays = freq - tables_ref[0]
        merges = freq + tables_ref[1]
        weight = (real * real + imag * imag) * (
            jnp.exp(-scaled * decays * decays) + jnp.exp(-scaled * merges * merges)
        )
        weight = weight * tables_ref[2] * scalars_ref[1, s]
        at = pl.ds(pl.multiple_of(s * 8, 8), 8)
        rate_acc[at, :] = jnp.sum(weight.reshape(WIDE // 8, 8, 128), axis=0)
        couple_acc[at, :] = jnp.sum((weight * tables_ref[3]).reshape(WIDE // 8, 8, 128), axis=0)

    @pl.loop(0, 15)
    def _(i):
        for j in range(3):
            one_mode(3 * i + j)

    sums = jnp.concatenate(
        [
            jnp.sum(rate_acc[...].reshape(PAD, 8, 128), axis=1),
            jnp.sum(couple_acc[...].reshape(PAD, 8, 128), axis=1),
        ],
        axis=0,
    )
    out_ref[:, 0:WIDE] = lax.dot_general(
        jnp.ones((8, 128), jnp.float32),
        sums,
        (((1,), (1,)), ((), ())),
        precision=lax.Precision.HIGHEST,
        preferred_element_type=jnp.float32,
    )
    out_ref[:, WIDE:128] = jnp.zeros((8, 128 - WIDE), jnp.float32)


VMEM = pl.BlockSpec(memory_space=pltpu.VMEM)
SMEM = pl.BlockSpec(memory_space=pltpu.SMEM)


def ring(count, step):
    return [(i, (i + step) % count) for i in range(count)]


def grid_shift(step_y, step_z):
    return [
        (y * RING_Z + z, (y + step_y) % RING_Y * RING_Z + (z + step_z) % RING_Z)
        for y in range(RING_Y)
        for z in range(RING_Z)
    ]


def pad_to(array, rows, cols):
    return jnp.pad(array, ((0, rows - array.shape[0]), (0, cols - array.shape[1])))


def body(
    force_third,
    phase_angle,
    eigenvectors,
    frequencies,
    deviation,
    send_rows,
    trip_table,
    irreducible,
    multiplicity,
    drive_term,
    boundary,
):
    f32, b16 = jnp.float32, jnp.bfloat16
    clus = lax.axis_index("clus")
    mode = lax.axis_index("mode")
    trip = lax.axis_index("trip")
    color = (trip // RING_Z + trip % RING_Z) % 2

    picked_force = lax.dynamic_index_in_dim(force_third, color, 0, keepdims=False)
    half0, half1 = picked_force[:, :SPLIT], picked_force[:, SPLIT:]
    up, down = ring(4, 1), ring(4, 3)
    with jax.named_scope("force_neighbours"):
        low0 = lax.ppermute(half0, "clus", up)
        high0 = lax.ppermute(half0, "clus", down)
        low1 = lax.ppermute(half1, "clus", up)
        high1 = lax.ppermute(half1, "clus", down)
    with jax.named_scope("force_second"):
        opp0 = lax.ppermute(low0, "clus", up)
        opp1 = lax.ppermute(high1, "clus", down)
        low_other0 = lax.ppermute(low0, "trip", grid_shift(1, 0))
        high_other0 = lax.ppermute(high0, "trip", grid_shift(0, 1))
        low_other1 = lax.ppermute(low1, "trip", grid_shift(-1, 0))
        high_other1 = lax.ppermute(high1, "trip", grid_shift(0, -1))
    with jax.named_scope("force_third_step"):
        opp_other0 = lax.ppermute(opp0, "trip", grid_shift(1, 0))
        opp_other1 = lax.ppermute(opp1, "trip", grid_shift(0, 1))

    with jax.named_scope("records"):
        extra = jnp.concatenate([frequencies, deviation], axis=1)[:, None, :]
        record = jnp.concatenate(
            [eigenvectors, extra, jnp.zeros((extra.shape[0], 5, 180), b16)], axis=1
        )
        share = lax.dynamic_slice_in_dim(record, 12 * (2 * clus + mode), 12, 1)
        chosen = pl.pallas_call(
            send_kernel,
            out_shape=jax.ShapeDtypeStruct((send_rows.shape[1],) + share.shape[1:], b16),
            in_specs=[SMEM, VMEM],
            out_specs=VMEM,
        )(send_rows, share)
        arrived = lax.all_to_all(chosen, "trip", 0, 0, tiled=True)
        angles = phase_angle.astype(f32)
        trig = jnp.stack([jnp.cos(angles), jnp.sin(angles)], axis=1).astype(b16)
        trig = trig.reshape(4, 4).T
        phases = jnp.pad(trig[:, None, :], ((0, 0), (0, 11), (0, 176)))
        outgoing = pl.pallas_call(
            pick_kernel,
            out_shape=jax.ShapeDtypeStruct((8, 4, 12, 180), b16),
            in_specs=[SMEM, VMEM, VMEM],
            out_specs=VMEM,
        )(trip_table, arrived, phases)
        members = lax.all_to_all(outgoing, ("clus", "mode"), 0, 0, tiled=True)
        factors = members[0::2, 3, 0, 0:4].astype(f32).reshape(16)
        blocks = jnp.transpose(members[:, :3], (1, 0, 2, 3)).reshape(3, 96, 180)
    with jax.named_scope("operands"):
        leading, middle, last = blocks[0, :90], blocks[1, :90], blocks[2, :90]
        freq = blocks[:, 90, :90].astype(f32)
        occupied = blocks[:, 90, 90:].astype(f32)

        def lead_part(row_rank):
            real = lax.dynamic_slice(leading, (45 * row_rank, 45 * mode), (45, 45)).T
            imag = lax.dynamic_slice(leading, (45 * row_rank, 90 + 45 * mode), (45, 45)).T
            real, imag = pad_to(real, PAD, PAD), pad_to(imag, PAD, PAD)
            return jnp.block([[real, -imag], [imag, real]])

        lead = jnp.concatenate([lead_part(mode), lead_part(1 - mode)], axis=1)
        mid_r, mid_i = pad_to(middle[:, :90].T, WIDE, WIDE), pad_to(middle[:, 90:].T, WIDE, WIDE)
        mid = jnp.block([[mid_r, -mid_i], [mid_i, mid_r]])
        last_r, last_i = pad_to(last[:, :90], 128, 128), pad_to(last[:, 90:], 128, 128)
        last_all = jnp.block([[last_r, last_i], [-last_i, last_r]])
        one = jnp.pad(freq[1], (0, 6), constant_values=1.0)[:, None]
        two = jnp.pad(freq[2], (0, 38), constant_values=1.0)[None, :]
        tables = jnp.stack(
            [
                one + two,
                one - two,
                1.0 / (one * two),
                jnp.pad(occupied[1], (0, 6))[:, None] + jnp.pad(occupied[2], (0, 38))[None, :],
            ]
        )
        zero = lax.dynamic_slice_in_dim(freq[0], 45 * mode, 45, 0)
        mult = lax.dynamic_index_in_dim(multiplicity, clus, 0, keepdims=False).astype(f32)
        scalars = jnp.stack([zero, mult / zero])
        where = jnp.stack([clus, color]).astype(jnp.int32)

    with jax.named_scope("transform"):
        mine = pl.pallas_call(
            transform_kernel,
            out_shape=jax.ShapeDtypeStruct((2, PAD, force_third.shape[2]), b16),
            in_specs=[SMEM, SMEM] + [VMEM] * 13,
            out_specs=VMEM,
            compiler_params=pltpu.CompilerParams(vmem_limit_bytes=48 << 20),
        )(
            where,
            factors,
            force_third,
            low0,
            low1,
            high0,
            high1,
            low_other0,
            low_other1,
            high_other0,
            high_other1,
            opp0,
            opp1,
            opp_other0,
            opp_other1,
        )
        other = lax.ppermute(mine, "mode", [(0, 1), (1, 0)])
    with jax.named_scope("interaction"):
        sums = pl.pallas_call(
            interaction_kernel,
            out_shape=jax.ShapeDtypeStruct((8, 128), f32),
            in_specs=[SMEM] + [VMEM] * 6,
            out_specs=VMEM,
            scratch_shapes=[
                pltpu.VMEM((2 * PAD, 8320), b16),
                pltpu.VMEM((90 * PAD, 256), b16),
                pltpu.VMEM((PAD * WIDE, 128), f32),
                pltpu.VMEM((PAD * WIDE, 128), f32),
                pltpu.VMEM((8 * PAD, 128), f32),
                pltpu.VMEM((8 * PAD, 128), f32),
            ],
            compiler_params=pltpu.CompilerParams(vmem_limit_bytes=48 << 20),
        )(scalars, lead, mid, last_all, tables, mine, other)
    with jax.named_scope("collect"):
        own_row = sums[0:1]
        rows = [own_row] + [lax.ppermute(own_row, "clus", ring(4, step)) for step in (1, 2, 3)]
        points = jnp.arange(32, dtype=jnp.int32)
        partial = jnp.zeros((32, 128), f32)
        for step in range(4):
            point = lax.dynamic_index_in_dim(irreducible, (clus - step) % 4, 0, keepdims=False)
            partial = partial + jnp.where((points == point)[:, None], rows[step], 0.0)
        received = lax.all_to_all(partial[:, None, :], "trip", 0, 0, tiled=True)
        final = jnp.sum(received[:, 0, :], axis=0)[None, :]
        gamma_total = final[:, 0:45] + boundary
        return gamma_total, (drive_term + final[:, PAD : PAD + 45]) / gamma_total


def solution(mesh):
    return jax.shard_map(
        body,
        mesh=mesh,
        in_specs=(
            P("clus", "mode", None),
            P("clus", "trip"),
            P("trip", None, None),
            P("trip", None),
            P("trip", None),
            P("trip", None),
            P("trip", None),
            P("trip"),
            P("trip"),
            P("trip", "mode"),
            P("trip", "mode"),
        ),
        out_specs=(P("trip", "mode"), P("trip", "mode")),
        check_vma=False,
    )
```

```python
import jax
import jax.numpy as jnp
from jax import lax
from jax.experimental import pallas as pl
from jax.experimental.pallas import tpu as pltpu
from jax.sharding import PartitionSpec as P

smearing = 0.3
SPLIT = 4096
LANES = 512
RING_Y = 4
RING_Z = 8
PAD = 48
WIDE = 96
PIECES = ((0, 0), (0, 1), (3, 0), (1, 0), (3, 1), (1, 1), (2, 0), (2, 1))


def send_kernel(rows_ref, share_ref, out_ref):
    for target in range(out_ref.shape[0]):
        out_ref[target] = share_ref[rows_ref[0, target]]


def pick_kernel(rank_ref, table_ref, arrived_ref, phase_ref, *out_refs):
    for offset, out_ref in enumerate(out_refs):
        triplet = (rank_ref[0] + offset) & 3
        for member in range(3):
            out_ref[member] = arrived_ref[table_ref[triplet, member]]
        out_ref[3] = phase_ref[triplet]


def operand_kernel(where_ref, *refs):
    members, refs = refs[:8], refs[8:]
    lead_ref, middle_ref, last_ref, tables_ref, scalars_ref, record = refs
    rank, mode, color, mult = where_ref[0], where_ref[1], where_ref[2], where_ref[3]
    f32 = jnp.float32
    record[...] = jnp.zeros(record.shape, f32)
    for source in range(8):
        block = 2 * ((rank - source // 2) & 3) + (mode if source % 2 == 0 else 1 - mode)
        rows = pl.ds(pl.multiple_of(16 * block, 16), 12)
        for member in range(3):
            values = members[source][member].astype(f32)
            record[member, rows, 0:90] = values[:, 0:90]
            record[member, rows, 128:218] = values[:, 90:180]
    records = [
        jnp.concatenate([record[member, 16 * j : 16 * j + 12, :] for j in range(8)], axis=0)
        for member in range(3)
    ]
    first = mode == 0

    def transposed(member):
        return records[member][:, 0:128].T, records[member][:, 128:256].T

    def halves(array):
        low, high = array[0:PAD], array[45 : 45 + PAD]
        return jnp.where(first, low, high), jnp.where(first, high, low)

    def own_columns(array):
        picked = jnp.where(first, array[:, 0:PAD], array[:, 45 : 45 + PAD])
        column = lax.broadcasted_iota(jnp.int32, picked.shape, 1)
        return jnp.where(column < 45, picked, 0.0)

    lead_r, lead_i = transposed(0)
    real_own, real_far = halves(own_columns(lead_r))
    imag_own, imag_far = halves(own_columns(lead_i))
    columns = []
    for offset, which in PIECES:
        trig = members[2 * ((4 - offset) % 4)][3].astype(f32)[0:1]
        pair = [trig[:, 0:1], trig[:, 1:2], trig[:, 2:3], trig[:, 3:4]]
        if offset == 0:
            cosine, sine = pair[2 * which], pair[2 * which + 1]
        else:
            early = color == which
            cosine = jnp.where(early, pair[0], pair[2])
            sine = jnp.where(early, pair[1], pair[3])
        columns.append(
            jnp.concatenate(
                [
                    cosine * real_own - sine * imag_own,
                    cosine * imag_own + sine * real_own,
                    cosine * real_far - sine * imag_far,
                    cosine * imag_far + sine * real_far,
                ],
                axis=0,
            )
        )
    lead_ref[...] = jnp.concatenate(columns, axis=1).astype(lead_ref.dtype)

    mid_r, mid_i = transposed(1)
    within = lax.broadcasted_iota(jnp.int32, (WIDE, WIDE), 1) < 90
    real = jnp.where(within, mid_r[0:WIDE], 0.0)
    imag = jnp.where(within, mid_i[0:WIDE], 0.0)
    middle_ref[...] = jnp.concatenate(
        [jnp.concatenate([real, -imag], axis=1), jnp.concatenate([imag, real], axis=1)], axis=0
    ).astype(middle_ref.dtype)

    last_r, last_i = records[2][:, 0:128], records[2][:, 128:256]
    within = lax.broadcasted_iota(jnp.int32, (WIDE, 128), 0) < 90
    real = jnp.where(within, last_r, 0.0)
    imag = jnp.where(within, last_i, 0.0)
    zeros = jnp.zeros((32, 256), f32)
    last_ref[...] = jnp.concatenate(
        [
            jnp.concatenate([real, imag], axis=1),
            zeros,
            jnp.concatenate([-imag, real], axis=1),
            zeros,
        ],
        axis=0,
    ).astype(last_ref.dtype)

    row = lax.broadcasted_iota(jnp.int32, (WIDE, 128), 0)
    column = lax.broadcasted_iota(jnp.int32, (WIDE, 128), 1)
    one = jnp.where(row < 90, jnp.broadcast_to(mid_r[0:WIDE, 90:91], (WIDE, 128)), 1.0)
    two = jnp.where(column < 90, jnp.broadcast_to(last_r[90:91, :], (WIDE, 128)), 1.0)
    tables_ref[0] = one + two
    tables_ref[1] = one - two
    tables_ref[2] = 1.0 / (one * two)
    tables_ref[3] = jnp.broadcast_to(mid_i[0:WIDE, 90:91], (WIDE, 128)) + jnp.broadcast_to(
        last_i[90:91, :], (WIDE, 128)
    )
    zero = halves(lead_r[:, 90:91])[0]
    zero = jnp.where(lax.broadcasted_iota(jnp.int32, (PAD, 1), 0) < 45, zero, 1.0)
    scalars_ref[0] = jnp.broadcast_to(zero, (PAD, 128))
    scalars_ref[1] = jnp.broadcast_to(mult.astype(f32) / zero, (PAD, 128))


def contract_kernel(lead_ref, own_ref, *refs):
    pieces, mine_ref, far_ref = refs[:-2], refs[-2], refs[-1]
    length = mine_ref.shape[1]
    begin = 0 if length == SPLIT else SPLIT

    def chunk(start, width):
        whole = start + begin
        if not isinstance(start, int):
            whole = pl.multiple_of(whole, LANES)
            start = pl.multiple_of(start, LANES)
        values = [own_ref[r, :, pl.ds(whole, width)] for r in range(2)]
        values += [piece[:, pl.ds(whole, width)] for piece in pieces[:2]]
        values += [piece[:, pl.ds(start, width)] for piece in pieces[2:]]
        rows = [jnp.pad(v, ((0, PAD - 45), (0, 0))) for v in values]
        product = jnp.dot(
            lead_ref[...], jnp.concatenate(rows, axis=0), preferred_element_type=jnp.float32
        ).astype(mine_ref.dtype)
        mine_ref[:, pl.ds(start, width)] = product[0 : 2 * PAD]
        far_ref[:, pl.ds(start, width)] = product[2 * PAD :]

    count = length // LANES

    @pl.loop(0, count)
    def _(i):
        chunk(i * LANES, LANES)

    if length % LANES:
        chunk(count * LANES, length % LANES)


def interaction_kernel(
    scalars_ref,
    middle_ref,
    last_ref,
    tables_ref,
    mine0_ref,
    other0_ref,
    mine1_ref,
    other1_ref,
    out_ref,
    flat,
    windows,
    mid_real,
    mid_imag,
    rate_acc,
    couple_acc,
):
    flat[:, 8064:8320] = jnp.zeros((2 * PAD, 256), flat.dtype)
    for begin, mine, other in ((0, mine0_ref, other0_ref), (SPLIT, mine1_ref, other1_ref)):
        for start in range(0, mine.shape[1], LANES):
            width = min(LANES, mine.shape[1] - start)
            cols = pl.ds(start, width)
            both = mine[:, cols].astype(jnp.float32) + other[:, cols].astype(jnp.float32)
            flat[:, begin + start : begin + start + width] = both.astype(flat.dtype)
    for b in range(90):
        tile, shift = divmod(90 * b, 128)
        pair = flat[:, tile * 128 : tile * 128 + 256]
        window = pair[:, shift : shift + 128]
        windows[b * PAD : (b + 1) * PAD, 0:128] = window[0:PAD]
        windows[b * PAD : (b + 1) * PAD, 128:256] = window[PAD:]
    zeros = jnp.zeros((PAD, 128), jnp.float32)
    for b in range(90, WIDE):
        mid_real[pl.ds(b, PAD, stride=WIDE), :] = zeros
        mid_imag[pl.ds(b, PAD, stride=WIDE), :] = zeros
    for group in range(9):
        product = jnp.dot(
            windows[group * 480 : (group + 1) * 480, :],
            last_ref[...],
            preferred_element_type=jnp.float32,
        )
        for i in range(10):
            rows = pl.ds(group * 10 + i, PAD, stride=WIDE)
            mid_real[rows, :] = product[i * PAD : (i + 1) * PAD, 0:128]
            mid_imag[rows, :] = product[i * PAD : (i + 1) * PAD, 128:256]

    scaled = 0.5 / (smearing * smearing)
    tail = jnp.zeros((8 * (PAD - 45), 128), jnp.float32)
    rate_acc[8 * 45 :, :] = tail
    couple_acc[8 * 45 :, :] = tail

    def one_mode(s):
        rows = pl.ds(pl.multiple_of(s * WIDE, WIDE), WIDE)
        operand = jnp.concatenate([mid_real[rows, :], mid_imag[rows, :]], axis=0)
        value = jnp.dot(
            middle_ref[...], operand.astype(jnp.bfloat16), preferred_element_type=jnp.float32
        )
        real = value[0:WIDE]
        imag = value[WIDE:]
        freq = scalars_ref[0, pl.ds(s, 1), :]
        decays = freq - tables_ref[0]
        merges = freq + tables_ref[1]
        weight = (real * real + imag * imag) * (
            jnp.exp(-scaled * decays * decays) + jnp.exp(-scaled * merges * merges)
        )
        weight = weight * tables_ref[2] * scalars_ref[1, pl.ds(s, 1), :]
        at = pl.ds(pl.multiple_of(s * 8, 8), 8)
        rate_acc[at, :] = jnp.sum(weight.reshape(WIDE // 8, 8, 128), axis=0)
        couple_acc[at, :] = jnp.sum((weight * tables_ref[3]).reshape(WIDE // 8, 8, 128), axis=0)

    @pl.loop(0, 15)
    def _(i):
        for j in range(3):
            one_mode(3 * i + j)

    sums = jnp.concatenate(
        [
            jnp.sum(rate_acc[...].reshape(PAD, 8, 128), axis=1),
            jnp.sum(couple_acc[...].reshape(PAD, 8, 128), axis=1),
        ],
        axis=0,
    )
    out_ref[:, 0:WIDE] = lax.dot_general(
        jnp.ones((8, 128), jnp.float32),
        sums,
        (((1,), (1,)), ((), ())),
        precision=lax.Precision.HIGHEST,
        preferred_element_type=jnp.float32,
    )
    out_ref[:, WIDE:128] = jnp.zeros((8, 128 - WIDE), jnp.float32)


VMEM = pl.BlockSpec(memory_space=pltpu.VMEM)
SMEM = pl.BlockSpec(memory_space=pltpu.SMEM)


def ring(count, step):
    return [(i, (i + step) % count) for i in range(count)]


def grid_shift(step_y, step_z):
    return [
        (y * RING_Z + z, (y + step_y) % RING_Y * RING_Z + (z + step_z) % RING_Z)
        for y in range(RING_Y)
        for z in range(RING_Z)
    ]


def body(
    force_third,
    phase_angle,
    eigenvectors,
    frequencies,
    deviation,
    send_rows,
    trip_table,
    irreducible,
    multiplicity,
    drive_term,
    boundary,
):
    f32, b16 = jnp.float32, jnp.bfloat16
    clus = lax.axis_index("clus")
    mode = lax.axis_index("mode")
    trip = lax.axis_index("trip")
    color = (trip // RING_Z + trip % RING_Z) % 2

    picked_force = lax.dynamic_index_in_dim(force_third, color, 0, keepdims=False)
    up, down = ring(4, 1), ring(4, 3)
    with jax.named_scope("force_neighbours"):
        low = lax.ppermute(picked_force, "clus", up)
        high = lax.ppermute(picked_force, "clus", down)

    with jax.named_scope("records"):
        extra = jnp.concatenate([frequencies, deviation], axis=1)[:, None, :]
        record = jnp.concatenate(
            [eigenvectors, extra, jnp.zeros((extra.shape[0], 5, 180), b16)], axis=1
        )
        share = lax.dynamic_slice_in_dim(record, 12 * (2 * clus + mode), 12, 1)
        chosen = pl.pallas_call(
            send_kernel,
            out_shape=jax.ShapeDtypeStruct((send_rows.shape[1],) + share.shape[1:], b16),
            in_specs=[SMEM, VMEM],
            out_specs=VMEM,
        )(send_rows, share)
        arrived = lax.all_to_all(chosen, "trip", 0, 0, tiled=True)
        angles = phase_angle.astype(f32)
        trig = jnp.stack([jnp.cos(angles), jnp.sin(angles)], axis=1).astype(b16)
        trig = trig.reshape(4, 4).T
        phases = jnp.pad(trig[:, None, :], ((0, 0), (0, 11), (0, 176)))
        picks = pl.pallas_call(
            pick_kernel,
            out_shape=(jax.ShapeDtypeStruct((4, 12, 180), b16),) * 4,
            in_specs=[SMEM, SMEM, VMEM, VMEM],
            out_specs=(VMEM,) * 4,
        )(clus.reshape(1).astype(jnp.int32), trip_table, arrived, phases)

    with jax.named_scope("force_second"):
        low, high, _ = lax.optimization_barrier((low, high, arrived))
        low0, low1 = low[:, :SPLIT], low[:, SPLIT:]
        high0, high1 = high[:, :SPLIT], high[:, SPLIT:]
        opp0 = lax.ppermute(low0, "clus", up)
        opp1 = lax.ppermute(high1, "clus", down)
        low_other0 = lax.ppermute(low0, "trip", grid_shift(1, 0))
        low_other1 = lax.ppermute(low1, "trip", grid_shift(-1, 0))
        high_other0 = lax.ppermute(high0, "trip", grid_shift(0, 1))
        high_other1 = lax.ppermute(high1, "trip", grid_shift(0, -1))
    with jax.named_scope("force_third_step"):
        opp_other0 = lax.ppermute(opp0, "trip", grid_shift(1, 0))
        opp_other1 = lax.ppermute(opp1, "trip", grid_shift(0, 1))

    with jax.named_scope("members"):
        swap = [(0, 1), (1, 0)]
        picks = lax.optimization_barrier(
            (*picks, opp0, opp1, low_other0, low_other1, high_other0, high_other1)
        )[:4]
        members = [picks[0]]
        for k in range(4):
            for far in (0, 1):
                if k or far:
                    step = [
                        (2 * c + m, (2 * c + 2 * k) % 8 + (m + far) % 2)
                        for c in range(4)
                        for m in range(2)
                    ]
                    members.append(lax.ppermute(picks[k], ("clus", "mode"), step))
    with jax.named_scope("operands"):
        mult = lax.dynamic_index_in_dim(multiplicity, clus, 0, keepdims=False)
        where = jnp.stack([clus, mode, color, mult]).astype(jnp.int32)
        lead, mid, last_all, tables, scalars = pl.pallas_call(
            operand_kernel,
            out_shape=(
                jax.ShapeDtypeStruct((4 * PAD, 8 * PAD), b16),
                jax.ShapeDtypeStruct((2 * WIDE, 2 * WIDE), b16),
                jax.ShapeDtypeStruct((256, 256), b16),
                jax.ShapeDtypeStruct((4, WIDE, 128), f32),
                jax.ShapeDtypeStruct((2, PAD, 128), f32),
            ),
            in_specs=[SMEM] + [VMEM] * 8,
            out_specs=(VMEM,) * 5,
            scratch_shapes=[pltpu.VMEM((3, 128, 256), f32)],
        )(where, *members)

    with jax.named_scope("contract"):
        own = lax.optimization_barrier((force_third, low))[0]
        products = []
        for parts in (
            (low_other0, high_other0, opp0, opp_other0),
            (low_other1, high_other1, opp1, opp_other1),
        ):
            length = parts[0].shape[1]
            mine, far = pl.pallas_call(
                contract_kernel,
                out_shape=(jax.ShapeDtypeStruct((2 * PAD, length), b16),) * 2,
                in_specs=[VMEM] * 8,
                out_specs=(VMEM, VMEM),
                compiler_params=pltpu.CompilerParams(vmem_limit_bytes=16 << 20),
                cost_estimate=pl.CostEstimate(
                    flops=2 * 192 * 384 * length, bytes_accessed=1000 * length, transcendentals=0
                ),
            )(lead, own, low, high, *parts)
            products += [mine, lax.ppermute(far, "mode", swap)]
    with jax.named_scope("interaction"):
        sums = pl.pallas_call(
            interaction_kernel,
            out_shape=jax.ShapeDtypeStruct((8, 128), f32),
            in_specs=[VMEM] * 8,
            out_specs=VMEM,
            scratch_shapes=[
                pltpu.VMEM((2 * PAD, 8320), b16),
                pltpu.VMEM((90 * PAD, 256), b16),
                pltpu.VMEM((PAD * WIDE, 128), f32),
                pltpu.VMEM((PAD * WIDE, 128), f32),
                pltpu.VMEM((8 * PAD, 128), f32),
                pltpu.VMEM((8 * PAD, 128), f32),
            ],
            compiler_params=pltpu.CompilerParams(vmem_limit_bytes=24 << 20),
        )(scalars, mid, last_all, tables, *products)
    with jax.named_scope("collect"):
        own_row = sums[0:1]
        rows = [own_row] + [lax.ppermute(own_row, "clus", ring(4, step)) for step in (1, 2, 3)]
        points = jnp.arange(32, dtype=jnp.int32)
        partial = jnp.zeros((32, 128), f32)
        for step in range(4):
            point = lax.dynamic_index_in_dim(irreducible, (clus - step) % 4, 0, keepdims=False)
            partial = partial + jnp.where((points == point)[:, None], rows[step], 0.0)
        received = lax.all_to_all(partial[:, None, :], "trip", 0, 0, tiled=True)
        final = jnp.sum(received[:, 0, :], axis=0)[None, :]
        gamma_total = final[:, 0:45] + boundary
        return gamma_total, (drive_term + final[:, PAD : PAD + 45]) / gamma_total


def solution(mesh):
    return jax.shard_map(
        body,
        mesh=mesh,
        in_specs=(
            P("clus", "mode", None),
            P("clus", "trip"),
            P("trip", None, None),
            P("trip", None),
            P("trip", None),
            P("trip", None),
            P("trip", None),
            P("trip"),
            P("trip"),
            P("trip", "mode"),
            P("trip", "mode"),
        ),
        out_specs=(P("trip", "mode"), P("trip", "mode")),
        check_vma=False,
    )
```

```python
import jax
import jax.numpy as jnp
from jax import lax
from jax.experimental import pallas as pl
from jax.experimental.pallas import tpu as pltpu
from jax.sharding import PartitionSpec as P

smearing = 0.3
PAD = 48
WIDE = 96
CHUNK = 2048
TOP = 23


def send_kernel(rows_ref, share_ref, out_ref):
    for target in range(out_ref.shape[0]):
        out_ref[target] = share_ref[rows_ref[0, target]]


def pick_kernel(table_ref, arrived_ref, phase_ref, out_ref):
    for triplet in range(4):
        for member in range(3):
            block = arrived_ref[table_ref[triplet, member]]
            out_ref[2 * triplet, member] = block
            out_ref[2 * triplet + 1, member] = block
        out_ref[2 * triplet, 3] = phase_ref[triplet]
        out_ref[2 * triplet + 1, 3] = phase_ref[triplet]


def whole_record(members_ref, slot):
    parts = [members_ref[j, slot].astype(jnp.float32) for j in range(8)]
    rows = jnp.concatenate(parts, axis=0)
    fill = jnp.zeros((WIDE, 38), jnp.float32)
    return jnp.concatenate([rows[:, 0:90], fill, rows[:, 90:180], fill], axis=1)


def operand_kernel(
    where_ref, members_ref, early_ref, late_ref, middle_ref, last_ref, tables_ref, scalars_ref
):
    rank, first, mult = where_ref[0], where_ref[1] == 0, where_ref[2]
    f32 = jnp.float32
    records = [whole_record(members_ref, member) for member in range(3)]
    lead_r, lead_i = records[0][:, 0:128].T, records[0][:, 128:256].T

    def halves(array):
        low, high = array[0:PAD], array[45 : 45 + PAD]
        return jnp.where(first, low, high), jnp.where(first, high, low)

    def sides(array):
        low, high = array[:, 0:PAD], array[:, 45 : 45 + PAD]
        return jnp.where(first, low, high), jnp.where(first, high, low)

    row = lax.broadcasted_iota(jnp.int32, (PAD, WIDE), 0)
    column = lax.broadcasted_iota(jnp.int32, (PAD, WIDE), 1)

    def spread(array, start, count):
        taken = (column // 2 + start == row) & (column < 2 * count)
        return jnp.dot(array, taken.astype(f32), preferred_element_type=f32)

    def turned(real, imag, offset):
        trig = members_ref[2 * ((rank + offset) & 3), 3].astype(f32)
        even = lax.broadcasted_iota(jnp.int32, (1, real.shape[1]), 1) % 2 == 0
        cosine = jnp.where(even, trig[0:1, 0:1], trig[0:1, 2:3])
        sine = jnp.where(even, trig[0:1, 1:2], trig[0:1, 3:4])
        return jnp.concatenate([cosine * real - sine * imag, cosine * imag + sine * real], axis=0)

    columns = []
    for array in (lead_r, lead_i):
        columns.append([halves(side) for side in sides(array)])
    whole = [[spread(columns[i][0][h], 0, 45) for i in range(2)] for h in range(2)]
    early_ref[...] = jnp.concatenate(
        [
            jnp.concatenate([turned(*whole[h], offset) for h in range(2)], axis=0)
            for offset in (0, 3, 1)
        ],
        axis=1,
    ).astype(early_ref.dtype)
    parts = []
    for side in range(2):
        for start, count in ((0, TOP), (TOP, 45 - TOP)):
            real, imag = (spread(columns[i][side][0], start, count)[:, 0:PAD] for i in range(2))
            parts.append(turned(real, imag, 2))
    late_ref[...] = jnp.concatenate(parts, axis=1).astype(late_ref.dtype)

    mid_r, mid_i = records[1][:, 0:128].T, records[1][:, 128:256].T
    within = lax.broadcasted_iota(jnp.int32, (WIDE, WIDE), 1) < 90
    real = jnp.where(within, mid_r[0:WIDE], 0.0)
    imag = jnp.where(within, mid_i[0:WIDE], 0.0)
    middle_ref[...] = jnp.concatenate(
        [jnp.concatenate([real, -imag], axis=1), jnp.concatenate([imag, real], axis=1)], axis=0
    ).astype(middle_ref.dtype)

    last_r, last_i = records[2][:, 0:128], records[2][:, 128:256]
    within = lax.broadcasted_iota(jnp.int32, (WIDE, 128), 0) < 90
    real = jnp.where(within, last_r, 0.0)
    imag = jnp.where(within, last_i, 0.0)
    zeros = jnp.zeros((32, 256), f32)
    last_ref[...] = jnp.concatenate(
        [
            jnp.concatenate([real, imag], axis=1),
            zeros,
            jnp.concatenate([-imag, real], axis=1),
            zeros,
        ],
        axis=0,
    ).astype(last_ref.dtype)

    row = lax.broadcasted_iota(jnp.int32, (WIDE, 128), 0)
    column = lax.broadcasted_iota(jnp.int32, (WIDE, 128), 1)
    one = jnp.where(row < 90, jnp.broadcast_to(mid_r[0:WIDE, 90:91], (WIDE, 128)), 1.0)
    two = jnp.where(column < 90, jnp.broadcast_to(last_r[90:91, :], (WIDE, 128)), 1.0)
    tables_ref[0] = one + two
    tables_ref[1] = one - two
    tables_ref[2] = 1.0 / (one * two)
    tables_ref[3] = jnp.broadcast_to(mid_i[0:WIDE, 90:91], (WIDE, 128)) + jnp.broadcast_to(
        last_i[90:91, :], (WIDE, 128)
    )
    zero = halves(lead_r[:, 90:91])[0]
    zero = jnp.where(lax.broadcasted_iota(jnp.int32, (PAD, 1), 0) < 45, zero, 1.0)
    scalars_ref[0] = jnp.broadcast_to(zero, (PAD, 128))
    scalars_ref[1] = jnp.broadcast_to(mult.astype(f32) / zero, (PAD, 128))


def rows_of(ref, cols, count):
    values = ref[:, :, cols]
    rows = values.shape[0] * values.shape[1]
    return jnp.pad(values.reshape(rows, values.shape[2]), ((0, count - rows), (0, 0)))


def early_kernel(lead_ref, own_ref, low_ref, high_ref, mine_ref, far_ref):
    total = own_ref.shape[2]
    for start in range(0, total, CHUNK):
        cols = slice(start, min(start + CHUNK, total))
        product = jnp.dot(
            lead_ref[...],
            jnp.concatenate([rows_of(ref, cols, WIDE) for ref in (own_ref, low_ref, high_ref)], axis=0),
            preferred_element_type=jnp.float32,
        )
        mine_ref[:, cols] = product[0:WIDE].astype(mine_ref.dtype)
        far_ref[:, cols] = product[WIDE:].astype(far_ref.dtype)


def interaction_kernel(
    scalars_ref,
    middle_ref,
    last_ref,
    tables_ref,
    late_ref,
    top_ref,
    bottom_ref,
    far_top_ref,
    far_bottom_ref,
    mine_ref,
    other_ref,
    out_ref,
    flat,
    windows,
    mid_real,
    mid_imag,
    rate_acc,
    couple_acc,
):
    total = mine_ref.shape[1]
    flat[:, 8064:8320] = jnp.zeros((WIDE, 256), flat.dtype)
    for start in range(0, total, 1024):
        cols = slice(start, min(start + 1024, total))
        late = (top_ref, bottom_ref, far_top_ref, far_bottom_ref)
        both = mine_ref[:, cols].astype(jnp.float32) + other_ref[:, cols].astype(jnp.float32)
        both = both + jnp.dot(
            late_ref[...],
            jnp.concatenate([rows_of(ref, cols, PAD) for ref in late], axis=0),
            preferred_element_type=jnp.float32,
        )
        flat[:, cols] = both.astype(flat.dtype)
    for b in range(90):
        tile, shift = divmod(90 * b, 128)
        pair = flat[:, tile * 128 : tile * 128 + 256]
        window = pair[:, shift : shift + 128]
        windows[b * PAD : (b + 1) * PAD, 0:128] = window[0:PAD]
        windows[b * PAD : (b + 1) * PAD, 128:256] = window[PAD:]
    zeros = jnp.zeros((PAD, 128), jnp.float32)
    for b in range(90, WIDE):
        mid_real[pl.ds(b, PAD, stride=WIDE), :] = zeros
        mid_imag[pl.ds(b, PAD, stride=WIDE), :] = zeros
    for group in range(9):
        product = jnp.dot(
            windows[group * 480 : (group + 1) * 480, :],
            last_ref[...],
            preferred_element_type=jnp.float32,
        )
        for i in range(10):
            rows = pl.ds(group * 10 + i, PAD, stride=WIDE)
            mid_real[rows, :] = product[i * PAD : (i + 1) * PAD, 0:128]
            mid_imag[rows, :] = product[i * PAD : (i + 1) * PAD, 128:256]

    scaled = 0.5 / (smearing * smearing)
    def two_modes(s):
        low = pl.ds(pl.multiple_of(s * WIDE, WIDE), WIDE)
        high = pl.ds(pl.multiple_of(s * WIDE + WIDE, WIDE), WIDE)
        operand = jnp.concatenate(
            [
                jnp.concatenate([ref[low, :], ref[high, :]], axis=1).astype(jnp.bfloat16)
                for ref in (mid_real, mid_imag)
            ],
            axis=0,
        )
        value = jnp.dot(middle_ref[...], operand, preferred_element_type=jnp.float32)
        for i in range(2):
            real = value[0:WIDE, 128 * i : 128 * i + 128]
            imag = value[WIDE:, 128 * i : 128 * i + 128]
            freq = scalars_ref[0, pl.ds(s + i, 1), :]
            decays = freq - tables_ref[0]
            merges = freq + tables_ref[1]
            weight = (real * real + imag * imag) * (
                jnp.exp(-scaled * decays * decays) + jnp.exp(-scaled * merges * merges)
            )
            weight = weight * tables_ref[2] * scalars_ref[1, pl.ds(s + i, 1), :]
            at = pl.ds(pl.multiple_of((s + i) * 8, 8), 8)
            rate_acc[at, :] = jnp.sum(weight.reshape(WIDE // 8, 8, 128), axis=0)
            weight = weight * tables_ref[3]
            couple_acc[at, :] = jnp.sum(weight.reshape(WIDE // 8, 8, 128), axis=0)

    @pl.loop(0, 12)
    def _(i):
        two_modes(4 * i)
        two_modes(4 * i + 2)

    sums = jnp.concatenate(
        [
            jnp.sum(rate_acc[...].reshape(PAD, 8, 128), axis=1),
            jnp.sum(couple_acc[...].reshape(PAD, 8, 128), axis=1),
        ],
        axis=0,
    )
    out_ref[:, 0:WIDE] = lax.dot_general(
        jnp.ones((8, 128), jnp.float32),
        sums,
        (((1,), (1,)), ((), ())),
        precision=lax.Precision.HIGHEST,
        preferred_element_type=jnp.float32,
    )
    out_ref[:, WIDE:128] = jnp.zeros((8, 128 - WIDE), jnp.float32)


VMEM = pl.BlockSpec(memory_space=pltpu.VMEM)
SMEM = pl.BlockSpec(memory_space=pltpu.SMEM)
PARAMS = pltpu.CompilerParams(vmem_limit_bytes=56 << 20)


def ring(count, step):
    return [(i, (i + step) % count) for i in range(count)]


def body(
    force_third,
    phase_angle,
    eigenvectors,
    frequencies,
    deviation,
    send_rows,
    trip_table,
    irreducible,
    multiplicity,
    drive_term,
    boundary,
):
    f32, b16 = jnp.float32, jnp.bfloat16
    clus = lax.axis_index("clus")
    mode = lax.axis_index("mode")
    group = ("clus", "mode")

    with jax.named_scope("records"):
        extra = jnp.concatenate([frequencies, deviation], axis=1)[:, None, :]
        record = jnp.concatenate(
            [eigenvectors, extra, jnp.zeros((extra.shape[0], 5, 180), b16)], axis=1
        )
        share = lax.dynamic_slice_in_dim(record, 12 * (2 * clus + mode), 12, 1)
        chosen = pl.pallas_call(
            send_kernel,
            out_shape=jax.ShapeDtypeStruct((send_rows.shape[1],) + share.shape[1:], b16),
            in_specs=[SMEM, VMEM],
            out_specs=VMEM,
            compiler_params=PARAMS,
        )(send_rows, share)
        arrived = lax.all_to_all(chosen, "trip", 0, 0, tiled=True)
        angles = phase_angle.astype(f32)
        trig = jnp.stack([jnp.cos(angles), jnp.sin(angles)], axis=1).astype(b16)
        phases = jnp.pad(trig.reshape(4, 4).T[:, None, :], ((0, 0), (0, 11), (0, 176)))

    with jax.named_scope("force"):
        own = jnp.transpose(force_third, (1, 0, 2))
        low = lax.ppermute(own, "clus", ring(4, 1))
        high = lax.ppermute(own, "clus", ring(4, 3))
        low, high, _ = lax.optimization_barrier((low, high, arrived))
        top = lax.ppermute(low[:TOP], "clus", ring(4, 1))
        bottom = lax.ppermute(high[TOP:], "clus", ring(4, 3))

    with jax.named_scope("members"):
        picks = pl.pallas_call(
            pick_kernel,
            out_shape=jax.ShapeDtypeStruct((8, 4, 12, 180), b16),
            in_specs=[SMEM, VMEM, VMEM],
            out_specs=VMEM,
            compiler_params=PARAMS,
        )(trip_table, arrived, phases)
        members = lax.all_to_all(picks, group, 0, 0, tiled=True)

    with jax.named_scope("operands"):
        mult = lax.dynamic_index_in_dim(multiplicity, clus, 0, keepdims=False)
        where = jnp.stack([clus, mode, mult]).astype(jnp.int32)
        early, late, mid, last_all, tables, scalars = pl.pallas_call(
            operand_kernel,
            out_shape=(
                jax.ShapeDtypeStruct((2 * WIDE, 3 * WIDE), b16),
                jax.ShapeDtypeStruct((WIDE, 4 * PAD), b16),
                jax.ShapeDtypeStruct((2 * WIDE, 2 * WIDE), b16),
                jax.ShapeDtypeStruct((256, 256), b16),
                jax.ShapeDtypeStruct((4, WIDE, 128), f32),
                jax.ShapeDtypeStruct((2, PAD, 128), f32),
            ),
            in_specs=[SMEM, VMEM],
            out_specs=(VMEM,) * 6,
            compiler_params=PARAMS,
        )(where, members)

    with jax.named_scope("contract"):
        total = force_third.shape[2]
        swap = [(0, 1), (1, 0)]
        mine, far = pl.pallas_call(
            early_kernel,
            out_shape=(jax.ShapeDtypeStruct((WIDE, total), b16),) * 2,
            in_specs=[VMEM] * 4,
            out_specs=(VMEM,) * 2,
            compiler_params=PARAMS,
            cost_estimate=pl.CostEstimate(
                flops=2 * 192 * 288 * total, bytes_accessed=1200 * total, transcendentals=0
            ),
        )(early, own, low, high)
        other = lax.ppermute(far, "mode", swap)
        far_top = lax.ppermute(top, "mode", swap)
        far_bottom = lax.ppermute(bottom, "mode", swap)

    with jax.named_scope("interaction"):
        sums = pl.pallas_call(
            interaction_kernel,
            out_shape=jax.ShapeDtypeStruct((8, 128), f32),
            in_specs=[VMEM] * 11,
            out_specs=VMEM,
            scratch_shapes=[
                pltpu.VMEM((WIDE, 8320), b16),
                pltpu.VMEM((90 * PAD, 256), b16),
                pltpu.VMEM((PAD * WIDE, 128), f32),
                pltpu.VMEM((PAD * WIDE, 128), f32),
                pltpu.VMEM((8 * PAD, 128), f32),
                pltpu.VMEM((8 * PAD, 128), f32),
            ],
            compiler_params=PARAMS,
        )(scalars, mid, last_all, tables, late, top, bottom, far_top, far_bottom, mine, other)
    with jax.named_scope("collect"):
        own_row = sums[0:1]
        rows = [own_row] + [lax.ppermute(own_row, "clus", ring(4, step)) for step in (1, 2, 3)]
        points = jnp.arange(32, dtype=jnp.int32)
        partial = jnp.zeros((32, 128), f32)
        for step in range(4):
            point = lax.dynamic_index_in_dim(irreducible, (clus - step) % 4, 0, keepdims=False)
            partial = partial + jnp.where((points == point)[:, None], rows[step], 0.0)
        received = lax.all_to_all(partial[:, None, :], "trip", 0, 0, tiled=True)
        final = jnp.sum(received[:, 0, :], axis=0)[None, :]
        gamma_total = final[:, 0:45] + boundary
        return gamma_total, (drive_term + final[:, PAD : PAD + 45]) / gamma_total


def solution(mesh):
    return jax.shard_map(
        body,
        mesh=mesh,
        in_specs=(
            P("clus", "mode", None),
            P("clus", "trip"),
            P("trip", None, None),
            P("trip", None),
            P("trip", None),
            P("trip", None),
            P("trip", None),
            P("trip"),
            P("trip"),
            P("trip", "mode"),
            P("trip", "mode"),
        ),
        out_specs=(P("trip", "mode"), P("trip", "mode")),
        check_vma=False,
    )
```

```python
import jax
import jax.numpy as jnp
from jax import lax
from jax.experimental import pallas as pl
from jax.experimental.pallas import tpu as pltpu
from jax.sharding import PartitionSpec as P

smearing = 0.3
PAD = 48
WIDE = 96
CHUNK = 2048
TOP = 23


def send_kernel(rows_ref, share_ref, out_ref):
    for target in range(out_ref.shape[0]):
        out_ref[target] = share_ref[rows_ref[0, target]]


def pick_kernel(table_ref, arrived_ref, phase_ref, out_ref):
    for triplet in range(4):
        for member in range(3):
            block = arrived_ref[table_ref[triplet, member]]
            out_ref[2 * triplet, member] = block
            out_ref[2 * triplet + 1, member] = block
        out_ref[2 * triplet, 3] = phase_ref[triplet]
        out_ref[2 * triplet + 1, 3] = phase_ref[triplet]


def whole_record(members_ref, slot):
    parts = [members_ref[j, slot].astype(jnp.float32) for j in range(8)]
    rows = jnp.concatenate(parts, axis=0)
    fill = jnp.zeros((WIDE, 38), jnp.float32)
    return jnp.concatenate([rows[:, 0:90], fill, rows[:, 90:180], fill], axis=1)


def operand_kernel(
    where_ref, members_ref, early_ref, late_ref, middle_ref, last_ref, tables_ref, scalars_ref
):
    rank, first, mult = where_ref[0], where_ref[1] == 0, where_ref[2]
    f32 = jnp.float32
    records = [whole_record(members_ref, member) for member in range(3)]
    lead_r, lead_i = records[0][:, 0:128].T, records[0][:, 128:256].T

    def halves(array):
        low, high = array[0:PAD], array[45 : 45 + PAD]
        return jnp.where(first, low, high), jnp.where(first, high, low)

    def sides(array):
        low, high = array[:, 0:PAD], array[:, 45 : 45 + PAD]
        return jnp.where(first, low, high), jnp.where(first, high, low)

    row = lax.broadcasted_iota(jnp.int32, (PAD, WIDE), 0)
    column = lax.broadcasted_iota(jnp.int32, (PAD, WIDE), 1)

    def spread(array, start, count):
        taken = (column // 2 + start == row) & (column < 2 * count)
        return jnp.dot(array, taken.astype(f32), preferred_element_type=f32)

    def turned(real, imag, offset):
        trig = members_ref[2 * ((rank + offset) & 3), 3].astype(f32)
        even = lax.broadcasted_iota(jnp.int32, (1, real.shape[1]), 1) % 2 == 0
        cosine = jnp.where(even, trig[0:1, 0:1], trig[0:1, 2:3])
        sine = jnp.where(even, trig[0:1, 1:2], trig[0:1, 3:4])
        return jnp.concatenate([cosine * real - sine * imag, cosine * imag + sine * real], axis=0)

    columns = []
    for array in (lead_r, lead_i):
        columns.append([halves(side) for side in sides(array)])
    whole = [[spread(columns[i][0][h], 0, 45) for i in range(2)] for h in range(2)]
    early_ref[...] = jnp.concatenate(
        [
            jnp.concatenate([turned(*whole[h], offset) for h in range(2)], axis=0)
            for offset in (0, 3, 1)
        ],
        axis=1,
    ).astype(early_ref.dtype)
    parts = []
    for side in range(2):
        for start, count in ((0, TOP), (TOP, 45 - TOP)):
            real, imag = (spread(columns[i][side][0], start, count)[:, 0:PAD] for i in range(2))
            parts.append(turned(real, imag, 2))
    late_ref[...] = jnp.concatenate(parts, axis=1).astype(late_ref.dtype)

    mid_r, mid_i = records[1][:, 0:128].T, records[1][:, 128:256].T
    within = lax.broadcasted_iota(jnp.int32, (WIDE, WIDE), 1) < 90
    real = jnp.where(within, mid_r[0:WIDE], 0.0)
    imag = jnp.where(within, mid_i[0:WIDE], 0.0)
    middle_ref[...] = jnp.concatenate(
        [jnp.concatenate([real, -imag], axis=1), jnp.concatenate([imag, real], axis=1)], axis=0
    ).astype(middle_ref.dtype)

    last_r, last_i = records[2][:, 0:128], records[2][:, 128:256]
    within = lax.broadcasted_iota(jnp.int32, (WIDE, 128), 0) < 90
    real = jnp.where(within, last_r, 0.0)
    imag = jnp.where(within, last_i, 0.0)
    zeros = jnp.zeros((32, 256), f32)
    last_ref[...] = jnp.concatenate(
        [
            jnp.concatenate([real, imag], axis=1),
            zeros,
            jnp.concatenate([-imag, real], axis=1),
            zeros,
        ],
        axis=0,
    ).astype(last_ref.dtype)

    row = lax.broadcasted_iota(jnp.int32, (WIDE, 128), 0)
    column = lax.broadcasted_iota(jnp.int32, (WIDE, 128), 1)
    one = jnp.where(row < 90, jnp.broadcast_to(mid_r[0:WIDE, 90:91], (WIDE, 128)), 1.0)
    two = jnp.where(column < 90, jnp.broadcast_to(last_r[90:91, :], (WIDE, 128)), 1.0)
    tables_ref[0] = one + two
    tables_ref[1] = one - two
    tables_ref[2] = 1.0 / (one * two)
    tables_ref[3] = jnp.broadcast_to(mid_i[0:WIDE, 90:91], (WIDE, 128)) + jnp.broadcast_to(
        last_i[90:91, :], (WIDE, 128)
    )
    zero = halves(lead_r[:, 90:91])[0]
    zero = jnp.where(lax.broadcasted_iota(jnp.int32, (PAD, 1), 0) < 45, zero, 1.0)
    scalars_ref[0] = jnp.broadcast_to(zero, (PAD, 128))
    scalars_ref[1] = jnp.broadcast_to(mult.astype(f32) / zero, (PAD, 128))


def rows_of(ref, cols, count):
    values = ref[:, :, cols]
    rows = values.shape[0] * values.shape[1]
    return jnp.pad(values.reshape(rows, values.shape[2]), ((0, count - rows), (0, 0)))


def early_kernel(lead_ref, own_ref, low_ref, high_ref, mine_ref, *far_refs):
    total = own_ref.shape[2]
    for start in range(0, total, CHUNK):
        cols = slice(start, min(start + CHUNK, total))
        product = jnp.dot(
            lead_ref[...],
            jnp.concatenate([rows_of(ref, cols, WIDE) for ref in (own_ref, low_ref, high_ref)], axis=0),
            preferred_element_type=jnp.float32,
        )
        mine_ref[:, cols] = product[0:WIDE].astype(mine_ref.dtype)
        for i, far_ref in enumerate(far_refs):
            rows = product[WIDE + 24 * i : WIDE + 24 * i + 24]
            far_ref[:, cols] = rows.astype(far_ref.dtype)


def interaction_kernel(
    scalars_ref,
    middle_ref,
    last_ref,
    tables_ref,
    late_ref,
    top_ref,
    bottom_ref,
    far_top_ref,
    far_bottom_ref,
    mine_ref,
    other0_ref,
    other1_ref,
    other2_ref,
    other3_ref,
    out_ref,
    flat,
    windows,
    mid_real,
    mid_imag,
    rate_acc,
    couple_acc,
):
    total = mine_ref.shape[1]
    flat[:, 8064:8320] = jnp.zeros((WIDE, 256), flat.dtype)
    for start in range(0, total, 1024):
        cols = slice(start, min(start + 1024, total))
        late = (top_ref, bottom_ref, far_top_ref, far_bottom_ref)
        others = (other0_ref, other1_ref, other2_ref, other3_ref)
        other = jnp.concatenate([ref[:, cols].astype(jnp.float32) for ref in others], axis=0)
        both = mine_ref[:, cols].astype(jnp.float32) + other
        both = both + jnp.dot(
            late_ref[...],
            jnp.concatenate([rows_of(ref, cols, PAD) for ref in late], axis=0),
            preferred_element_type=jnp.float32,
        )
        flat[:, cols] = both.astype(flat.dtype)
    for b in range(90):
        tile, shift = divmod(90 * b, 128)
        pair = flat[:, tile * 128 : tile * 128 + 256]
        window = pair[:, shift : shift + 128]
        windows[b * PAD : (b + 1) * PAD, 0:128] = window[0:PAD]
        windows[b * PAD : (b + 1) * PAD, 128:256] = window[PAD:]
    zeros = jnp.zeros((PAD, 128), jnp.float32)
    for b in range(90, WIDE):
        mid_real[pl.ds(b, PAD, stride=WIDE), :] = zeros
        mid_imag[pl.ds(b, PAD, stride=WIDE), :] = zeros
    for group in range(9):
        product = jnp.dot(
            windows[group * 480 : (group + 1) * 480, :],
            last_ref[...],
            preferred_element_type=jnp.float32,
        )
        for i in range(10):
            rows = pl.ds(group * 10 + i, PAD, stride=WIDE)
            mid_real[rows, :] = product[i * PAD : (i + 1) * PAD, 0:128]
            mid_imag[rows, :] = product[i * PAD : (i + 1) * PAD, 128:256]

    scaled = 0.5 / (smearing * smearing)
    def two_modes(s):
        low = pl.ds(pl.multiple_of(s * WIDE, WIDE), WIDE)
        high = pl.ds(pl.multiple_of(s * WIDE + WIDE, WIDE), WIDE)
        operand = jnp.concatenate(
            [
                jnp.concatenate([ref[low, :], ref[high, :]], axis=1).astype(jnp.bfloat16)
                for ref in (mid_real, mid_imag)
            ],
            axis=0,
        )
        value = jnp.dot(middle_ref[...], operand, preferred_element_type=jnp.float32)
        for i in range(2):
            real = value[0:WIDE, 128 * i : 128 * i + 128]
            imag = value[WIDE:, 128 * i : 128 * i + 128]
            freq = scalars_ref[0, pl.ds(s + i, 1), :]
            decays = freq - tables_ref[0]
            merges = freq + tables_ref[1]
            weight = (real * real + imag * imag) * (
                jnp.exp(-scaled * decays * decays) + jnp.exp(-scaled * merges * merges)
            )
            weight = weight * tables_ref[2] * scalars_ref[1, pl.ds(s + i, 1), :]
            at = pl.ds(pl.multiple_of((s + i) * 8, 8), 8)
            rate_acc[at, :] = jnp.sum(weight.reshape(WIDE // 8, 8, 128), axis=0)
            weight = weight * tables_ref[3]
            couple_acc[at, :] = jnp.sum(weight.reshape(WIDE // 8, 8, 128), axis=0)

    @pl.loop(0, 12)
    def _(i):
        two_modes(4 * i)
        two_modes(4 * i + 2)

    sums = jnp.concatenate(
        [
            jnp.sum(rate_acc[...].reshape(PAD, 8, 128), axis=1),
            jnp.sum(couple_acc[...].reshape(PAD, 8, 128), axis=1),
        ],
        axis=0,
    )
    out_ref[:, 0:WIDE] = lax.dot_general(
        jnp.ones((8, 128), jnp.float32),
        sums,
        (((1,), (1,)), ((), ())),
        precision=lax.Precision.HIGHEST,
        preferred_element_type=jnp.float32,
    )
    out_ref[:, WIDE:128] = jnp.zeros((8, 128 - WIDE), jnp.float32)


VMEM = pl.BlockSpec(memory_space=pltpu.VMEM)
SMEM = pl.BlockSpec(memory_space=pltpu.SMEM)
PARAMS = pltpu.CompilerParams(vmem_limit_bytes=56 << 20)


def ring(count, step):
    return [(i, (i + step) % count) for i in range(count)]


def body(
    force_third,
    phase_angle,
    eigenvectors,
    frequencies,
    deviation,
    send_rows,
    trip_table,
    irreducible,
    multiplicity,
    drive_term,
    boundary,
):
    f32, b16 = jnp.float32, jnp.bfloat16
    clus = lax.axis_index("clus")
    mode = lax.axis_index("mode")
    group = ("clus", "mode")

    with jax.named_scope("records"):
        extra = jnp.concatenate([frequencies, deviation], axis=1)[:, None, :]
        record = jnp.concatenate(
            [eigenvectors, extra, jnp.zeros((extra.shape[0], 5, 180), b16)], axis=1
        )
        share = lax.dynamic_slice_in_dim(record, 12 * (2 * clus + mode), 12, 1)
        chosen = pl.pallas_call(
            send_kernel,
            out_shape=jax.ShapeDtypeStruct((send_rows.shape[1],) + share.shape[1:], b16),
            in_specs=[SMEM, VMEM],
            out_specs=VMEM,
            compiler_params=PARAMS,
        )(send_rows, share)
        arrived = lax.all_to_all(chosen, "trip", 0, 0, tiled=True)
        angles = phase_angle.astype(f32)
        trig = jnp.stack([jnp.cos(angles), jnp.sin(angles)], axis=1).astype(b16)
        phases = jnp.pad(trig.reshape(4, 4).T[:, None, :], ((0, 0), (0, 11), (0, 176)))

    with jax.named_scope("force"):
        own = jnp.transpose(force_third, (1, 0, 2))
        low = lax.ppermute(own, "clus", ring(4, 1))
        high = lax.ppermute(own, "clus", ring(4, 3))
        low, high, _ = lax.optimization_barrier((low, high, arrived))
        top = lax.ppermute(low[:TOP], "clus", ring(4, 1))
        bottom = lax.ppermute(high[TOP:], "clus", ring(4, 3))

    with jax.named_scope("members"):
        picks = pl.pallas_call(
            pick_kernel,
            out_shape=jax.ShapeDtypeStruct((8, 4, 12, 180), b16),
            in_specs=[SMEM, VMEM, VMEM],
            out_specs=VMEM,
            compiler_params=PARAMS,
        )(trip_table, arrived, phases)
        members = lax.all_to_all(picks, group, 0, 0, tiled=True)

    with jax.named_scope("operands"):
        mult = lax.dynamic_index_in_dim(multiplicity, clus, 0, keepdims=False)
        where = jnp.stack([clus, mode, mult]).astype(jnp.int32)
        early, late, mid, last_all, tables, scalars = pl.pallas_call(
            operand_kernel,
            out_shape=(
                jax.ShapeDtypeStruct((2 * WIDE, 3 * WIDE), b16),
                jax.ShapeDtypeStruct((WIDE, 4 * PAD), b16),
                jax.ShapeDtypeStruct((2 * WIDE, 2 * WIDE), b16),
                jax.ShapeDtypeStruct((256, 256), b16),
                jax.ShapeDtypeStruct((4, WIDE, 128), f32),
                jax.ShapeDtypeStruct((2, PAD, 128), f32),
            ),
            in_specs=[SMEM, VMEM],
            out_specs=(VMEM,) * 6,
            compiler_params=PARAMS,
        )(where, members)

    with jax.named_scope("contract"):
        total = force_third.shape[2]
        swap = [(0, 1), (1, 0)]
        mine, *far = pl.pallas_call(
            early_kernel,
            out_shape=(jax.ShapeDtypeStruct((WIDE, total), b16),)
            + (jax.ShapeDtypeStruct((WIDE // 4, total), b16),) * 4,
            in_specs=[VMEM] * 4,
            out_specs=(VMEM,) * 5,
            compiler_params=PARAMS,
            cost_estimate=pl.CostEstimate(
                flops=2 * 192 * 288 * total, bytes_accessed=1200 * total, transcendentals=0
            ),
        )(early, own, low, high)
        other = [lax.ppermute(rows, "mode", swap) for rows in far]
        far_top = lax.ppermute(top, "mode", swap)
        far_bottom = lax.ppermute(bottom, "mode", swap)

    with jax.named_scope("interaction"):
        sums = pl.pallas_call(
            interaction_kernel,
            out_shape=jax.ShapeDtypeStruct((8, 128), f32),
            in_specs=[VMEM] * 14,
            out_specs=VMEM,
            scratch_shapes=[
                pltpu.VMEM((WIDE, 8320), b16),
                pltpu.VMEM((90 * PAD, 256), b16),
                pltpu.VMEM((PAD * WIDE, 128), f32),
                pltpu.VMEM((PAD * WIDE, 128), f32),
                pltpu.VMEM((8 * PAD, 128), f32),
                pltpu.VMEM((8 * PAD, 128), f32),
            ],
            compiler_params=PARAMS,
        )(scalars, mid, last_all, tables, late, top, bottom, far_top, far_bottom, mine, *other)
    with jax.named_scope("collect"):
        own_row = sums[0:1]
        rows = [own_row] + [lax.ppermute(own_row, "clus", ring(4, step)) for step in (1, 2, 3)]
        points = jnp.arange(32, dtype=jnp.int32)
        partial = jnp.zeros((32, 128), f32)
        for step in range(4):
            point = lax.dynamic_index_in_dim(irreducible, (clus - step) % 4, 0, keepdims=False)
            partial = partial + jnp.where((points == point)[:, None], rows[step], 0.0)
        received = lax.all_to_all(partial[:, None, :], "trip", 0, 0, tiled=True)
        final = jnp.sum(received[:, 0, :], axis=0)[None, :]
        gamma_total = final[:, 0:45] + boundary
        return gamma_total, (drive_term + final[:, PAD : PAD + 45]) / gamma_total


def solution(mesh):
    return jax.shard_map(
        body,
        mesh=mesh,
        in_specs=(
            P("clus", "mode", None),
            P("clus", "trip"),
            P("trip", None, None),
            P("trip", None),
            P("trip", None),
            P("trip", None),
            P("trip", None),
            P("trip"),
            P("trip"),
            P("trip", "mode"),
            P("trip", "mode"),
        ),
        out_specs=(P("trip", "mode"), P("trip", "mode")),
        check_vma=False,
    )
```

```python
import jax
import jax.numpy as jnp
from jax import lax
from jax.experimental import pallas as pl
from jax.experimental.pallas import tpu as pltpu
from jax.sharding import PartitionSpec as P

smearing = 0.3
PAD = 48
WIDE = 96
CHUNK = 2048
TOP = 23


def send_kernel(rows_ref, share_ref, out_ref):
    for target in range(out_ref.shape[0]):
        out_ref[target] = share_ref[rows_ref[0, target]]


def pick_kernel(table_ref, arrived_ref, phase_ref, out_ref):
    for triplet in range(4):
        for member in range(3):
            block = arrived_ref[table_ref[triplet, member]]
            out_ref[2 * triplet, member, 0:12] = block
            out_ref[2 * triplet + 1, member, 0:12] = block
            fill = jnp.zeros((4, block.shape[1]), block.dtype)
            out_ref[2 * triplet, member, 12:16] = fill
            out_ref[2 * triplet + 1, member, 12:16] = fill
        out_ref[2 * triplet, 3] = phase_ref[triplet]
        out_ref[2 * triplet + 1, 3] = phase_ref[triplet]


def whole_record(members_ref, slot):
    parts = [members_ref[j, slot].astype(jnp.float32)[0:12] for j in range(8)]
    rows = jnp.concatenate(parts, axis=0)
    fill = jnp.zeros((WIDE, 38), jnp.float32)
    return jnp.concatenate([rows[:, 0:90], fill, rows[:, 90:180], fill], axis=1)


def operand_kernel(
    where_ref, members_ref, early_ref, late_ref, middle_ref, last_ref, tables_ref, scalars_ref
):
    rank, first, mult = where_ref[0], where_ref[1] == 0, where_ref[2]
    f32 = jnp.float32
    records = [whole_record(members_ref, member) for member in range(3)]
    lead_r, lead_i = records[0][:, 0:128].T, records[0][:, 128:256].T

    def halves(array):
        low, high = array[0:PAD], array[45 : 45 + PAD]
        return jnp.where(first, low, high), jnp.where(first, high, low)

    def sides(array):
        low, high = array[:, 0:PAD], array[:, 45 : 45 + PAD]
        return jnp.where(first, low, high), jnp.where(first, high, low)

    row = lax.broadcasted_iota(jnp.int32, (PAD, WIDE), 0)
    column = lax.broadcasted_iota(jnp.int32, (PAD, WIDE), 1)

    def spread(array, start, count):
        taken = (column // 2 + start == row) & (column < 2 * count)
        return jnp.dot(array, taken.astype(f32), preferred_element_type=f32)

    def turned(real, imag, offset):
        trig = members_ref[2 * ((rank + offset) & 3), 3].astype(f32)
        even = lax.broadcasted_iota(jnp.int32, (1, real.shape[1]), 1) % 2 == 0
        cosine = jnp.where(even, trig[0:1, 0:1], trig[0:1, 2:3])
        sine = jnp.where(even, trig[0:1, 1:2], trig[0:1, 3:4])
        return jnp.concatenate([cosine * real - sine * imag, cosine * imag + sine * real], axis=0)

    columns = []
    for array in (lead_r, lead_i):
        columns.append([halves(side) for side in sides(array)])
    whole = [[spread(columns[i][0][h], 0, 45) for i in range(2)] for h in range(2)]
    early_ref[...] = jnp.concatenate(
        [
            jnp.concatenate([turned(*whole[h], offset) for h in range(2)], axis=0)
            for offset in (0, 3, 1)
        ],
        axis=1,
    ).astype(early_ref.dtype)
    parts = []
    for side in range(2):
        for start, count in ((0, TOP), (TOP, 45 - TOP)):
            real, imag = (spread(columns[i][side][0], start, count)[:, 0:PAD] for i in range(2))
            parts.append(turned(real, imag, 2))
    late_ref[...] = jnp.concatenate(parts, axis=1).astype(late_ref.dtype)

    mid_r, mid_i = records[1][:, 0:128].T, records[1][:, 128:256].T
    within = lax.broadcasted_iota(jnp.int32, (WIDE, WIDE), 1) < 90
    real = jnp.where(within, mid_r[0:WIDE], 0.0)
    imag = jnp.where(within, mid_i[0:WIDE], 0.0)
    middle_ref[...] = jnp.concatenate(
        [jnp.concatenate([real, -imag], axis=1), jnp.concatenate([imag, real], axis=1)], axis=0
    ).astype(middle_ref.dtype)

    last_r, last_i = records[2][:, 0:128], records[2][:, 128:256]
    within = lax.broadcasted_iota(jnp.int32, (WIDE, 128), 0) < 90
    real = jnp.where(within, last_r, 0.0)
    imag = jnp.where(within, last_i, 0.0)
    zeros = jnp.zeros((32, 256), f32)
    last_ref[...] = jnp.concatenate(
        [
            jnp.concatenate([real, imag], axis=1),
            zeros,
            jnp.concatenate([-imag, real], axis=1),
            zeros,
        ],
        axis=0,
    ).astype(last_ref.dtype)

    row = lax.broadcasted_iota(jnp.int32, (WIDE, 128), 0)
    column = lax.broadcasted_iota(jnp.int32, (WIDE, 128), 1)
    one = jnp.where(row < 90, jnp.broadcast_to(mid_r[0:WIDE, 90:91], (WIDE, 128)), 1.0)
    two = jnp.where(column < 90, jnp.broadcast_to(last_r[90:91, :], (WIDE, 128)), 1.0)
    tables_ref[0] = one + two
    tables_ref[1] = one - two
    tables_ref[2] = 1.0 / (one * two)
    tables_ref[3] = jnp.broadcast_to(mid_i[0:WIDE, 90:91], (WIDE, 128)) + jnp.broadcast_to(
        last_i[90:91, :], (WIDE, 128)
    )
    zero = halves(lead_r[:, 90:91])[0]
    zero = jnp.where(lax.broadcasted_iota(jnp.int32, (PAD, 1), 0) < 45, zero, 1.0)
    scalars_ref[0] = jnp.broadcast_to(zero, (PAD, 128))
    scalars_ref[1] = jnp.broadcast_to(mult.astype(f32) / zero, (PAD, 128))


def rows_of(ref, cols, count):
    values = ref[:, :, cols]
    rows = values.shape[0] * values.shape[1]
    return jnp.pad(values.reshape(rows, values.shape[2]), ((0, count - rows), (0, 0)))


def early_kernel(lead_ref, own_ref, low_ref, high_ref, mine_ref, *far_refs):
    total = own_ref.shape[2]
    for start in range(0, total, CHUNK):
        cols = slice(start, min(start + CHUNK, total))
        product = jnp.dot(
            lead_ref[...],
            jnp.concatenate([rows_of(ref, cols, WIDE) for ref in (own_ref, low_ref, high_ref)], axis=0),
            preferred_element_type=jnp.float32,
        )
        mine_ref[:, cols] = product[0:WIDE].astype(mine_ref.dtype)
        for i, far_ref in enumerate(far_refs):
            rows = product[WIDE + 24 * i : WIDE + 24 * i + 24]
            far_ref[:, cols] = rows.astype(far_ref.dtype)


def interaction_kernel(
    scalars_ref,
    middle_ref,
    last_ref,
    tables_ref,
    late_ref,
    top_ref,
    bottom_ref,
    far_top_ref,
    far_bottom_ref,
    mine_ref,
    other0_ref,
    other1_ref,
    other2_ref,
    other3_ref,
    out_ref,
    flat,
    windows,
    mid_real,
    mid_imag,
    rate_acc,
    couple_acc,
):
    total = mine_ref.shape[1]
    flat[:, 8064:8320] = jnp.zeros((WIDE, 256), flat.dtype)
    for start in range(0, total, 1024):
        cols = slice(start, min(start + 1024, total))
        late = (top_ref, bottom_ref, far_top_ref, far_bottom_ref)
        others = (other0_ref, other1_ref, other2_ref, other3_ref)
        other = jnp.concatenate([ref[:, cols].astype(jnp.float32) for ref in others], axis=0)
        both = mine_ref[:, cols].astype(jnp.float32) + other
        both = both + jnp.dot(
            late_ref[...],
            jnp.concatenate([rows_of(ref, cols, PAD) for ref in late], axis=0),
            preferred_element_type=jnp.float32,
        )
        flat[:, cols] = both.astype(flat.dtype)
    for b in range(90):
        tile, shift = divmod(90 * b, 128)
        pair = flat[:, tile * 128 : tile * 128 + 256]
        window = pair[:, shift : shift + 128]
        windows[b * PAD : (b + 1) * PAD, 0:128] = window[0:PAD]
        windows[b * PAD : (b + 1) * PAD, 128:256] = window[PAD:]
    zeros = jnp.zeros((PAD, 128), jnp.float32)
    for b in range(90, WIDE):
        mid_real[pl.ds(b, PAD, stride=WIDE), :] = zeros
        mid_imag[pl.ds(b, PAD, stride=WIDE), :] = zeros
    for group in range(9):
        product = jnp.dot(
            windows[group * 480 : (group + 1) * 480, :],
            last_ref[...],
            preferred_element_type=jnp.float32,
        )
        for i in range(10):
            rows = pl.ds(group * 10 + i, PAD, stride=WIDE)
            mid_real[rows, :] = product[i * PAD : (i + 1) * PAD, 0:128]
            mid_imag[rows, :] = product[i * PAD : (i + 1) * PAD, 128:256]

    scaled = 0.5 / (smearing * smearing)
    def two_modes(s):
        low = pl.ds(pl.multiple_of(s * WIDE, WIDE), WIDE)
        high = pl.ds(pl.multiple_of(s * WIDE + WIDE, WIDE), WIDE)
        operand = jnp.concatenate(
            [
                jnp.concatenate([ref[low, :], ref[high, :]], axis=1).astype(jnp.bfloat16)
                for ref in (mid_real, mid_imag)
            ],
            axis=0,
        )
        value = jnp.dot(middle_ref[...], operand, preferred_element_type=jnp.float32)
        for i in range(2):
            real = value[0:WIDE, 128 * i : 128 * i + 128]
            imag = value[WIDE:, 128 * i : 128 * i + 128]
            freq = scalars_ref[0, pl.ds(s + i, 1), :]
            decays = freq - tables_ref[0]
            merges = freq + tables_ref[1]
            weight = (real * real + imag * imag) * (
                jnp.exp(-scaled * decays * decays) + jnp.exp(-scaled * merges * merges)
            )
            weight = weight * tables_ref[2] * scalars_ref[1, pl.ds(s + i, 1), :]
            at = pl.ds(pl.multiple_of((s + i) * 8, 8), 8)
            rate_acc[at, :] = jnp.sum(weight.reshape(WIDE // 8, 8, 128), axis=0)
            weight = weight * tables_ref[3]
            couple_acc[at, :] = jnp.sum(weight.reshape(WIDE // 8, 8, 128), axis=0)

    @pl.loop(0, 12)
    def _(i):
        two_modes(4 * i)
        two_modes(4 * i + 2)

    sums = jnp.concatenate(
        [
            jnp.sum(rate_acc[...].reshape(PAD, 8, 128), axis=1),
            jnp.sum(couple_acc[...].reshape(PAD, 8, 128), axis=1),
        ],
        axis=0,
    )
    out_ref[:, 0:WIDE] = lax.dot_general(
        jnp.ones((8, 128), jnp.float32),
        sums,
        (((1,), (1,)), ((), ())),
        precision=lax.Precision.HIGHEST,
        preferred_element_type=jnp.float32,
    )
    out_ref[:, WIDE:128] = jnp.zeros((8, 128 - WIDE), jnp.float32)


VMEM = pl.BlockSpec(memory_space=pltpu.VMEM)
SMEM = pl.BlockSpec(memory_space=pltpu.SMEM)
PARAMS = pltpu.CompilerParams(vmem_limit_bytes=56 << 20)


def ring(count, step):
    return [(i, (i + step) % count) for i in range(count)]


def body(
    force_third,
    phase_angle,
    eigenvectors,
    frequencies,
    deviation,
    send_rows,
    trip_table,
    irreducible,
    multiplicity,
    drive_term,
    boundary,
):
    f32, b16 = jnp.float32, jnp.bfloat16
    clus = lax.axis_index("clus")
    mode = lax.axis_index("mode")
    group = ("clus", "mode")

    with jax.named_scope("records"):
        extra = jnp.concatenate([frequencies, deviation], axis=1)[:, None, :]
        record = jnp.concatenate(
            [eigenvectors, extra, jnp.zeros((extra.shape[0], 5, 180), b16)], axis=1
        )
        share = lax.dynamic_slice_in_dim(record, 12 * (2 * clus + mode), 12, 1)
        chosen = pl.pallas_call(
            send_kernel,
            out_shape=jax.ShapeDtypeStruct((send_rows.shape[1],) + share.shape[1:], b16),
            in_specs=[SMEM, VMEM],
            out_specs=VMEM,
            compiler_params=PARAMS,
        )(send_rows, share)
        arrived = lax.all_to_all(chosen, "trip", 0, 0, tiled=True)
        angles = phase_angle.astype(f32)
        trig = jnp.stack([jnp.cos(angles), jnp.sin(angles)], axis=1).astype(b16)
        phases = jnp.pad(trig.reshape(4, 4).T[:, None, :], ((0, 0), (0, 15), (0, 176)))

    with jax.named_scope("force"):
        own = jnp.transpose(force_third, (1, 0, 2))
        low = lax.ppermute(own, "clus", ring(4, 1))
        high = lax.ppermute(own, "clus", ring(4, 3))

    with jax.named_scope("members"):
        picks = pl.pallas_call(
            pick_kernel,
            out_shape=jax.ShapeDtypeStruct((8, 4, 16, 180), b16),
            in_specs=[SMEM, VMEM, VMEM],
            out_specs=VMEM,
            compiler_params=PARAMS,
        )(trip_table, arrived, phases)
        members = lax.all_to_all(picks, group, 0, 0, tiled=True)

    with jax.named_scope("force_second"):
        low, high, _ = lax.optimization_barrier((low, high, members))
        top = lax.ppermute(low[:TOP], "clus", ring(4, 1))
        bottom = lax.ppermute(high[TOP:], "clus", ring(4, 3))

    with jax.named_scope("operands"):
        mult = lax.dynamic_index_in_dim(multiplicity, clus, 0, keepdims=False)
        where = jnp.stack([clus, mode, mult]).astype(jnp.int32)
        early, late, mid, last_all, tables, scalars = pl.pallas_call(
            operand_kernel,
            out_shape=(
                jax.ShapeDtypeStruct((2 * WIDE, 3 * WIDE), b16),
                jax.ShapeDtypeStruct((WIDE, 4 * PAD), b16),
                jax.ShapeDtypeStruct((2 * WIDE, 2 * WIDE), b16),
                jax.ShapeDtypeStruct((256, 256), b16),
                jax.ShapeDtypeStruct((4, WIDE, 128), f32),
                jax.ShapeDtypeStruct((2, PAD, 128), f32),
            ),
            in_specs=[SMEM, VMEM],
            out_specs=(VMEM,) * 6,
            compiler_params=PARAMS,
        )(where, members)

    with jax.named_scope("contract"):
        total = force_third.shape[2]
        swap = [(0, 1), (1, 0)]
        mine, *far = pl.pallas_call(
            early_kernel,
            out_shape=(jax.ShapeDtypeStruct((WIDE, total), b16),)
            + (jax.ShapeDtypeStruct((WIDE // 4, total), b16),) * 4,
            in_specs=[VMEM] * 4,
            out_specs=(VMEM,) * 5,
            compiler_params=PARAMS,
            cost_estimate=pl.CostEstimate(
                flops=2 * 192 * 288 * total, bytes_accessed=1200 * total, transcendentals=0
            ),
        )(early, own, low, high)
        other = [lax.ppermute(rows, "mode", swap) for rows in far]
        far_top = lax.ppermute(top, "mode", swap)
        far_bottom = lax.ppermute(bottom, "mode", swap)

    with jax.named_scope("interaction"):
        sums = pl.pallas_call(
            interaction_kernel,
            out_shape=jax.ShapeDtypeStruct((8, 128), f32),
            in_specs=[VMEM] * 14,
            out_specs=VMEM,
            scratch_shapes=[
                pltpu.VMEM((WIDE, 8320), b16),
                pltpu.VMEM((90 * PAD, 256), b16),
                pltpu.VMEM((PAD * WIDE, 128), f32),
                pltpu.VMEM((PAD * WIDE, 128), f32),
                pltpu.VMEM((8 * PAD, 128), f32),
                pltpu.VMEM((8 * PAD, 128), f32),
            ],
            compiler_params=PARAMS,
        )(scalars, mid, last_all, tables, late, top, bottom, far_top, far_bottom, mine, *other)
    with jax.named_scope("collect"):
        own_row = sums[0:1]
        rows = [own_row] + [lax.ppermute(own_row, "clus", ring(4, step)) for step in (1, 2, 3)]
        points = jnp.arange(32, dtype=jnp.int32)
        partial = jnp.zeros((32, 128), f32)
        for step in range(4):
            point = lax.dynamic_index_in_dim(irreducible, (clus - step) % 4, 0, keepdims=False)
            partial = partial + jnp.where((points == point)[:, None], rows[step], 0.0)
        received = lax.all_to_all(partial[:, None, :], "trip", 0, 0, tiled=True)
        final = jnp.sum(received[:, 0, :], axis=0)[None, :]
        gamma_total = final[:, 0:45] + boundary
        return gamma_total, (drive_term + final[:, PAD : PAD + 45]) / gamma_total


def solution(mesh):
    return jax.shard_map(
        body,
        mesh=mesh,
        in_specs=(
            P("clus", "mode", None),
            P("clus", "trip"),
            P("trip", None, None),
            P("trip", None),
            P("trip", None),
            P("trip", None),
            P("trip", None),
            P("trip"),
            P("trip"),
            P("trip", "mode"),
            P("trip", "mode"),
        ),
        out_specs=(P("trip", "mode"), P("trip", "mode")),
        check_vma=False,
    )
```

```python
import jax
import jax.numpy as jnp
from jax import lax
from jax.experimental import pallas as pl
from jax.experimental.pallas import tpu as pltpu
from jax.sharding import PartitionSpec as P

smearing = 0.3
PAD = 48
WIDE = 96
CHUNK = 2048
TOP = 23


def send_kernel(rows_ref, share_ref, out_ref):
    for target in range(out_ref.shape[0]):
        out_ref[target] = share_ref[rows_ref[0, target]]


def pick_kernel(table_ref, arrived_ref, phase_ref, out_ref):
    for triplet in range(4):
        for member in range(3):
            block = arrived_ref[table_ref[triplet, member]]
            out_ref[2 * triplet, member, 0:12] = block
            out_ref[2 * triplet + 1, member, 0:12] = block
            fill = jnp.zeros((4, block.shape[1]), block.dtype)
            out_ref[2 * triplet, member, 12:16] = fill
            out_ref[2 * triplet + 1, member, 12:16] = fill
        out_ref[2 * triplet, 3] = phase_ref[triplet]
        out_ref[2 * triplet + 1, 3] = phase_ref[triplet]


def whole_record(members_ref, slot):
    parts = [members_ref[j, slot].astype(jnp.float32)[0:12] for j in range(8)]
    rows = jnp.concatenate(parts, axis=0)
    fill = jnp.zeros((WIDE, 38), jnp.float32)
    return jnp.concatenate([rows[:, 0:90], fill, rows[:, 90:180], fill], axis=1)


def operand_kernel(
    where_ref, members_ref, early_ref, late_ref, middle_ref, last_ref, tables_ref, scalars_ref
):
    rank, first, mult = where_ref[0], where_ref[1] == 0, where_ref[2]
    f32 = jnp.float32
    records = [whole_record(members_ref, member) for member in range(3)]
    lead_r, lead_i = records[0][:, 0:128].T, records[0][:, 128:256].T

    def halves(array):
        low, high = array[0:PAD], array[45 : 45 + PAD]
        return jnp.where(first, low, high), jnp.where(first, high, low)

    def sides(array):
        low, high = array[:, 0:PAD], array[:, 45 : 45 + PAD]
        return jnp.where(first, low, high), jnp.where(first, high, low)

    row = lax.broadcasted_iota(jnp.int32, (PAD, WIDE), 0)
    column = lax.broadcasted_iota(jnp.int32, (PAD, WIDE), 1)

    def spread(array, start, count):
        taken = (column // 2 + start == row) & (column < 2 * count)
        return jnp.dot(array, taken.astype(f32), preferred_element_type=f32)

    def turned(real, imag, offset):
        trig = members_ref[2 * ((rank + offset) & 3), 3].astype(f32)
        even = lax.broadcasted_iota(jnp.int32, (1, real.shape[1]), 1) % 2 == 0
        cosine = jnp.where(even, trig[0:1, 0:1], trig[0:1, 2:3])
        sine = jnp.where(even, trig[0:1, 1:2], trig[0:1, 3:4])
        return jnp.concatenate([cosine * real - sine * imag, cosine * imag + sine * real], axis=0)

    columns = []
    for array in (lead_r, lead_i):
        columns.append([halves(side) for side in sides(array)])
    whole = [[spread(columns[i][0][h], 0, 45) for i in range(2)] for h in range(2)]
    early_ref[...] = jnp.concatenate(
        [
            jnp.concatenate([turned(*whole[h], offset) for h in range(2)], axis=0)
            for offset in (0, 3, 1)
        ],
        axis=1,
    ).astype(early_ref.dtype)
    parts = []
    for side in range(2):
        for start, count in ((0, TOP), (TOP, 45 - TOP)):
            real, imag = (spread(columns[i][side][0], start, count)[:, 0:PAD] for i in range(2))
            parts.append(turned(real, imag, 2))
    late_ref[...] = jnp.concatenate(parts, axis=1).astype(late_ref.dtype)

    mid_r, mid_i = records[1][:, 0:128].T, records[1][:, 128:256].T
    within = lax.broadcasted_iota(jnp.int32, (WIDE, WIDE), 1) < 90
    real = jnp.where(within, mid_r[0:WIDE], 0.0)
    imag = jnp.where(within, mid_i[0:WIDE], 0.0)
    middle_ref[...] = jnp.concatenate(
        [jnp.concatenate([real, -imag], axis=1), jnp.concatenate([imag, real], axis=1)], axis=0
    ).astype(middle_ref.dtype)

    last_r, last_i = records[2][:, 0:128], records[2][:, 128:256]
    within = lax.broadcasted_iota(jnp.int32, (WIDE, 128), 0) < 90
    real = jnp.where(within, last_r, 0.0)
    imag = jnp.where(within, last_i, 0.0)
    zeros = jnp.zeros((32, 256), f32)
    last_ref[...] = jnp.concatenate(
        [
            jnp.concatenate([real, imag], axis=1),
            zeros,
            jnp.concatenate([-imag, real], axis=1),
            zeros,
        ],
        axis=0,
    ).astype(last_ref.dtype)

    row = lax.broadcasted_iota(jnp.int32, (WIDE, 128), 0)
    column = lax.broadcasted_iota(jnp.int32, (WIDE, 128), 1)
    one = jnp.where(row < 90, jnp.broadcast_to(mid_r[0:WIDE, 90:91], (WIDE, 128)), 1.0)
    two = jnp.where(column < 90, jnp.broadcast_to(last_r[90:91, :], (WIDE, 128)), 1.0)
    tables_ref[0] = one + two
    tables_ref[1] = one - two
    tables_ref[2] = 1.0 / (one * two)
    tables_ref[3] = jnp.broadcast_to(mid_i[0:WIDE, 90:91], (WIDE, 128)) + jnp.broadcast_to(
        last_i[90:91, :], (WIDE, 128)
    )
    zero = halves(lead_r[:, 90:91])[0]
    zero = jnp.where(lax.broadcasted_iota(jnp.int32, (PAD, 1), 0) < 45, zero, 1.0)
    scalars_ref[0] = jnp.broadcast_to(zero, (PAD, 128))
    scalars_ref[1] = jnp.broadcast_to(mult.astype(f32) / zero, (PAD, 128))


def rows_of(ref, cols, count):
    values = ref[:, :, cols]
    rows = values.shape[0] * values.shape[1]
    return jnp.pad(values.reshape(rows, values.shape[2]), ((0, count - rows), (0, 0)))


def early_kernel(lead_ref, own_ref, low_ref, high_ref, mine_ref, *far_refs):
    total = own_ref.shape[2]
    for start in range(0, total, CHUNK):
        cols = slice(start, min(start + CHUNK, total))
        product = jnp.dot(
            lead_ref[...],
            jnp.concatenate([rows_of(ref, cols, WIDE) for ref in (own_ref, low_ref, high_ref)], axis=0),
            preferred_element_type=jnp.float32,
        )
        mine_ref[:, cols] = product[0:WIDE].astype(mine_ref.dtype)
        for i, far_ref in enumerate(far_refs):
            rows = product[WIDE + 24 * i : WIDE + 24 * i + 24]
            far_ref[:, cols] = rows.astype(far_ref.dtype)


def interaction_kernel(*refs):
    count = 14
    operands, out_ref, buffers = refs[:count], refs[count], refs[count + 1 : 2 * count + 1]
    flat, windows, mid_real, mid_imag, rate_acc, couple_acc, done = refs[2 * count + 1 :]
    scalars_ref, middle_ref, last_ref, tables_ref, late_ref = buffers[:5]
    top_ref, bottom_ref, far_top_ref, far_bottom_ref, mine_ref = buffers[5:10]
    late, others = buffers[5:9], buffers[10:]
    total = mine_ref.shape[1]
    pieces = [slice(at, min(at + CHUNK, total)) for at in range(0, total, CHUNK)]
    whole = {}
    for i in range(5):
        whole[i] = pltpu.make_async_copy(operands[i], buffers[i], done.at[i, 0])
    parts = {}
    for k, cols in enumerate(pieces):
        for i in range(5, count):
            where = (slice(None),) * (len(operands[i].shape) - 1) + (cols,)
            parts[i, k] = pltpu.make_async_copy(
                operands[i].at[where], buffers[i].at[where], done.at[i, k]
            )
    whole[4].start()
    for i in range(5, count):
        parts[i, 0].start()
    whole[2].start()
    for k in range(1, len(pieces)):
        for i in range(5, count):
            parts[i, k].start()
    for i in (0, 1, 3):
        whole[i].start()

    flat[:, 8064:8320] = jnp.zeros((WIDE, 256), flat.dtype)
    zeros = jnp.zeros((PAD, 128), jnp.float32)
    for b in range(90, WIDE):
        mid_real[pl.ds(b, PAD, stride=WIDE), :] = zeros
        mid_imag[pl.ds(b, PAD, stride=WIDE), :] = zeros

    def window_of(b):
        tile, shift = divmod(90 * b, 128)
        pair = flat[:, tile * 128 : tile * 128 + 256]
        window = pair[:, shift : shift + 128]
        windows[b * PAD : (b + 1) * PAD, 0:128] = window[0:PAD]
        windows[b * PAD : (b + 1) * PAD, 128:256] = window[PAD:]

    def product_of(group):
        product = jnp.dot(
            windows[group * 480 : (group + 1) * 480, :],
            last_ref[...],
            preferred_element_type=jnp.float32,
        )
        for i in range(10):
            rows = pl.ds(group * 10 + i, PAD, stride=WIDE)
            mid_real[rows, :] = product[i * PAD : (i + 1) * PAD, 0:128]
            mid_imag[rows, :] = product[i * PAD : (i + 1) * PAD, 128:256]

    whole[4].wait()
    b = 0
    for k, cols in enumerate(pieces):
        for i in range(5, count):
            parts[i, k].wait()
        if k == 0:
            whole[2].wait()
        other = jnp.concatenate([ref[:, cols].astype(jnp.float32) for ref in others], axis=0)
        both = mine_ref[:, cols].astype(jnp.float32) + other
        both = both + jnp.dot(
            late_ref[...],
            jnp.concatenate([rows_of(ref, cols, PAD) for ref in late], axis=0),
            preferred_element_type=jnp.float32,
        )
        flat[:, cols] = both.astype(flat.dtype)
        ready = 8320 if cols.stop == total else cols.stop
        while b < 90 and 90 * b // 128 * 128 + 256 <= ready:
            window_of(b)
            b += 1
            if b % 10 == 0:
                product_of(b // 10 - 1)
    for i in (0, 1, 3):
        whole[i].wait()

    scaled = 0.5 / (smearing * smearing)
    def two_modes(s):
        low = pl.ds(pl.multiple_of(s * WIDE, WIDE), WIDE)
        high = pl.ds(pl.multiple_of(s * WIDE + WIDE, WIDE), WIDE)
        operand = jnp.concatenate(
            [
                jnp.concatenate([ref[low, :], ref[high, :]], axis=1).astype(jnp.bfloat16)
                for ref in (mid_real, mid_imag)
            ],
            axis=0,
        )
        value = jnp.dot(middle_ref[...], operand, preferred_element_type=jnp.float32)
        for i in range(2):
            real = value[0:WIDE, 128 * i : 128 * i + 128]
            imag = value[WIDE:, 128 * i : 128 * i + 128]
            freq = scalars_ref[0, pl.ds(s + i, 1), :]
            decays = freq - tables_ref[0]
            merges = freq + tables_ref[1]
            weight = (real * real + imag * imag) * (
                jnp.exp(-scaled * decays * decays) + jnp.exp(-scaled * merges * merges)
            )
            weight = weight * tables_ref[2] * scalars_ref[1, pl.ds(s + i, 1), :]
            at = pl.ds(pl.multiple_of((s + i) * 8, 8), 8)
            rate_acc[at, :] = jnp.sum(weight.reshape(WIDE // 8, 8, 128), axis=0)
            weight = weight * tables_ref[3]
            couple_acc[at, :] = jnp.sum(weight.reshape(WIDE // 8, 8, 128), axis=0)

    @pl.loop(0, 12)
    def _(i):
        two_modes(4 * i)
        two_modes(4 * i + 2)

    sums = jnp.concatenate(
        [
            jnp.sum(rate_acc[...].reshape(PAD, 8, 128), axis=1),
            jnp.sum(couple_acc[...].reshape(PAD, 8, 128), axis=1),
        ],
        axis=0,
    )
    out_ref[:, 0:WIDE] = lax.dot_general(
        jnp.ones((8, 128), jnp.float32),
        sums,
        (((1,), (1,)), ((), ())),
        precision=lax.Precision.HIGHEST,
        preferred_element_type=jnp.float32,
    )[0:1]
    out_ref[:, WIDE:128] = jnp.zeros((1, 128 - WIDE), jnp.float32)


VMEM = pl.BlockSpec(memory_space=pltpu.VMEM)
SMEM = pl.BlockSpec(memory_space=pltpu.SMEM)
PARAMS = pltpu.CompilerParams(vmem_limit_bytes=56 << 20)


def ring(count, step):
    return [(i, (i + step) % count) for i in range(count)]


def body(
    force_third,
    phase_angle,
    eigenvectors,
    frequencies,
    deviation,
    send_rows,
    trip_table,
    irreducible,
    multiplicity,
    drive_term,
    boundary,
):
    f32, b16 = jnp.float32, jnp.bfloat16
    clus = lax.axis_index("clus")
    mode = lax.axis_index("mode")
    group = ("clus", "mode")

    with jax.named_scope("records"):
        extra = jnp.concatenate([frequencies, deviation], axis=1)[:, None, :]
        record = jnp.concatenate(
            [eigenvectors, extra, jnp.zeros((extra.shape[0], 5, 180), b16)], axis=1
        )
        share = lax.dynamic_slice_in_dim(record, 12 * (2 * clus + mode), 12, 1)
        chosen = pl.pallas_call(
            send_kernel,
            out_shape=jax.ShapeDtypeStruct((send_rows.shape[1],) + share.shape[1:], b16),
            in_specs=[SMEM, VMEM],
            out_specs=VMEM,
            compiler_params=PARAMS,
        )(send_rows, share)
        arrived = lax.all_to_all(chosen, "trip", 0, 0, tiled=True)
        angles = phase_angle.astype(f32)
        trig = jnp.stack([jnp.cos(angles), jnp.sin(angles)], axis=1).astype(b16)
        phases = jnp.pad(trig.reshape(4, 4).T[:, None, :], ((0, 0), (0, 15), (0, 176)))

    with jax.named_scope("force"):
        own = jnp.transpose(force_third, (1, 0, 2))
        low = lax.ppermute(own, "clus", ring(4, 1))
        high = lax.ppermute(own, "clus", ring(4, 3))

    with jax.named_scope("members"):
        picks = pl.pallas_call(
            pick_kernel,
            out_shape=jax.ShapeDtypeStruct((8, 4, 16, 180), b16),
            in_specs=[SMEM, VMEM, VMEM],
            out_specs=VMEM,
            compiler_params=PARAMS,
        )(trip_table, arrived, phases)
        members = lax.all_to_all(picks, group, 0, 0, tiled=True)

    with jax.named_scope("force_second"):
        low_top, high_bottom, _ = lax.optimization_barrier((low[:TOP], high[TOP:], members))
        top = lax.ppermute(low_top, "clus", ring(4, 1))
        bottom = lax.ppermute(high_bottom, "clus", ring(4, 3))

    with jax.named_scope("operands"):
        mult = lax.dynamic_index_in_dim(multiplicity, clus, 0, keepdims=False)
        where = jnp.stack([clus, mode, mult]).astype(jnp.int32)
        early, late, mid, last_all, tables, scalars = pl.pallas_call(
            operand_kernel,
            out_shape=(
                jax.ShapeDtypeStruct((2 * WIDE, 3 * WIDE), b16),
                jax.ShapeDtypeStruct((WIDE, 4 * PAD), b16),
                jax.ShapeDtypeStruct((2 * WIDE, 2 * WIDE), b16),
                jax.ShapeDtypeStruct((256, 256), b16),
                jax.ShapeDtypeStruct((4, WIDE, 128), f32),
                jax.ShapeDtypeStruct((2, PAD, 128), f32),
            ),
            in_specs=[SMEM, VMEM],
            out_specs=(VMEM,) * 6,
            compiler_params=PARAMS,
        )(where, members)

    with jax.named_scope("contract"):
        total = force_third.shape[2]
        swap = [(0, 1), (1, 0)]
        mine, *far = pl.pallas_call(
            early_kernel,
            out_shape=(jax.ShapeDtypeStruct((WIDE, total), b16),)
            + (jax.ShapeDtypeStruct((WIDE // 4, total), b16),) * 4,
            in_specs=[VMEM] * 4,
            out_specs=(VMEM,) * 5,
            compiler_params=PARAMS,
            cost_estimate=pl.CostEstimate(
                flops=2 * 192 * 288 * total, bytes_accessed=1200 * total, transcendentals=0
            ),
        )(early, own, low, high)
        other = [lax.ppermute(rows, "mode", swap) for rows in far]
        far_top = lax.ppermute(top, "mode", swap)
        far_bottom = lax.ppermute(bottom, "mode", swap)

    with jax.named_scope("interaction"):
        inputs = (scalars, mid, last_all, tables, late, top, bottom, far_top, far_bottom, mine, *other)
        sums = pl.pallas_call(
            interaction_kernel,
            out_shape=jax.ShapeDtypeStruct((1, 128), f32),
            in_specs=[pl.BlockSpec(memory_space=pl.ANY)] * len(inputs),
            out_specs=VMEM,
            scratch_shapes=[pltpu.VMEM(x.shape, x.dtype) for x in inputs]
            + [
                pltpu.VMEM((WIDE, 8320), b16),
                pltpu.VMEM((90 * PAD, 256), b16),
                pltpu.VMEM((PAD * WIDE, 128), f32),
                pltpu.VMEM((PAD * WIDE, 128), f32),
                pltpu.VMEM((8 * PAD, 128), f32),
                pltpu.VMEM((8 * PAD, 128), f32),
                pltpu.SemaphoreType.DMA((len(inputs), 4)),
            ],
            compiler_params=PARAMS,
        )(*inputs)
    with jax.named_scope("collect"):
        own_row = sums
        rows = [own_row] + [lax.ppermute(own_row, "clus", ring(4, step)) for step in (1, 2, 3)]
        points = jnp.arange(32, dtype=jnp.int32)
        partial = jnp.zeros((32, 128), f32)
        for step in range(4):
            point = lax.dynamic_index_in_dim(irreducible, (clus - step) % 4, 0, keepdims=False)
            partial = partial + jnp.where((points == point)[:, None], rows[step], 0.0)
        received = lax.all_to_all(partial[:, None, :], "trip", 0, 0, tiled=True)
        final = jnp.sum(received[:, 0, :], axis=0)[None, :]
        gamma_total = final[:, 0:45] + boundary
        return gamma_total, (drive_term + final[:, PAD : PAD + 45]) / gamma_total


def solution(mesh):
    return jax.shard_map(
        body,
        mesh=mesh,
        in_specs=(
            P("clus", "mode", None),
            P("clus", "trip"),
            P("trip", None, None),
            P("trip", None),
            P("trip", None),
            P("trip", None),
            P("trip", None),
            P("trip"),
            P("trip"),
            P("trip", "mode"),
            P("trip", "mode"),
        ),
        out_specs=(P("trip", "mode"), P("trip", "mode")),
        check_vma=False,
    )
```

```python
import jax
import jax.numpy as jnp
from jax import lax
from jax.experimental import pallas as pl
from jax.experimental.pallas import tpu as pltpu
from jax.sharding import PartitionSpec as P

smearing = 0.3
PAD = 48
WIDE = 96
CHUNK = 2048
HALF = 23
SHARED = 22
TOP = 12
SLOT = 32
RING_Y = 4
RING_Z = 8


def send_kernel(rows_ref, share_ref, out_ref):
    for target in range(out_ref.shape[0]):
        out_ref[target] = share_ref[rows_ref[0, target]]


def pick_kernel(table_ref, arrived_ref, phase_ref, out_ref):
    for triplet in range(4):
        for member in range(3):
            block = arrived_ref[table_ref[triplet, member]]
            out_ref[2 * triplet, member, 0:12] = block
            out_ref[2 * triplet + 1, member, 0:12] = block
            fill = jnp.zeros((4, block.shape[1]), block.dtype)
            out_ref[2 * triplet, member, 12:16] = fill
            out_ref[2 * triplet + 1, member, 12:16] = fill
        out_ref[2 * triplet, 3] = phase_ref[triplet]
        out_ref[2 * triplet + 1, 3] = phase_ref[triplet]


def whole_record(members_ref, slot):
    parts = [members_ref[j, slot].astype(jnp.float32)[0:12] for j in range(8)]
    rows = jnp.concatenate(parts, axis=0)
    fill = jnp.zeros((WIDE, 38), jnp.float32)
    return jnp.concatenate([rows[:, 0:90], fill, rows[:, 90:180], fill], axis=1)


def operand_kernel(
    where_ref, members_ref, early_ref, late_ref, middle_ref, last_ref, tables_ref, scalars_ref
):
    rank, first, mult, color = where_ref[0], where_ref[1] == 0, where_ref[2], where_ref[3]
    f32 = jnp.float32
    records = [whole_record(members_ref, member) for member in range(3)]
    lead_r, lead_i = records[0][:, 0:128].T, records[0][:, 128:256].T

    def halves(array):
        low, high = array[0:PAD], array[45 : 45 + PAD]
        return jnp.where(first, low, high), jnp.where(first, high, low)

    def sides(array):
        low, high = array[:, 0:PAD], array[:, 45 : 45 + PAD]
        return jnp.where(first, low, high), jnp.where(first, high, low)

    row = lax.broadcasted_iota(jnp.int32, (PAD, WIDE), 0)
    column = lax.broadcasted_iota(jnp.int32, (PAD, WIDE), 1)

    def spread(array, start, count, again=False):
        taken = (column // 2 + start == row) & (column < 2 * count)
        if again:
            taken = taken & (row != SHARED)
        return jnp.dot(array, taken.astype(f32), preferred_element_type=f32)

    def turned(real, imag, offset):
        trig = members_ref[2 * ((rank + offset) & 3), 3].astype(f32)
        even = lax.broadcasted_iota(jnp.int32, (1, real.shape[1]), 1) % 2 == 0
        cosine = jnp.where(even, trig[0:1, 0:1], trig[0:1, 2:3])
        sine = jnp.where(even, trig[0:1, 1:2], trig[0:1, 3:4])
        return jnp.concatenate([cosine * real - sine * imag, cosine * imag + sine * real], axis=0)

    columns = []
    for array in (lead_r, lead_i):
        columns.append([halves(side) for side in sides(array)])
    same, differ = SHARED * color, SHARED * (1 - color)
    blocks = []
    for offset, start, count, width, again in (
        (0, 0, 45, WIDE, False),
        (3, same, HALF, PAD, False),
        (3, differ, HALF, PAD, True),
        (1, same, HALF, PAD, False),
        (1, differ, HALF, PAD, True),
    ):
        rows = []
        for h in range(2):
            real, imag = (
                spread(columns[i][0][h], start, count, again)[:, 0:width] for i in range(2)
            )
            rows.append(turned(real, imag, offset))
        blocks.append(jnp.concatenate(rows, axis=0))
    early_ref[...] = jnp.concatenate(blocks, axis=1).astype(early_ref.dtype)
    parts = []
    for side in range(2):
        for start, again in ((same, False), (differ, True)):
            for skip, count in ((0, TOP), (TOP, HALF - TOP)):
                real, imag = (
                    spread(columns[i][side][0], start + skip, count, again)[:, 0:SLOT]
                    for i in range(2)
                )
                parts.append(turned(real, imag, 2))
    late_ref[...] = jnp.concatenate(parts, axis=1).astype(late_ref.dtype)

    mid_r, mid_i = records[1][:, 0:128].T, records[1][:, 128:256].T
    within = lax.broadcasted_iota(jnp.int32, (WIDE, WIDE), 1) < 90
    real = jnp.where(within, mid_r[0:WIDE], 0.0)
    imag = jnp.where(within, mid_i[0:WIDE], 0.0)
    middle_ref[...] = jnp.concatenate(
        [jnp.concatenate([real, -imag], axis=1), jnp.concatenate([imag, real], axis=1)], axis=0
    ).astype(middle_ref.dtype)

    last_r, last_i = records[2][:, 0:128], records[2][:, 128:256]
    within = lax.broadcasted_iota(jnp.int32, (WIDE, 128), 0) < 90
    real = jnp.where(within, last_r, 0.0)
    imag = jnp.where(within, last_i, 0.0)
    zeros = jnp.zeros((32, 256), f32)
    last_ref[...] = jnp.concatenate(
        [
            jnp.concatenate([real, imag], axis=1),
            zeros,
            jnp.concatenate([-imag, real], axis=1),
            zeros,
        ],
        axis=0,
    ).astype(last_ref.dtype)

    row = lax.broadcasted_iota(jnp.int32, (WIDE, 128), 0)
    column = lax.broadcasted_iota(jnp.int32, (WIDE, 128), 1)
    one = jnp.where(row < 90, jnp.broadcast_to(mid_r[0:WIDE, 90:91], (WIDE, 128)), 1.0)
    two = jnp.where(column < 90, jnp.broadcast_to(last_r[90:91, :], (WIDE, 128)), 1.0)
    tables_ref[0] = one + two
    tables_ref[1] = one - two
    tables_ref[2] = 1.0 / (one * two)
    tables_ref[3] = jnp.broadcast_to(mid_i[0:WIDE, 90:91], (WIDE, 128)) + jnp.broadcast_to(
        last_i[90:91, :], (WIDE, 128)
    )
    zero = halves(lead_r[:, 90:91])[0]
    zero = jnp.where(lax.broadcasted_iota(jnp.int32, (PAD, 1), 0) < 45, zero, 1.0)
    scalars_ref[0] = jnp.broadcast_to(zero, (PAD, 128))
    scalars_ref[1] = jnp.broadcast_to(mult.astype(f32) / zero, (PAD, 128))


def rows_of(ref, cols, count):
    values = ref[:, :, cols]
    rows = values.shape[0] * values.shape[1]
    return jnp.pad(values.reshape(rows, values.shape[2]), ((0, count - rows), (0, 0)))


def early_kernel(lead_ref, own_ref, *refs):
    halves, mine_ref, far_refs = refs[:4], refs[4], refs[5:]
    total = own_ref.shape[2]
    for start in range(0, total, CHUNK):
        cols = slice(start, min(start + CHUNK, total))
        product = jnp.dot(
            lead_ref[...],
            jnp.concatenate(
                [rows_of(own_ref, cols, WIDE)] + [rows_of(ref, cols, PAD) for ref in halves], axis=0
            ),
            preferred_element_type=jnp.float32,
        )
        mine_ref[:, cols] = product[0:WIDE].astype(mine_ref.dtype)
        for i, far_ref in enumerate(far_refs):
            rows = product[WIDE + 48 * i : WIDE + 48 * i + 48]
            far_ref[:, cols] = rows.astype(far_ref.dtype)


def interaction_kernel(*refs):
    count = 16
    operands, out_ref, buffers = refs[:count], refs[count], refs[count + 1 : 2 * count + 1]
    flat, windows, mid_real, mid_imag, rate_acc, couple_acc, done = refs[2 * count + 1 :]
    scalars_ref, middle_ref, last_ref, tables_ref, late_ref = buffers[:5]
    late, mine_ref, others = buffers[5:13], buffers[13], buffers[14:]
    total = mine_ref.shape[1]
    pieces = [slice(at, min(at + CHUNK, total)) for at in range(0, total, CHUNK)]
    whole = {}
    for i in range(5):
        whole[i] = pltpu.make_async_copy(operands[i], buffers[i], done.at[i, 0])
    parts = {}
    for k, cols in enumerate(pieces):
        for i in range(5, count):
            where = (slice(None),) * (len(operands[i].shape) - 1) + (cols,)
            parts[i, k] = pltpu.make_async_copy(
                operands[i].at[where], buffers[i].at[where], done.at[i, k]
            )
    whole[4].start()
    for i in range(5, count):
        parts[i, 0].start()
    whole[2].start()
    for k in range(1, len(pieces)):
        for i in range(5, count):
            parts[i, k].start()
    for i in (0, 1, 3):
        whole[i].start()

    flat[:, 8064:8320] = jnp.zeros((WIDE, 256), flat.dtype)
    zeros = jnp.zeros((PAD, 128), jnp.float32)
    for b in range(90, WIDE):
        mid_real[pl.ds(b, PAD, stride=WIDE), :] = zeros
        mid_imag[pl.ds(b, PAD, stride=WIDE), :] = zeros

    def window_of(b):
        tile, shift = divmod(90 * b, 128)
        pair = flat[:, tile * 128 : tile * 128 + 256]
        window = pair[:, shift : shift + 128]
        windows[b * PAD : (b + 1) * PAD, 0:128] = window[0:PAD]
        windows[b * PAD : (b + 1) * PAD, 128:256] = window[PAD:]

    def product_of(group):
        product = jnp.dot(
            windows[group * 480 : (group + 1) * 480, :],
            last_ref[...],
            preferred_element_type=jnp.float32,
        )
        for i in range(10):
            rows = pl.ds(group * 10 + i, PAD, stride=WIDE)
            mid_real[rows, :] = product[i * PAD : (i + 1) * PAD, 0:128]
            mid_imag[rows, :] = product[i * PAD : (i + 1) * PAD, 128:256]

    whole[4].wait()
    b = 0
    for k, cols in enumerate(pieces):
        for i in range(5, count):
            parts[i, k].wait()
        if k == 0:
            whole[2].wait()
        other = jnp.concatenate([ref[:, cols].astype(jnp.float32) for ref in others], axis=0)
        both = mine_ref[:, cols].astype(jnp.float32) + other
        both = both + jnp.dot(
            late_ref[...],
            jnp.concatenate([rows_of(ref, cols, SLOT) for ref in late], axis=0),
            preferred_element_type=jnp.float32,
        )
        flat[:, cols] = both.astype(flat.dtype)
        ready = 8320 if cols.stop == total else cols.stop
        while b < 90 and 90 * b // 128 * 128 + 256 <= ready:
            window_of(b)
            b += 1
            if b % 10 == 0:
                product_of(b // 10 - 1)
    for i in (0, 1, 3):
        whole[i].wait()

    scaled = 0.5 / (smearing * smearing)
    def two_modes(s):
        low = pl.ds(s * WIDE, WIDE)
        high = pl.ds(s * WIDE + WIDE, WIDE)
        operand = jnp.concatenate(
            [
                jnp.concatenate([ref[low, :], ref[high, :]], axis=1).astype(jnp.bfloat16)
                for ref in (mid_real, mid_imag)
            ],
            axis=0,
        )
        value = jnp.dot(middle_ref[...], operand, preferred_element_type=jnp.float32)
        for i in range(2):
            real = value[0:WIDE, 128 * i : 128 * i + 128]
            imag = value[WIDE:, 128 * i : 128 * i + 128]
            freq = scalars_ref[0, pl.ds(s + i, 1), :]
            decays = freq - tables_ref[0]
            merges = freq + tables_ref[1]
            weight = (real * real + imag * imag) * (
                jnp.exp(-scaled * decays * decays) + jnp.exp(-scaled * merges * merges)
            )
            weight = weight * tables_ref[2] * scalars_ref[1, pl.ds(s + i, 1), :]
            at = pl.ds((s + i) * 8, 8)
            rate_acc[at, :] = jnp.sum(weight.reshape(WIDE // 8, 8, 128), axis=0)
            weight = weight * tables_ref[3]
            couple_acc[at, :] = jnp.sum(weight.reshape(WIDE // 8, 8, 128), axis=0)

    for i in range(24):
        two_modes(2 * i)

    sums = jnp.concatenate(
        [
            jnp.sum(rate_acc[...].reshape(PAD, 8, 128), axis=1),
            jnp.sum(couple_acc[...].reshape(PAD, 8, 128), axis=1),
        ],
        axis=0,
    )
    out_ref[:, 0:WIDE] = lax.dot_general(
        jnp.ones((8, 128), jnp.float32),
        sums,
        (((1,), (1,)), ((), ())),
        precision=lax.Precision.HIGHEST,
        preferred_element_type=jnp.float32,
    )[0:1]
    out_ref[:, WIDE:128] = jnp.zeros((1, 128 - WIDE), jnp.float32)


VMEM = pl.BlockSpec(memory_space=pltpu.VMEM)
SMEM = pl.BlockSpec(memory_space=pltpu.SMEM)
PARAMS = pltpu.CompilerParams(vmem_limit_bytes=56 << 20)


def grid_shift(step_y, step_z):
    return [
        (y * RING_Z + z, (y + step_y) % RING_Y * RING_Z + (z + step_z) % RING_Z)
        for y in range(RING_Y)
        for z in range(RING_Z)
    ]


def ring(count, step):
    return [(i, (i + step) % count) for i in range(count)]


def body(
    force_third,
    phase_angle,
    eigenvectors,
    frequencies,
    deviation,
    send_rows,
    trip_table,
    irreducible,
    multiplicity,
    drive_term,
    boundary,
):
    f32, b16 = jnp.float32, jnp.bfloat16
    clus = lax.axis_index("clus")
    mode = lax.axis_index("mode")
    trip = lax.axis_index("trip")
    color = (trip // RING_Z + trip % RING_Z) % 2
    group = ("clus", "mode")

    with jax.named_scope("records"):
        extra = jnp.concatenate([frequencies, deviation], axis=1)[:, None, :]
        record = jnp.concatenate(
            [eigenvectors, extra, jnp.zeros((extra.shape[0], 5, 180), b16)], axis=1
        )
        share = lax.dynamic_slice_in_dim(record, 12 * (2 * clus + mode), 12, 1)
        chosen = pl.pallas_call(
            send_kernel,
            out_shape=jax.ShapeDtypeStruct((send_rows.shape[1],) + share.shape[1:], b16),
            in_specs=[SMEM, VMEM],
            out_specs=VMEM,
            compiler_params=PARAMS,
        )(send_rows, share)
        arrived = lax.all_to_all(chosen, "trip", 0, 0, tiled=True)
        angles = phase_angle.astype(f32)
        trig = jnp.stack([jnp.cos(angles), jnp.sin(angles)], axis=1).astype(b16)
        phases = jnp.pad(trig.reshape(4, 4).T[:, None, :], ((0, 0), (0, 15), (0, 176)))

    with jax.named_scope("force"):
        own = jnp.transpose(force_third, (1, 0, 2))
        half = lax.dynamic_slice_in_dim(own, SHARED * color, HALF, 0)
        low = lax.ppermute(half, "clus", ring(4, 1))
        high = lax.ppermute(half, "clus", ring(4, 3))

    with jax.named_scope("force_second"):
        low, high, _ = lax.optimization_barrier((low, high, arrived))
        low_other = lax.ppermute(low, "trip", grid_shift(1, 0))
        high_other = lax.ppermute(high, "trip", grid_shift(0, 1))
        top = lax.ppermute(low[:TOP], "clus", ring(4, 1))
        bottom = lax.ppermute(high[TOP:], "clus", ring(4, 3))

    with jax.named_scope("members"):
        picks = pl.pallas_call(
            pick_kernel,
            out_shape=jax.ShapeDtypeStruct((8, 4, 16, 180), b16),
            in_specs=[SMEM, VMEM, VMEM],
            out_specs=VMEM,
            compiler_params=PARAMS,
        )(trip_table, arrived, phases)
        members = lax.all_to_all(picks, group, 0, 0, tiled=True)

    with jax.named_scope("force_shared"):
        sent_top, sent_bottom, _ = lax.optimization_barrier((top, bottom, members))
        top_other = lax.ppermute(sent_top, "trip", grid_shift(-1, 0))
        bottom_other = lax.ppermute(sent_bottom, "trip", grid_shift(0, -1))

    with jax.named_scope("operands"):
        mult = lax.dynamic_index_in_dim(multiplicity, clus, 0, keepdims=False)
        where = jnp.stack([clus, mode, mult, color]).astype(jnp.int32)
        early, late, mid, last_all, tables, scalars = pl.pallas_call(
            operand_kernel,
            out_shape=(
                jax.ShapeDtypeStruct((2 * WIDE, 3 * WIDE), b16),
                jax.ShapeDtypeStruct((WIDE, 8 * SLOT), b16),
                jax.ShapeDtypeStruct((2 * WIDE, 2 * WIDE), b16),
                jax.ShapeDtypeStruct((256, 256), b16),
                jax.ShapeDtypeStruct((4, WIDE, 128), f32),
                jax.ShapeDtypeStruct((2, PAD, 128), f32),
            ),
            in_specs=[SMEM, VMEM],
            out_specs=(VMEM,) * 6,
            compiler_params=PARAMS,
        )(where, members)

    with jax.named_scope("contract"):
        total = force_third.shape[2]
        swap = [(0, 1), (1, 0)]
        mine, *far = pl.pallas_call(
            early_kernel,
            out_shape=(jax.ShapeDtypeStruct((WIDE, total), b16),)
            + (jax.ShapeDtypeStruct((WIDE // 2, total), b16),) * 2,
            in_specs=[VMEM] * 6,
            out_specs=(VMEM,) * 3,
            compiler_params=PARAMS,
            cost_estimate=pl.CostEstimate(
                flops=2 * 192 * 288 * total, bytes_accessed=1200 * total, transcendentals=0
            ),
        )(early, own, low, low_other, high, high_other)
        other = [lax.ppermute(rows, "mode", swap) for rows in far]
        late_rows = [top, bottom, top_other, bottom_other]
        late_rows += [lax.ppermute(rows, "mode", swap) for rows in late_rows]

    with jax.named_scope("interaction"):
        inputs = (scalars, mid, last_all, tables, late, *late_rows, mine, *other)
        sums = pl.pallas_call(
            interaction_kernel,
            out_shape=jax.ShapeDtypeStruct((1, 128), f32),
            in_specs=[pl.BlockSpec(memory_space=pl.ANY)] * len(inputs),
            out_specs=VMEM,
            scratch_shapes=[pltpu.VMEM(x.shape, x.dtype) for x in inputs]
            + [
                pltpu.VMEM((WIDE, 8320), b16),
                pltpu.VMEM((90 * PAD, 256), b16),
                pltpu.VMEM((PAD * WIDE, 128), f32),
                pltpu.VMEM((PAD * WIDE, 128), f32),
                pltpu.VMEM((8 * PAD, 128), f32),
                pltpu.VMEM((8 * PAD, 128), f32),
                pltpu.SemaphoreType.DMA((len(inputs), 4)),
            ],
            compiler_params=PARAMS,
        )(*inputs)
    with jax.named_scope("collect"):
        own_row = sums
        rows = [own_row] + [lax.ppermute(own_row, "clus", ring(4, step)) for step in (1, 2, 3)]
        points = jnp.arange(32, dtype=jnp.int32)
        partial = jnp.zeros((32, 128), f32)
        for step in range(4):
            point = lax.dynamic_index_in_dim(irreducible, (clus - step) % 4, 0, keepdims=False)
            partial = partial + jnp.where((points == point)[:, None], rows[step], 0.0)
        received = lax.all_to_all(partial[:, None, :], "trip", 0, 0, tiled=True)
        final = jnp.sum(received[:, 0, :], axis=0)[None, :]
        gamma_total = final[:, 0:45] + boundary
        return gamma_total, (drive_term + final[:, PAD : PAD + 45]) / gamma_total


def solution(mesh):
    return jax.shard_map(
        body,
        mesh=mesh,
        in_specs=(
            P("clus", "mode", None),
            P("clus", "trip"),
            P("trip", None, None),
            P("trip", None),
            P("trip", None),
            P("trip", None),
            P("trip", None),
            P("trip"),
            P("trip"),
            P("trip", "mode"),
            P("trip", "mode"),
        ),
        out_specs=(P("trip", "mode"), P("trip", "mode")),
        check_vma=False,
    )
```

```python
import jax
import jax.numpy as jnp
from jax import lax
from jax.experimental import pallas as pl
from jax.experimental.pallas import tpu as pltpu
from jax.sharding import PartitionSpec as P

smearing = 0.3
PAD = 48
WIDE = 96
CHUNK = 2048
HALF = 23
SHARED = 22
TOP = 12
SLOT = 32
RING_Y = 4
RING_Z = 8


def send_kernel(rows_ref, share_ref, out_ref):
    for target in range(out_ref.shape[0]):
        out_ref[target] = share_ref[rows_ref[0, target]]


def pick_kernel(table_ref, arrived_ref, phase_ref, out_ref):
    for triplet in range(4):
        for member in range(3):
            block = arrived_ref[table_ref[triplet, member]]
            out_ref[2 * triplet, member, 0:12] = block
            out_ref[2 * triplet + 1, member, 0:12] = block
            fill = jnp.zeros((4, block.shape[1]), block.dtype)
            out_ref[2 * triplet, member, 12:16] = fill
            out_ref[2 * triplet + 1, member, 12:16] = fill
        out_ref[2 * triplet, 3] = phase_ref[triplet]
        out_ref[2 * triplet + 1, 3] = phase_ref[triplet]


def whole_record(members_ref, slot):
    parts = [members_ref[j, slot].astype(jnp.float32)[0:12] for j in range(8)]
    rows = jnp.concatenate(parts, axis=0)
    fill = jnp.zeros((WIDE, 38), jnp.float32)
    return jnp.concatenate([rows[:, 0:90], fill, rows[:, 90:180], fill], axis=1)


def operand_kernel(
    where_ref, members_ref, early_ref, late_ref, middle_ref, last_ref, tables_ref, scalars_ref
):
    rank, first, mult, color = where_ref[0], where_ref[1] == 0, where_ref[2], where_ref[3]
    f32 = jnp.float32
    records = [whole_record(members_ref, member) for member in range(3)]
    lead_r, lead_i = records[0][:, 0:128].T, records[0][:, 128:256].T

    def halves(array):
        low, high = array[0:PAD], array[45 : 45 + PAD]
        return jnp.where(first, low, high), jnp.where(first, high, low)

    def sides(array):
        low, high = array[:, 0:PAD], array[:, 45 : 45 + PAD]
        return jnp.where(first, low, high), jnp.where(first, high, low)

    row = lax.broadcasted_iota(jnp.int32, (PAD, WIDE), 0)
    column = lax.broadcasted_iota(jnp.int32, (PAD, WIDE), 1)

    def spread(array, start, count, again=False):
        taken = (column // 2 + start == row) & (column < 2 * count)
        if again:
            taken = taken & (row != SHARED)
        return jnp.dot(array, taken.astype(f32), preferred_element_type=f32)

    def turned(real, imag, offset):
        trig = members_ref[2 * ((rank + offset) & 3), 3].astype(f32)
        even = lax.broadcasted_iota(jnp.int32, (1, real.shape[1]), 1) % 2 == 0
        cosine = jnp.where(even, trig[0:1, 0:1], trig[0:1, 2:3])
        sine = jnp.where(even, trig[0:1, 1:2], trig[0:1, 3:4])
        return jnp.concatenate([cosine * real - sine * imag, cosine * imag + sine * real], axis=0)

    columns = []
    for array in (lead_r, lead_i):
        columns.append([halves(side) for side in sides(array)])
    same, differ = SHARED * color, SHARED * (1 - color)
    blocks = []
    for offset, start, count, width, again in (
        (0, 0, 45, WIDE, False),
        (3, same, HALF, PAD, False),
        (3, differ, HALF, PAD, True),
        (1, same, HALF, PAD, False),
        (1, differ, HALF, PAD, True),
    ):
        rows = []
        for h in range(2):
            real, imag = (
                spread(columns[i][0][h], start, count, again)[:, 0:width] for i in range(2)
            )
            rows.append(turned(real, imag, offset))
        blocks.append(jnp.concatenate(rows, axis=0))
    early_ref[...] = jnp.concatenate(blocks, axis=1).astype(early_ref.dtype)
    parts = []
    for side in range(2):
        for start, again in ((same, False), (differ, True)):
            for skip, count in ((0, TOP), (TOP, HALF - TOP)):
                real, imag = (
                    spread(columns[i][side][0], start + skip, count, again)[:, 0:SLOT]
                    for i in range(2)
                )
                parts.append(turned(real, imag, 2))
    late_ref[...] = jnp.concatenate(parts, axis=1).astype(late_ref.dtype)

    mid_r, mid_i = records[1][:, 0:128].T, records[1][:, 128:256].T
    within = lax.broadcasted_iota(jnp.int32, (WIDE, WIDE), 1) < 90
    real = jnp.where(within, mid_r[0:WIDE], 0.0)
    imag = jnp.where(within, mid_i[0:WIDE], 0.0)
    middle_ref[...] = jnp.concatenate(
        [jnp.concatenate([real, -imag], axis=1), jnp.concatenate([imag, real], axis=1)], axis=0
    ).astype(middle_ref.dtype)

    last_r, last_i = records[2][:, 0:128], records[2][:, 128:256]
    within = lax.broadcasted_iota(jnp.int32, (WIDE, 128), 0) < 90
    real = jnp.where(within, last_r, 0.0)
    imag = jnp.where(within, last_i, 0.0)
    zeros = jnp.zeros((32, 256), f32)
    last_ref[...] = jnp.concatenate(
        [
            jnp.concatenate([real, imag], axis=1),
            zeros,
            jnp.concatenate([-imag, real], axis=1),
            zeros,
        ],
        axis=0,
    ).astype(last_ref.dtype)

    row = lax.broadcasted_iota(jnp.int32, (WIDE, 128), 0)
    column = lax.broadcasted_iota(jnp.int32, (WIDE, 128), 1)
    one = jnp.where(row < 90, jnp.broadcast_to(mid_r[0:WIDE, 90:91], (WIDE, 128)), 1.0)
    two = jnp.where(column < 90, jnp.broadcast_to(last_r[90:91, :], (WIDE, 128)), 1.0)
    tables_ref[0] = one + two
    tables_ref[1] = one - two
    tables_ref[2] = 1.0 / (one * two)
    tables_ref[3] = jnp.broadcast_to(mid_i[0:WIDE, 90:91], (WIDE, 128)) + jnp.broadcast_to(
        last_i[90:91, :], (WIDE, 128)
    )
    zero = halves(lead_r[:, 90:91])[0]
    zero = jnp.where(lax.broadcasted_iota(jnp.int32, (PAD, 1), 0) < 45, zero, 1.0)
    scalars_ref[0] = jnp.broadcast_to(zero, (PAD, 128))
    scalars_ref[1] = jnp.broadcast_to(mult.astype(f32) / zero, (PAD, 128))


def rows_of(ref, cols, count):
    values = ref[:, :, cols]
    rows = values.shape[0] * values.shape[1]
    return jnp.pad(values.reshape(rows, values.shape[2]), ((0, count - rows), (0, 0)))


def early_kernel(lead_ref, own_ref, *refs):
    halves, mine_ref, far_refs = refs[:4], refs[4], refs[5:]
    total = own_ref.shape[2]
    for start in range(0, total, CHUNK):
        cols = slice(start, min(start + CHUNK, total))
        product = jnp.dot(
            lead_ref[...],
            jnp.concatenate(
                [rows_of(own_ref, cols, WIDE)] + [rows_of(ref, cols, PAD) for ref in halves], axis=0
            ),
            preferred_element_type=jnp.float32,
        )
        mine_ref[:, cols] = product[0:WIDE].astype(mine_ref.dtype)
        for i, far_ref in enumerate(far_refs):
            rows = product[WIDE + 32 * i : WIDE + 32 * i + 32]
            far_ref[:, cols] = rows.astype(far_ref.dtype)


def interaction_kernel(*refs):
    count = 17
    operands, out_ref, buffers = refs[:count], refs[count], refs[count + 1 : 2 * count + 1]
    flat, windows, mid_real, mid_imag, rate_acc, couple_acc, done = refs[2 * count + 1 :]
    scalars_ref, middle_ref, last_ref, tables_ref, late_ref = buffers[:5]
    late, mine_ref, others = buffers[5:13], buffers[13], buffers[14:]
    total = mine_ref.shape[1]
    pieces = [slice(at, min(at + CHUNK, total)) for at in range(0, total, CHUNK)]
    whole = {}
    for i in range(5):
        whole[i] = pltpu.make_async_copy(operands[i], buffers[i], done.at[i, 0])
    parts = {}
    for k, cols in enumerate(pieces):
        for i in range(5, count):
            where = (slice(None),) * (len(operands[i].shape) - 1) + (cols,)
            parts[i, k] = pltpu.make_async_copy(
                operands[i].at[where], buffers[i].at[where], done.at[i, k]
            )
    whole[4].start()
    for i in range(5, count):
        parts[i, 0].start()
    whole[2].start()
    for k in range(1, len(pieces)):
        for i in range(5, count):
            parts[i, k].start()
    for i in (0, 1, 3):
        whole[i].start()

    flat[:, 8064:8320] = jnp.zeros((WIDE, 256), flat.dtype)
    zeros = jnp.zeros((PAD, 128), jnp.float32)
    for b in range(90, WIDE):
        mid_real[pl.ds(b, PAD, stride=WIDE), :] = zeros
        mid_imag[pl.ds(b, PAD, stride=WIDE), :] = zeros

    def window_of(b):
        tile, shift = divmod(90 * b, 128)
        pair = flat[:, tile * 128 : tile * 128 + 256]
        window = pair[:, shift : shift + 128]
        windows[b * PAD : (b + 1) * PAD, 0:128] = window[0:PAD]
        windows[b * PAD : (b + 1) * PAD, 128:256] = window[PAD:]

    def product_of(group):
        product = jnp.dot(
            windows[group * 480 : (group + 1) * 480, :],
            last_ref[...],
            preferred_element_type=jnp.float32,
        )
        for i in range(10):
            rows = pl.ds(group * 10 + i, PAD, stride=WIDE)
            mid_real[rows, :] = product[i * PAD : (i + 1) * PAD, 0:128]
            mid_imag[rows, :] = product[i * PAD : (i + 1) * PAD, 128:256]

    whole[4].wait()
    b = 0
    for k, cols in enumerate(pieces):
        for i in range(5, count):
            parts[i, k].wait()
        if k == 0:
            whole[2].wait()
        other = jnp.concatenate([ref[:, cols].astype(jnp.float32) for ref in others], axis=0)
        both = mine_ref[:, cols].astype(jnp.float32) + other
        both = both + jnp.dot(
            late_ref[...],
            jnp.concatenate([rows_of(ref, cols, SLOT) for ref in late], axis=0),
            preferred_element_type=jnp.float32,
        )
        flat[:, cols] = both.astype(flat.dtype)
        ready = 8320 if cols.stop == total else cols.stop
        while b < 90 and 90 * b // 128 * 128 + 256 <= ready:
            window_of(b)
            b += 1
            if b % 10 == 0:
                product_of(b // 10 - 1)
    for i in (0, 1, 3):
        whole[i].wait()

    scaled = 0.5 / (smearing * smearing)
    def two_modes(s):
        low = pl.ds(s * WIDE, WIDE)
        high = pl.ds(s * WIDE + WIDE, WIDE)
        operand = jnp.concatenate(
            [
                jnp.concatenate([ref[low, :], ref[high, :]], axis=1).astype(jnp.bfloat16)
                for ref in (mid_real, mid_imag)
            ],
            axis=0,
        )
        value = jnp.dot(middle_ref[...], operand, preferred_element_type=jnp.float32)
        for i in range(2):
            real = value[0:WIDE, 128 * i : 128 * i + 128]
            imag = value[WIDE:, 128 * i : 128 * i + 128]
            freq = scalars_ref[0, pl.ds(s + i, 1), :]
            decays = freq - tables_ref[0]
            merges = freq + tables_ref[1]
            weight = (real * real + imag * imag) * (
                jnp.exp(-scaled * decays * decays) + jnp.exp(-scaled * merges * merges)
            )
            weight = weight * tables_ref[2] * scalars_ref[1, pl.ds(s + i, 1), :]
            at = pl.ds((s + i) * 8, 8)
            rate_acc[at, :] = jnp.sum(weight.reshape(WIDE // 8, 8, 128), axis=0)
            weight = weight * tables_ref[3]
            couple_acc[at, :] = jnp.sum(weight.reshape(WIDE // 8, 8, 128), axis=0)

    for i in range(24):
        two_modes(2 * i)

    sums = jnp.concatenate(
        [
            jnp.sum(rate_acc[...].reshape(PAD, 8, 128), axis=1),
            jnp.sum(couple_acc[...].reshape(PAD, 8, 128), axis=1),
        ],
        axis=0,
    )
    out_ref[:, 0:WIDE] = lax.dot_general(
        jnp.ones((8, 128), jnp.float32),
        sums,
        (((1,), (1,)), ((), ())),
        precision=lax.Precision.HIGHEST,
        preferred_element_type=jnp.float32,
    )[0:1]
    out_ref[:, WIDE:128] = jnp.zeros((1, 128 - WIDE), jnp.float32)


VMEM = pl.BlockSpec(memory_space=pltpu.VMEM)
SMEM = pl.BlockSpec(memory_space=pltpu.SMEM)
PARAMS = pltpu.CompilerParams(vmem_limit_bytes=56 << 20)


def grid_shift(step_y, step_z):
    return [
        (y * RING_Z + z, (y + step_y) % RING_Y * RING_Z + (z + step_z) % RING_Z)
        for y in range(RING_Y)
        for z in range(RING_Z)
    ]


def ring(count, step):
    return [(i, (i + step) % count) for i in range(count)]


def body(
    force_third,
    phase_angle,
    eigenvectors,
    frequencies,
    deviation,
    send_rows,
    trip_table,
    irreducible,
    multiplicity,
    drive_term,
    boundary,
):
    f32, b16 = jnp.float32, jnp.bfloat16
    clus = lax.axis_index("clus")
    mode = lax.axis_index("mode")
    trip = lax.axis_index("trip")
    color = (trip // RING_Z + trip % RING_Z) % 2
    group = ("clus", "mode")

    with jax.named_scope("records"):
        extra = jnp.concatenate([frequencies, deviation], axis=1)[:, None, :]
        record = jnp.concatenate(
            [eigenvectors, extra, jnp.zeros((extra.shape[0], 5, 180), b16)], axis=1
        )
        share = lax.dynamic_slice_in_dim(record, 12 * (2 * clus + mode), 12, 1)
        chosen = pl.pallas_call(
            send_kernel,
            out_shape=jax.ShapeDtypeStruct((send_rows.shape[1],) + share.shape[1:], b16),
            in_specs=[SMEM, VMEM],
            out_specs=VMEM,
            compiler_params=PARAMS,
        )(send_rows, share)
        arrived = lax.all_to_all(chosen, "trip", 0, 0, tiled=True)
        angles = phase_angle.astype(f32)
        trig = jnp.stack([jnp.cos(angles), jnp.sin(angles)], axis=1).astype(b16)
        phases = jnp.pad(trig.reshape(4, 4).T[:, None, :], ((0, 0), (0, 15), (0, 176)))

    with jax.named_scope("force"):
        own = jnp.transpose(force_third, (1, 0, 2))
        half = lax.dynamic_slice_in_dim(own, SHARED * color, HALF, 0)
        low = lax.ppermute(half, "clus", ring(4, 1))
        high = lax.ppermute(half, "clus", ring(4, 3))

    with jax.named_scope("force_second"):
        low, high, _ = lax.optimization_barrier((low, high, arrived))
        low_other = lax.ppermute(low, "trip", grid_shift(1, 0))
        high_other = lax.ppermute(high, "trip", grid_shift(0, 1))
        top = lax.ppermute(low[:TOP], "clus", ring(4, 1))
        bottom = lax.ppermute(high[TOP:], "clus", ring(4, 3))

    with jax.named_scope("members"):
        picks = pl.pallas_call(
            pick_kernel,
            out_shape=jax.ShapeDtypeStruct((8, 4, 16, 180), b16),
            in_specs=[SMEM, VMEM, VMEM],
            out_specs=VMEM,
            compiler_params=PARAMS,
        )(trip_table, arrived, phases)
        members = lax.all_to_all(picks, group, 0, 0, tiled=True)

    with jax.named_scope("force_shared"):
        sent_top, sent_bottom, _ = lax.optimization_barrier((top, bottom, members))
        top_other = lax.ppermute(sent_top, "trip", grid_shift(-1, 0))
        bottom_other = lax.ppermute(sent_bottom, "trip", grid_shift(0, -1))

    with jax.named_scope("operands"):
        mult = lax.dynamic_index_in_dim(multiplicity, clus, 0, keepdims=False)
        where = jnp.stack([clus, mode, mult, color]).astype(jnp.int32)
        early, late, mid, last_all, tables, scalars = pl.pallas_call(
            operand_kernel,
            out_shape=(
                jax.ShapeDtypeStruct((2 * WIDE, 3 * WIDE), b16),
                jax.ShapeDtypeStruct((WIDE, 8 * SLOT), b16),
                jax.ShapeDtypeStruct((2 * WIDE, 2 * WIDE), b16),
                jax.ShapeDtypeStruct((256, 256), b16),
                jax.ShapeDtypeStruct((4, WIDE, 128), f32),
                jax.ShapeDtypeStruct((2, PAD, 128), f32),
            ),
            in_specs=[SMEM, VMEM],
            out_specs=(VMEM,) * 6,
            compiler_params=PARAMS,
        )(where, members)

    with jax.named_scope("contract"):
        total = force_third.shape[2]
        swap = [(0, 1), (1, 0)]
        mine, *far = pl.pallas_call(
            early_kernel,
            out_shape=(jax.ShapeDtypeStruct((WIDE, total), b16),)
            + (jax.ShapeDtypeStruct((WIDE // 3, total), b16),) * 3,
            in_specs=[VMEM] * 6,
            out_specs=(VMEM,) * 4,
            compiler_params=PARAMS,
            cost_estimate=pl.CostEstimate(
                flops=2 * 192 * 288 * total, bytes_accessed=1200 * total, transcendentals=0
            ),
        )(early, own, low, low_other, high, high_other)
        other = [lax.ppermute(rows, "mode", swap) for rows in far]
        late_rows = [top, bottom, top_other, bottom_other]
        late_rows += [lax.ppermute(rows, "mode", swap) for rows in late_rows]

    with jax.named_scope("interaction"):
        inputs = (scalars, mid, last_all, tables, late, *late_rows, mine, *other)
        sums = pl.pallas_call(
            interaction_kernel,
            out_shape=jax.ShapeDtypeStruct((1, 128), f32),
            in_specs=[pl.BlockSpec(memory_space=pl.ANY)] * len(inputs),
            out_specs=VMEM,
            scratch_shapes=[pltpu.VMEM(x.shape, x.dtype) for x in inputs]
            + [
                pltpu.VMEM((WIDE, 8320), b16),
                pltpu.VMEM((90 * PAD, 256), b16),
                pltpu.VMEM((PAD * WIDE, 128), f32),
                pltpu.VMEM((PAD * WIDE, 128), f32),
                pltpu.VMEM((8 * PAD, 128), f32),
                pltpu.VMEM((8 * PAD, 128), f32),
                pltpu.SemaphoreType.DMA((len(inputs), 4)),
            ],
            compiler_params=PARAMS,
        )(*inputs)
    with jax.named_scope("collect"):
        own_row = sums
        rows = [own_row] + [lax.ppermute(own_row, "clus", ring(4, step)) for step in (1, 2, 3)]
        points = jnp.arange(32, dtype=jnp.int32)
        partial = jnp.zeros((32, 128), f32)
        for step in range(4):
            point = lax.dynamic_index_in_dim(irreducible, (clus - step) % 4, 0, keepdims=False)
            partial = partial + jnp.where((points == point)[:, None], rows[step], 0.0)
        received = lax.all_to_all(partial[:, None, :], "trip", 0, 0, tiled=True)
        final = jnp.sum(received[:, 0, :], axis=0)[None, :]
        gamma_total = final[:, 0:45] + boundary
        return gamma_total, (drive_term + final[:, PAD : PAD + 45]) / gamma_total


def solution(mesh):
    return jax.shard_map(
        body,
        mesh=mesh,
        in_specs=(
            P("clus", "mode", None),
            P("clus", "trip"),
            P("trip", None, None),
            P("trip", None),
            P("trip", None),
            P("trip", None),
            P("trip", None),
            P("trip"),
            P("trip"),
            P("trip", "mode"),
            P("trip", "mode"),
        ),
        out_specs=(P("trip", "mode"), P("trip", "mode")),
        check_vma=False,
    )
```

```python
import jax
import jax.numpy as jnp
from jax import lax
from jax.experimental import pallas as pl
from jax.experimental.pallas import tpu as pltpu
from jax.sharding import PartitionSpec as P

smearing = 0.3
PAD = 48
WIDE = 96
CHUNK = 2048
TOP = 23


def send_kernel(rows_ref, share_ref, out_ref):
    for target in range(out_ref.shape[0]):
        out_ref[target] = share_ref[rows_ref[0, target]]


def pick_kernel(table_ref, arrived_ref, phase_ref, out_ref):
    for triplet in range(4):
        for member in range(3):
            block = arrived_ref[table_ref[triplet, member]]
            out_ref[2 * triplet, member, 0:12] = block
            out_ref[2 * triplet + 1, member, 0:12] = block
            fill = jnp.zeros((4, block.shape[1]), block.dtype)
            out_ref[2 * triplet, member, 12:16] = fill
            out_ref[2 * triplet + 1, member, 12:16] = fill
        out_ref[2 * triplet, 3] = phase_ref[triplet]
        out_ref[2 * triplet + 1, 3] = phase_ref[triplet]


def whole_record(members_ref, slot):
    parts = [members_ref[j, slot].astype(jnp.float32)[0:12] for j in range(8)]
    rows = jnp.concatenate(parts, axis=0)
    fill = jnp.zeros((WIDE, 38), jnp.float32)
    return jnp.concatenate([rows[:, 0:90], fill, rows[:, 90:180], fill], axis=1)


def operand_kernel(
    where_ref, members_ref, early_ref, late_ref, middle_ref, last_ref, tables_ref, scalars_ref
):
    rank, first, mult = where_ref[0], where_ref[1] == 0, where_ref[2]
    f32 = jnp.float32
    records = [whole_record(members_ref, member) for member in range(3)]
    lead_r, lead_i = records[0][:, 0:128].T, records[0][:, 128:256].T

    def halves(array):
        low, high = array[0:PAD], array[45 : 45 + PAD]
        return jnp.where(first, low, high), jnp.where(first, high, low)

    def sides(array):
        low, high = array[:, 0:PAD], array[:, 45 : 45 + PAD]
        return jnp.where(first, low, high), jnp.where(first, high, low)

    row = lax.broadcasted_iota(jnp.int32, (PAD, WIDE), 0)
    column = lax.broadcasted_iota(jnp.int32, (PAD, WIDE), 1)

    def spread(array, start, count):
        taken = (column // 2 + start == row) & (column < 2 * count)
        return jnp.dot(array, taken.astype(f32), preferred_element_type=f32)

    def turned(real, imag, offset):
        trig = members_ref[2 * ((rank + offset) & 3), 3].astype(f32)
        even = lax.broadcasted_iota(jnp.int32, (1, real.shape[1]), 1) % 2 == 0
        cosine = jnp.where(even, trig[0:1, 0:1], trig[0:1, 2:3])
        sine = jnp.where(even, trig[0:1, 1:2], trig[0:1, 3:4])
        return jnp.concatenate([cosine * real - sine * imag, cosine * imag + sine * real], axis=0)

    columns = []
    for array in (lead_r, lead_i):
        columns.append([halves(side) for side in sides(array)])
    blocks = []
    for offset, start, count, width in (
        (0, 0, 45, WIDE),
        (3, 0, TOP, PAD),
        (3, TOP, 45 - TOP, PAD),
        (1, 0, TOP, PAD),
        (1, TOP, 45 - TOP, PAD),
    ):
        rows = []
        for h in range(2):
            real, imag = (spread(columns[i][0][h], start, count)[:, 0:width] for i in range(2))
            rows.append(turned(real, imag, offset))
        blocks.append(jnp.concatenate(rows, axis=0))
    early_ref[...] = jnp.concatenate(blocks, axis=1).astype(early_ref.dtype)
    parts = []
    for side in range(2):
        for start, count in ((0, TOP), (TOP, 45 - TOP)):
            real, imag = (spread(columns[i][side][0], start, count)[:, 0:PAD] for i in range(2))
            parts.append(turned(real, imag, 2))
    late_ref[...] = jnp.concatenate(parts, axis=1).astype(late_ref.dtype)

    mid_r, mid_i = records[1][:, 0:128].T, records[1][:, 128:256].T
    within = lax.broadcasted_iota(jnp.int32, (WIDE, WIDE), 1) < 90
    real = jnp.where(within, mid_r[0:WIDE], 0.0)
    imag = jnp.where(within, mid_i[0:WIDE], 0.0)
    middle_ref[...] = jnp.concatenate(
        [jnp.concatenate([real, -imag], axis=1), jnp.concatenate([imag, real], axis=1)], axis=0
    ).astype(middle_ref.dtype)

    last_r, last_i = records[2][:, 0:128], records[2][:, 128:256]
    within = lax.broadcasted_iota(jnp.int32, (WIDE, 128), 0) < 90
    real = jnp.where(within, last_r, 0.0)
    imag = jnp.where(within, last_i, 0.0)
    zeros = jnp.zeros((32, 256), f32)
    last_ref[...] = jnp.concatenate(
        [
            jnp.concatenate([real, imag], axis=1),
            zeros,
            jnp.concatenate([-imag, real], axis=1),
            zeros,
        ],
        axis=0,
    ).astype(last_ref.dtype)

    row = lax.broadcasted_iota(jnp.int32, (WIDE, 128), 0)
    column = lax.broadcasted_iota(jnp.int32, (WIDE, 128), 1)
    one = jnp.where(row < 90, jnp.broadcast_to(mid_r[0:WIDE, 90:91], (WIDE, 128)), 1.0)
    two = jnp.where(column < 90, jnp.broadcast_to(last_r[90:91, :], (WIDE, 128)), 1.0)
    tables_ref[0] = one + two
    tables_ref[1] = one - two
    tables_ref[2] = 1.0 / (one * two)
    tables_ref[3] = jnp.broadcast_to(mid_i[0:WIDE, 90:91], (WIDE, 128)) + jnp.broadcast_to(
        last_i[90:91, :], (WIDE, 128)
    )
    zero = halves(lead_r[:, 90:91])[0]
    zero = jnp.where(lax.broadcasted_iota(jnp.int32, (PAD, 1), 0) < 45, zero, 1.0)
    scalars_ref[0] = jnp.broadcast_to(zero, (PAD, 128))
    scalars_ref[1] = jnp.broadcast_to(mult.astype(f32) / zero, (PAD, 128))


def rows_of(ref, cols, count):
    values = ref[:, :, cols]
    rows = values.shape[0] * values.shape[1]
    return jnp.pad(values.reshape(rows, values.shape[2]), ((0, count - rows), (0, 0)))


def early_kernel(lead_ref, own_ref, *refs):
    halves, mine_ref, far_refs = refs[:4], refs[4], refs[5:]
    total = own_ref.shape[2]
    for start in range(0, total, CHUNK):
        cols = slice(start, min(start + CHUNK, total))
        product = jnp.dot(
            lead_ref[...],
            jnp.concatenate(
                [rows_of(own_ref, cols, WIDE)] + [rows_of(ref, cols, PAD) for ref in halves], axis=0
            ),
            preferred_element_type=jnp.float32,
        )
        mine_ref[:, cols] = product[0:WIDE].astype(mine_ref.dtype)
        for i, far_ref in enumerate(far_refs):
            rows = product[WIDE + 48 * i : WIDE + 48 * i + 48]
            far_ref[:, cols] = rows.astype(far_ref.dtype)


def interaction_kernel(*refs):
    count = 12
    operands, out_ref, buffers = refs[:count], refs[count], refs[count + 1 : 2 * count + 1]
    flat, windows, mid_real, mid_imag, rate_acc, couple_acc, done = refs[2 * count + 1 :]
    scalars_ref, middle_ref, last_ref, tables_ref, late_ref = buffers[:5]
    top_ref, bottom_ref, far_top_ref, far_bottom_ref, mine_ref = buffers[5:10]
    late, others = buffers[5:9], buffers[10:]
    total = mine_ref.shape[1]
    pieces = [slice(at, min(at + CHUNK, total)) for at in range(0, total, CHUNK)]
    whole = {}
    for i in range(5):
        whole[i] = pltpu.make_async_copy(operands[i], buffers[i], done.at[i, 0])
    parts = {}
    for k, cols in enumerate(pieces):
        for i in range(5, count):
            where = (slice(None),) * (len(operands[i].shape) - 1) + (cols,)
            parts[i, k] = pltpu.make_async_copy(
                operands[i].at[where], buffers[i].at[where], done.at[i, k]
            )
    whole[4].start()
    for i in range(5, count):
        parts[i, 0].start()
    whole[2].start()
    for k in range(1, len(pieces)):
        for i in range(5, count):
            parts[i, k].start()
    for i in (0, 1, 3):
        whole[i].start()

    flat[:, 8064:8320] = jnp.zeros((WIDE, 256), flat.dtype)
    zeros = jnp.zeros((PAD, 128), jnp.float32)
    for b in range(90, WIDE):
        mid_real[pl.ds(b, PAD, stride=WIDE), :] = zeros
        mid_imag[pl.ds(b, PAD, stride=WIDE), :] = zeros

    def window_of(b):
        tile, shift = divmod(90 * b, 128)
        pair = flat[:, tile * 128 : tile * 128 + 256]
        window = pair[:, shift : shift + 128]
        windows[b * PAD : (b + 1) * PAD, 0:128] = window[0:PAD]
        windows[b * PAD : (b + 1) * PAD, 128:256] = window[PAD:]

    def product_of(group):
        product = jnp.dot(
            windows[group * 480 : (group + 1) * 480, :],
            last_ref[...],
            preferred_element_type=jnp.float32,
        )
        for i in range(10):
            rows = pl.ds(group * 10 + i, PAD, stride=WIDE)
            mid_real[rows, :] = product[i * PAD : (i + 1) * PAD, 0:128]
            mid_imag[rows, :] = product[i * PAD : (i + 1) * PAD, 128:256]

    whole[4].wait()
    b = 0
    for k, cols in enumerate(pieces):
        for i in range(5, count):
            parts[i, k].wait()
        if k == 0:
            whole[2].wait()
        other = jnp.concatenate([ref[:, cols].astype(jnp.float32) for ref in others], axis=0)
        both = mine_ref[:, cols].astype(jnp.float32) + other
        both = both + jnp.dot(
            late_ref[...],
            jnp.concatenate([rows_of(ref, cols, PAD) for ref in late], axis=0),
            preferred_element_type=jnp.float32,
        )
        flat[:, cols] = both.astype(flat.dtype)
        ready = 8320 if cols.stop == total else cols.stop
        while b < 90 and 90 * b // 128 * 128 + 256 <= ready:
            window_of(b)
            b += 1
            if b % 10 == 0:
                product_of(b // 10 - 1)
    for i in (0, 1, 3):
        whole[i].wait()

    scaled = 0.5 / (smearing * smearing)
    def two_modes(s):
        low = pl.ds(s * WIDE, WIDE)
        high = pl.ds(s * WIDE + WIDE, WIDE)
        operand = jnp.concatenate(
            [
                jnp.concatenate([ref[low, :], ref[high, :]], axis=1).astype(jnp.bfloat16)
                for ref in (mid_real, mid_imag)
            ],
            axis=0,
        )
        value = jnp.dot(middle_ref[...], operand, preferred_element_type=jnp.float32)
        for i in range(2):
            real = value[0:WIDE, 128 * i : 128 * i + 128]
            imag = value[WIDE:, 128 * i : 128 * i + 128]
            freq = scalars_ref[0, pl.ds(s + i, 1), :]
            decays = freq - tables_ref[0]
            merges = freq + tables_ref[1]
            weight = (real * real + imag * imag) * (
                jnp.exp(-scaled * decays * decays) + jnp.exp(-scaled * merges * merges)
            )
            weight = weight * tables_ref[2] * scalars_ref[1, pl.ds(s + i, 1), :]
            at = pl.ds((s + i) * 8, 8)
            rate_acc[at, :] = jnp.sum(weight.reshape(WIDE // 8, 8, 128), axis=0)
            weight = weight * tables_ref[3]
            couple_acc[at, :] = jnp.sum(weight.reshape(WIDE // 8, 8, 128), axis=0)

    for i in range(24):
        two_modes(2 * i)

    sums = jnp.concatenate(
        [
            jnp.sum(rate_acc[...].reshape(PAD, 8, 128), axis=1),
            jnp.sum(couple_acc[...].reshape(PAD, 8, 128), axis=1),
        ],
        axis=0,
    )
    out_ref[:, 0:WIDE] = lax.dot_general(
        jnp.ones((8, 128), jnp.float32),
        sums,
        (((1,), (1,)), ((), ())),
        precision=lax.Precision.HIGHEST,
        preferred_element_type=jnp.float32,
    )[0:1]
    out_ref[:, WIDE:128] = jnp.zeros((1, 128 - WIDE), jnp.float32)


VMEM = pl.BlockSpec(memory_space=pltpu.VMEM)
SMEM = pl.BlockSpec(memory_space=pltpu.SMEM)
PARAMS = pltpu.CompilerParams(vmem_limit_bytes=56 << 20)


def ring(count, step):
    return [(i, (i + step) % count) for i in range(count)]


def body(
    force_third,
    phase_angle,
    eigenvectors,
    frequencies,
    deviation,
    send_rows,
    trip_table,
    irreducible,
    multiplicity,
    drive_term,
    boundary,
):
    f32, b16 = jnp.float32, jnp.bfloat16
    clus = lax.axis_index("clus")
    mode = lax.axis_index("mode")
    group = ("clus", "mode")

    with jax.named_scope("records"):
        extra = jnp.concatenate([frequencies, deviation], axis=1)[:, None, :]
        record = jnp.concatenate(
            [eigenvectors, extra, jnp.zeros((extra.shape[0], 5, 180), b16)], axis=1
        )
        share = lax.dynamic_slice_in_dim(record, 12 * (2 * clus + mode), 12, 1)
        chosen = pl.pallas_call(
            send_kernel,
            out_shape=jax.ShapeDtypeStruct((send_rows.shape[1],) + share.shape[1:], b16),
            in_specs=[SMEM, VMEM],
            out_specs=VMEM,
            compiler_params=PARAMS,
        )(send_rows, share)
        arrived = lax.all_to_all(chosen, "trip", 0, 0, tiled=True)
        angles = phase_angle.astype(f32)
        trig = jnp.stack([jnp.cos(angles), jnp.sin(angles)], axis=1).astype(b16)
        phases = jnp.pad(trig.reshape(4, 4).T[:, None, :], ((0, 0), (0, 15), (0, 176)))

    with jax.named_scope("force"):
        own = jnp.transpose(force_third, (1, 0, 2))
        own_top, own_bottom = own[:TOP], own[TOP:]
        low_top = lax.ppermute(own_top, "clus", ring(4, 1))
        high_bottom = lax.ppermute(own_bottom, "clus", ring(4, 3))
        own_top, own_bottom, _ = lax.optimization_barrier((own_top, own_bottom, chosen))
        low_bottom = lax.ppermute(own_bottom, "clus", ring(4, 1))
        high_top = lax.ppermute(own_top, "clus", ring(4, 3))

    with jax.named_scope("force_second"):
        passed_top, passed_bottom, _ = lax.optimization_barrier((low_top, high_bottom, arrived))
        top = lax.ppermute(passed_top, "clus", ring(4, 1))
        bottom = lax.ppermute(passed_bottom, "clus", ring(4, 3))

    with jax.named_scope("members"):
        picks = pl.pallas_call(
            pick_kernel,
            out_shape=jax.ShapeDtypeStruct((8, 4, 16, 180), b16),
            in_specs=[SMEM, VMEM, VMEM],
            out_specs=VMEM,
            compiler_params=PARAMS,
        )(trip_table, arrived, phases)
        members = lax.all_to_all(picks, group, 0, 0, tiled=True)

    with jax.named_scope("operands"):
        mult = lax.dynamic_index_in_dim(multiplicity, clus, 0, keepdims=False)
        where = jnp.stack([clus, mode, mult]).astype(jnp.int32)
        early, late, mid, last_all, tables, scalars = pl.pallas_call(
            operand_kernel,
            out_shape=(
                jax.ShapeDtypeStruct((2 * WIDE, 3 * WIDE), b16),
                jax.ShapeDtypeStruct((WIDE, 4 * PAD), b16),
                jax.ShapeDtypeStruct((2 * WIDE, 2 * WIDE), b16),
                jax.ShapeDtypeStruct((256, 256), b16),
                jax.ShapeDtypeStruct((4, WIDE, 128), f32),
                jax.ShapeDtypeStruct((2, PAD, 128), f32),
            ),
            in_specs=[SMEM, VMEM],
            out_specs=(VMEM,) * 6,
            compiler_params=PARAMS,
        )(where, members)

    with jax.named_scope("contract"):
        total = force_third.shape[2]
        swap = [(0, 1), (1, 0)]
        mine, *far = pl.pallas_call(
            early_kernel,
            out_shape=(jax.ShapeDtypeStruct((WIDE, total), b16),)
            + (jax.ShapeDtypeStruct((WIDE // 2, total), b16),) * 2,
            in_specs=[VMEM] * 6,
            out_specs=(VMEM,) * 3,
            compiler_params=PARAMS,
            cost_estimate=pl.CostEstimate(
                flops=2 * 192 * 288 * total, bytes_accessed=1200 * total, transcendentals=0
            ),
        )(early, own, low_top, low_bottom, high_top, high_bottom)
        other = [lax.ppermute(rows, "mode", swap) for rows in far]
        far_top = lax.ppermute(top, "mode", swap)
        far_bottom = lax.ppermute(bottom, "mode", swap)

    with jax.named_scope("interaction"):
        inputs = (scalars, mid, last_all, tables, late, top, bottom, far_top, far_bottom, mine, *other)
        sums = pl.pallas_call(
            interaction_kernel,
            out_shape=jax.ShapeDtypeStruct((1, 128), f32),
            in_specs=[pl.BlockSpec(memory_space=pl.ANY)] * len(inputs),
            out_specs=VMEM,
            scratch_shapes=[pltpu.VMEM(x.shape, x.dtype) for x in inputs]
            + [
                pltpu.VMEM((WIDE, 8320), b16),
                pltpu.VMEM((90 * PAD, 256), b16),
                pltpu.VMEM((PAD * WIDE, 128), f32),
                pltpu.VMEM((PAD * WIDE, 128), f32),
                pltpu.VMEM((8 * PAD, 128), f32),
                pltpu.VMEM((8 * PAD, 128), f32),
                pltpu.SemaphoreType.DMA((len(inputs), 4)),
            ],
            compiler_params=PARAMS,
        )(*inputs)
    with jax.named_scope("collect"):
        own_row = sums
        rows = [own_row] + [lax.ppermute(own_row, "clus", ring(4, step)) for step in (1, 2, 3)]
        points = jnp.arange(32, dtype=jnp.int32)
        partial = jnp.zeros((32, 128), f32)
        for step in range(4):
            point = lax.dynamic_index_in_dim(irreducible, (clus - step) % 4, 0, keepdims=False)
            partial = partial + jnp.where((points == point)[:, None], rows[step], 0.0)
        received = lax.all_to_all(partial[:, None, :], "trip", 0, 0, tiled=True)
        final = jnp.sum(received[:, 0, :], axis=0)[None, :]
        gamma_total = final[:, 0:45] + boundary
        return gamma_total, (drive_term + final[:, PAD : PAD + 45]) / gamma_total


def solution(mesh):
    return jax.shard_map(
        body,
        mesh=mesh,
        in_specs=(
            P("clus", "mode", None),
            P("clus", "trip"),
            P("trip", None, None),
            P("trip", None),
            P("trip", None),
            P("trip", None),
            P("trip", None),
            P("trip"),
            P("trip"),
            P("trip", "mode"),
            P("trip", "mode"),
        ),
        out_specs=(P("trip", "mode"), P("trip", "mode")),
        check_vma=False,
    )
```

```python
import jax
import jax.numpy as jnp
from jax import lax
from jax.experimental import pallas as pl
from jax.experimental.pallas import tpu as pltpu
from jax.sharding import PartitionSpec as P

smearing = 0.3
PAD = 48
WIDE = 96
CHUNK = 2048
HALF = 23
SHARED = 22
TOP = 12
SLOT = 32
RING_Y = 4
RING_Z = 8


def send_kernel(rows_ref, share_ref, out_ref):
    for z in range(RING_Z):
        for y in range(RING_Y):
            out_ref[z, y] = share_ref[rows_ref[0, y * RING_Z + z]]


def pick_kernel(table_ref, arrived_ref, phase_ref, out_ref):
    for triplet in range(4):
        for member in range(3):
            source = table_ref[triplet, member]
            block = arrived_ref[source & (RING_Z - 1), source >> 3]
            out_ref[2 * triplet, member] = block
            out_ref[2 * triplet + 1, member] = block
        out_ref[2 * triplet, 3] = phase_ref[triplet]
        out_ref[2 * triplet + 1, 3] = phase_ref[triplet]


def whole_record(members_ref, slot):
    parts = [members_ref[j, slot].astype(jnp.float32)[0:12] for j in range(8)]
    rows = jnp.concatenate(parts, axis=0)
    fill = jnp.zeros((WIDE, 38), jnp.float32)
    return jnp.concatenate([rows[:, 0:90], fill, rows[:, 90:180], fill], axis=1)


def operand_kernel(
    where_ref, members_ref, early_ref, late_ref, middle_ref, last_ref, tables_ref, scalars_ref
):
    rank, first, mult, color = where_ref[0], where_ref[1] == 0, where_ref[2], where_ref[3]
    f32 = jnp.float32
    records = [whole_record(members_ref, member) for member in range(3)]
    lead_r, lead_i = records[0][:, 0:128].T, records[0][:, 128:256].T

    def halves(array):
        low, high = array[0:PAD], array[45 : 45 + PAD]
        return jnp.where(first, low, high), jnp.where(first, high, low)

    def sides(array):
        low, high = array[:, 0:PAD], array[:, 45 : 45 + PAD]
        return jnp.where(first, low, high), jnp.where(first, high, low)

    row = lax.broadcasted_iota(jnp.int32, (PAD, WIDE), 0)
    column = lax.broadcasted_iota(jnp.int32, (PAD, WIDE), 1)

    def spread(array, start, count, again=False):
        taken = (column // 2 + start == row) & (column < 2 * count)
        if again:
            taken = taken & (row != SHARED)
        return jnp.dot(array, taken.astype(f32), preferred_element_type=f32)

    def turned(real, imag, offset):
        trig = members_ref[2 * ((rank + offset) & 3), 3].astype(f32)
        even = lax.broadcasted_iota(jnp.int32, (1, real.shape[1]), 1) % 2 == 0
        cosine = jnp.where(even, trig[0:1, 0:1], trig[0:1, 2:3])
        sine = jnp.where(even, trig[0:1, 1:2], trig[0:1, 3:4])
        return jnp.concatenate([cosine * real - sine * imag, cosine * imag + sine * real], axis=0)

    columns = []
    for array in (lead_r, lead_i):
        columns.append([halves(side) for side in sides(array)])
    same, differ = SHARED * color, SHARED * (1 - color)
    blocks = []
    for offset, start, count, width, again in (
        (0, 0, 45, WIDE, False),
        (3, same, HALF, PAD, False),
        (3, differ, HALF, PAD, True),
        (1, same, HALF, PAD, False),
        (1, differ, HALF, PAD, True),
    ):
        rows = []
        for h in range(2):
            real, imag = (
                spread(columns[i][0][h], start, count, again)[:, 0:width] for i in range(2)
            )
            rows.append(turned(real, imag, offset))
        blocks.append(jnp.concatenate(rows, axis=0))
    early_ref[...] = jnp.concatenate(blocks, axis=1).astype(early_ref.dtype)
    parts = []
    for side in range(2):
        for start, again in ((same, False), (differ, True)):
            for skip, count in ((0, TOP), (TOP, HALF - TOP)):
                real, imag = (
                    spread(columns[i][side][0], start + skip, count, again)[:, 0:SLOT]
                    for i in range(2)
                )
                parts.append(turned(real, imag, 2))
    late_ref[...] = jnp.concatenate(parts, axis=1).astype(late_ref.dtype)

    mid_r, mid_i = records[1][:, 0:128].T, records[1][:, 128:256].T
    within = lax.broadcasted_iota(jnp.int32, (WIDE, WIDE), 1) < 90
    real = jnp.where(within, mid_r[0:WIDE], 0.0)
    imag = jnp.where(within, mid_i[0:WIDE], 0.0)
    middle_ref[...] = jnp.concatenate(
        [jnp.concatenate([real, -imag], axis=1), jnp.concatenate([imag, real], axis=1)], axis=0
    ).astype(middle_ref.dtype)

    last_r, last_i = records[2][:, 0:128], records[2][:, 128:256]
    within = lax.broadcasted_iota(jnp.int32, (WIDE, 128), 0) < 90
    real = jnp.where(within, last_r, 0.0)
    imag = jnp.where(within, last_i, 0.0)
    zeros = jnp.zeros((32, 256), f32)
    last_ref[...] = jnp.concatenate(
        [
            jnp.concatenate([real, imag], axis=1),
            zeros,
            jnp.concatenate([-imag, real], axis=1),
            zeros,
        ],
        axis=0,
    ).astype(last_ref.dtype)

    row = lax.broadcasted_iota(jnp.int32, (WIDE, 128), 0)
    column = lax.broadcasted_iota(jnp.int32, (WIDE, 128), 1)
    one = jnp.where(row < 90, jnp.broadcast_to(mid_r[0:WIDE, 90:91], (WIDE, 128)), 1.0)
    two = jnp.where(column < 90, jnp.broadcast_to(last_r[90:91, :], (WIDE, 128)), 1.0)
    tables_ref[0] = one + two
    tables_ref[1] = one - two
    tables_ref[2] = 1.0 / (one * two)
    tables_ref[3] = jnp.broadcast_to(mid_i[0:WIDE, 90:91], (WIDE, 128)) + jnp.broadcast_to(
        last_i[90:91, :], (WIDE, 128)
    )
    zero = halves(lead_r[:, 90:91])[0]
    zero = jnp.where(lax.broadcasted_iota(jnp.int32, (PAD, 1), 0) < 45, zero, 1.0)
    scalars_ref[0] = jnp.broadcast_to(zero, (PAD, 128))
    scalars_ref[1] = jnp.broadcast_to(mult.astype(f32) / zero, (PAD, 128))


def rows_of(ref, cols, count):
    values = ref[:, :, cols]
    rows = values.shape[0] * values.shape[1]
    return jnp.pad(values.reshape(rows, values.shape[2]), ((0, count - rows), (0, 0)))


def early_kernel(lead_ref, own_ref, *refs):
    halves, mine_ref, far_refs = refs[:4], refs[4], refs[5:]
    total = own_ref.shape[2]
    for start in range(0, total, CHUNK):
        cols = slice(start, min(start + CHUNK, total))
        product = jnp.dot(
            lead_ref[...],
            jnp.concatenate(
                [rows_of(own_ref, cols, WIDE)] + [rows_of(ref, cols, PAD) for ref in halves], axis=0
            ),
            preferred_element_type=jnp.float32,
        )
        mine_ref[:, cols] = product[0:WIDE].astype(mine_ref.dtype)
        for i, far_ref in enumerate(far_refs):
            rows = product[WIDE + 32 * i : WIDE + 32 * i + 32]
            far_ref[:, cols] = rows.astype(far_ref.dtype)


def interaction_kernel(*refs):
    count = 17
    operands, out_ref, buffers = refs[:count], refs[count], refs[count + 1 : 2 * count + 1]
    flat, windows, mid_real, mid_imag, rate_acc, couple_acc, done = refs[2 * count + 1 :]
    scalars_ref, middle_ref, last_ref, tables_ref, late_ref = buffers[:5]
    late, mine_ref, others = buffers[5:13], buffers[13], buffers[14:]
    total = mine_ref.shape[1]
    pieces = [slice(at, min(at + CHUNK, total)) for at in range(0, total, CHUNK)]
    whole = {}
    for i in range(5):
        whole[i] = pltpu.make_async_copy(operands[i], buffers[i], done.at[i, 0])
    parts = {}
    for k, cols in enumerate(pieces):
        for i in range(5, count):
            where = (slice(None),) * (len(operands[i].shape) - 1) + (cols,)
            parts[i, k] = pltpu.make_async_copy(
                operands[i].at[where], buffers[i].at[where], done.at[i, k]
            )
    whole[4].start()
    for i in range(5, count):
        parts[i, 0].start()
    whole[2].start()
    for k in range(1, len(pieces)):
        for i in range(5, count):
            parts[i, k].start()
    for i in (0, 1, 3):
        whole[i].start()

    flat[:, 8064:8320] = jnp.zeros((WIDE, 256), flat.dtype)
    zeros = jnp.zeros((PAD, 128), jnp.float32)
    for b in range(90, WIDE):
        mid_real[pl.ds(b, PAD, stride=WIDE), :] = zeros
        mid_imag[pl.ds(b, PAD, stride=WIDE), :] = zeros

    def window_of(b):
        tile, shift = divmod(90 * b, 128)
        pair = flat[:, tile * 128 : tile * 128 + 256]
        window = pair[:, shift : shift + 128]
        windows[b * PAD : (b + 1) * PAD, 0:128] = window[0:PAD]
        windows[b * PAD : (b + 1) * PAD, 128:256] = window[PAD:]

    def product_of(group):
        product = jnp.dot(
            windows[group * 480 : (group + 1) * 480, :],
            last_ref[...],
            preferred_element_type=jnp.float32,
        )
        for i in range(10):
            rows = pl.ds(group * 10 + i, PAD, stride=WIDE)
            mid_real[rows, :] = product[i * PAD : (i + 1) * PAD, 0:128]
            mid_imag[rows, :] = product[i * PAD : (i + 1) * PAD, 128:256]

    whole[4].wait()
    b = 0
    for k, cols in enumerate(pieces):
        for i in range(5, count):
            parts[i, k].wait()
        if k == 0:
            whole[2].wait()
        other = jnp.concatenate([ref[:, cols].astype(jnp.float32) for ref in others], axis=0)
        both = mine_ref[:, cols].astype(jnp.float32) + other
        both = both + jnp.dot(
            late_ref[...],
            jnp.concatenate([rows_of(ref, cols, SLOT) for ref in late], axis=0),
            preferred_element_type=jnp.float32,
        )
        flat[:, cols] = both.astype(flat.dtype)
        ready = 8320 if cols.stop == total else cols.stop
        while b < 90 and 90 * b // 128 * 128 + 256 <= ready:
            window_of(b)
            b += 1
            if b % 10 == 0:
                product_of(b // 10 - 1)
    for i in (0, 1, 3):
        whole[i].wait()

    scaled = 0.5 / (smearing * smearing)
    def two_modes(s):
        low = pl.ds(s * WIDE, WIDE)
        high = pl.ds(s * WIDE + WIDE, WIDE)
        operand = jnp.concatenate(
            [
                jnp.concatenate([ref[low, :], ref[high, :]], axis=1).astype(jnp.bfloat16)
                for ref in (mid_real, mid_imag)
            ],
            axis=0,
        )
        value = jnp.dot(middle_ref[...], operand, preferred_element_type=jnp.float32)
        for i in range(2):
            real = value[0:WIDE, 128 * i : 128 * i + 128]
            imag = value[WIDE:, 128 * i : 128 * i + 128]
            freq = scalars_ref[0, pl.ds(s + i, 1), :]
            decays = freq - tables_ref[0]
            merges = freq + tables_ref[1]
            weight = (real * real + imag * imag) * (
                jnp.exp(-scaled * decays * decays) + jnp.exp(-scaled * merges * merges)
            )
            weight = weight * tables_ref[2] * scalars_ref[1, pl.ds(s + i, 1), :]
            at = pl.ds((s + i) * 8, 8)
            rate_acc[at, :] = jnp.sum(weight.reshape(WIDE // 8, 8, 128), axis=0)
            weight = weight * tables_ref[3]
            couple_acc[at, :] = jnp.sum(weight.reshape(WIDE // 8, 8, 128), axis=0)

    for i in range(24):
        two_modes(2 * i)

    sums = jnp.concatenate(
        [
            jnp.sum(rate_acc[...].reshape(PAD, 8, 128), axis=1),
            jnp.sum(couple_acc[...].reshape(PAD, 8, 128), axis=1),
        ],
        axis=0,
    )
    out_ref[:, 0:WIDE] = lax.dot_general(
        jnp.ones((8, 128), jnp.float32),
        sums,
        (((1,), (1,)), ((), ())),
        precision=lax.Precision.HIGHEST,
        preferred_element_type=jnp.float32,
    )[0:1]
    out_ref[:, WIDE:128] = jnp.zeros((1, 128 - WIDE), jnp.float32)


VMEM = pl.BlockSpec(memory_space=pltpu.VMEM)
SMEM = pl.BlockSpec(memory_space=pltpu.SMEM)
PARAMS = pltpu.CompilerParams(vmem_limit_bytes=56 << 20)


def grid_shift(step_y, step_z):
    return [
        (y * RING_Z + z, (y + step_y) % RING_Y * RING_Z + (z + step_z) % RING_Z)
        for y in range(RING_Y)
        for z in range(RING_Z)
    ]


def ring(count, step):
    return [(i, (i + step) % count) for i in range(count)]


def body(
    force_third,
    phase_angle,
    eigenvectors,
    frequencies,
    deviation,
    send_rows,
    trip_table,
    irreducible,
    multiplicity,
    drive_term,
    boundary,
):
    f32, b16 = jnp.float32, jnp.bfloat16
    clus = lax.axis_index("clus")
    mode = lax.axis_index("mode")
    color = (lax.axis_index("trip_y") + lax.axis_index("trip_z")) % 2
    trip = ("trip_y", "trip_z")
    group = ("clus", "mode")

    with jax.named_scope("records"):
        extra = jnp.concatenate([frequencies, deviation], axis=1)[:, None, :]
        record = jnp.concatenate(
            [eigenvectors, extra, jnp.zeros((extra.shape[0], 5, 180), b16)], axis=1
        )
        share = lax.dynamic_slice_in_dim(record, 12 * (2 * clus + mode), 12, 1)
        share = jnp.pad(share, ((0, 0), (0, 4), (0, 0)))
        chosen = pl.pallas_call(
            send_kernel,
            out_shape=jax.ShapeDtypeStruct((RING_Z, RING_Y) + share.shape[1:], b16),
            in_specs=[SMEM, VMEM],
            out_specs=VMEM,
            compiler_params=PARAMS,
        )(send_rows, share)
        halfway = lax.all_to_all(chosen, "trip_z", 0, 0, tiled=True)
        arrived = lax.all_to_all(halfway, "trip_y", 1, 1, tiled=True)
        angles = phase_angle.astype(f32)
        trig = jnp.stack([jnp.cos(angles), jnp.sin(angles)], axis=1).astype(b16)
        phases = jnp.pad(trig.reshape(4, 4).T[:, None, :], ((0, 0), (0, 15), (0, 176)))

    with jax.named_scope("force"):
        own = jnp.transpose(force_third, (1, 0, 2))
        half = lax.dynamic_slice_in_dim(own, SHARED * color, HALF, 0)
        low = lax.ppermute(half, "clus", ring(4, 1))
        high = lax.ppermute(half, "clus", ring(4, 3))

    with jax.named_scope("members"):
        picks = pl.pallas_call(
            pick_kernel,
            out_shape=jax.ShapeDtypeStruct((8, 4, 16, 180), b16),
            in_specs=[SMEM, VMEM, VMEM],
            out_specs=VMEM,
            compiler_params=PARAMS,
        )(trip_table, arrived, phases)
        members = lax.all_to_all(picks, group, 0, 0, tiled=True)

    with jax.named_scope("force_second"):
        low, high, low_top, high_rest, _ = lax.optimization_barrier(
            (low, high, low[:TOP], high[TOP:], members)
        )
        top = lax.ppermute(low_top, "clus", ring(4, 1))
        bottom = lax.ppermute(high_rest, "clus", ring(4, 3))
        low_other = lax.ppermute(low, trip, grid_shift(1, 0))
        high_other = lax.ppermute(high, trip, grid_shift(0, 1))
        top_other = lax.ppermute(top, trip, grid_shift(-1, 0))
        bottom_other = lax.ppermute(bottom, trip, grid_shift(0, -1))

    with jax.named_scope("operands"):
        mult = lax.dynamic_index_in_dim(multiplicity, clus, 0, keepdims=False)
        where = jnp.stack([clus, mode, mult, color]).astype(jnp.int32)
        early, late, mid, last_all, tables, scalars = pl.pallas_call(
            operand_kernel,
            out_shape=(
                jax.ShapeDtypeStruct((2 * WIDE, 3 * WIDE), b16),
                jax.ShapeDtypeStruct((WIDE, 8 * SLOT), b16),
                jax.ShapeDtypeStruct((2 * WIDE, 2 * WIDE), b16),
                jax.ShapeDtypeStruct((256, 256), b16),
                jax.ShapeDtypeStruct((4, WIDE, 128), f32),
                jax.ShapeDtypeStruct((2, PAD, 128), f32),
            ),
            in_specs=[SMEM, VMEM],
            out_specs=(VMEM,) * 6,
            compiler_params=PARAMS,
        )(where, members)

    with jax.named_scope("contract"):
        total = force_third.shape[2]
        swap = [(0, 1), (1, 0)]
        mine, *far = pl.pallas_call(
            early_kernel,
            out_shape=(jax.ShapeDtypeStruct((WIDE, total), b16),)
            + (jax.ShapeDtypeStruct((WIDE // 3, total), b16),) * 3,
            in_specs=[VMEM] * 6,
            out_specs=(VMEM,) * 4,
            compiler_params=PARAMS,
            cost_estimate=pl.CostEstimate(
                flops=2 * 192 * 288 * total, bytes_accessed=1200 * total, transcendentals=0
            ),
        )(early, own, low, low_other, high, high_other)
        other = [lax.ppermute(rows, "mode", swap) for rows in far]
        late_rows = [top, bottom, top_other, bottom_other]
        late_rows += [lax.ppermute(rows, "mode", swap) for rows in late_rows]

    with jax.named_scope("interaction"):
        inputs = (scalars, mid, last_all, tables, late, *late_rows, mine, *other)
        sums = pl.pallas_call(
            interaction_kernel,
            out_shape=jax.ShapeDtypeStruct((1, 128), f32),
            in_specs=[pl.BlockSpec(memory_space=pl.ANY)] * len(inputs),
            out_specs=VMEM,
            scratch_shapes=[pltpu.VMEM(x.shape, x.dtype) for x in inputs]
            + [
                pltpu.VMEM((WIDE, 8320), b16),
                pltpu.VMEM((90 * PAD, 256), b16),
                pltpu.VMEM((PAD * WIDE, 128), f32),
                pltpu.VMEM((PAD * WIDE, 128), f32),
                pltpu.VMEM((8 * PAD, 128), f32),
                pltpu.VMEM((8 * PAD, 128), f32),
                pltpu.SemaphoreType.DMA((len(inputs), 4)),
            ],
            compiler_params=PARAMS,
        )(*inputs)
    with jax.named_scope("collect"):
        own_row = sums
        rows = [own_row] + [lax.ppermute(own_row, "clus", ring(4, step)) for step in (1, 2, 3)]
        points = jnp.arange(32, dtype=jnp.int32)
        partial = jnp.zeros((32, 128), f32)
        for step in range(4):
            point = lax.dynamic_index_in_dim(irreducible, (clus - step) % 4, 0, keepdims=False)
            partial = partial + jnp.where((points == point)[:, None], rows[step], 0.0)
        received = lax.all_to_all(partial[:, None, :], trip, 0, 0, tiled=True)
        final = jnp.sum(received[:, 0, :], axis=0)[None, :]
        gamma_total = final[:, 0:45] + boundary
        return gamma_total, (drive_term + final[:, PAD : PAD + 45]) / gamma_total


def solution(mesh):
    devices = mesh.devices.reshape(4, RING_Y, RING_Z, 2)
    mesh = jax.sharding.Mesh(devices, ("clus", "trip_y", "trip_z", "mode"))
    trip = ("trip_y", "trip_z")
    return jax.shard_map(
        body,
        mesh=mesh,
        in_specs=(
            P("clus", "mode", None),
            P("clus", trip),
            P(trip, None, None),
            P(trip, None),
            P(trip, None),
            P(trip, None),
            P(trip, None),
            P(trip),
            P(trip),
            P(trip, "mode"),
            P(trip, "mode"),
        ),
        out_specs=(P(trip, "mode"), P(trip, "mode")),
        check_vma=False,
    )
```

```python
import jax
import jax.numpy as jnp
from jax import lax
from jax.experimental import pallas as pl
from jax.experimental.pallas import tpu as pltpu
from jax.sharding import PartitionSpec as P

smearing = 0.3
PAD = 48
WIDE = 96
CHUNK = 2048
TOP = 23


def send_kernel(rows_ref, share_ref, out_ref):
    for target in range(out_ref.shape[0]):
        out_ref[target] = share_ref[rows_ref[0, target]]


def pick_kernel(table_ref, arrived_ref, phase_ref, out_ref):
    for triplet in range(4):
        for member in range(3):
            block = arrived_ref[table_ref[triplet, member]]
            out_ref[2 * triplet, member, 0:12] = block
            out_ref[2 * triplet + 1, member, 0:12] = block
            fill = jnp.zeros((4, block.shape[1]), block.dtype)
            out_ref[2 * triplet, member, 12:16] = fill
            out_ref[2 * triplet + 1, member, 12:16] = fill
        out_ref[2 * triplet, 3] = phase_ref[triplet]
        out_ref[2 * triplet + 1, 3] = phase_ref[triplet]


def whole_record(members_ref, slot):
    parts = [members_ref[j, slot].astype(jnp.float32)[0:12] for j in range(8)]
    rows = jnp.concatenate(parts, axis=0)
    fill = jnp.zeros((WIDE, 38), jnp.float32)
    return jnp.concatenate([rows[:, 0:90], fill, rows[:, 90:180], fill], axis=1)


def operand_kernel(
    where_ref, members_ref, early_ref, late_ref, middle_ref, last_ref, tables_ref, scalars_ref
):
    rank, first, mult = where_ref[0], where_ref[1] == 0, where_ref[2]
    f32 = jnp.float32
    records = [whole_record(members_ref, member) for member in range(3)]
    lead_r, lead_i = records[0][:, 0:128].T, records[0][:, 128:256].T

    def halves(array):
        low, high = array[0:PAD], array[45 : 45 + PAD]
        return jnp.where(first, low, high), jnp.where(first, high, low)

    def sides(array):
        low, high = array[:, 0:PAD], array[:, 45 : 45 + PAD]
        return jnp.where(first, low, high), jnp.where(first, high, low)

    row = lax.broadcasted_iota(jnp.int32, (PAD, WIDE), 0)
    column = lax.broadcasted_iota(jnp.int32, (PAD, WIDE), 1)

    def spread(array, start, count):
        taken = (column // 2 + start == row) & (column < 2 * count)
        return jnp.dot(array, taken.astype(f32), preferred_element_type=f32)

    def turned(real, imag, offset):
        trig = members_ref[2 * ((rank + offset) & 3), 3].astype(f32)
        even = lax.broadcasted_iota(jnp.int32, (1, real.shape[1]), 1) % 2 == 0
        cosine = jnp.where(even, trig[0:1, 0:1], trig[0:1, 2:3])
        sine = jnp.where(even, trig[0:1, 1:2], trig[0:1, 3:4])
        return jnp.concatenate([cosine * real - sine * imag, cosine * imag + sine * real], axis=0)

    columns = []
    for array in (lead_r, lead_i):
        columns.append([halves(side) for side in sides(array)])
    whole = [[spread(columns[i][0][h], 0, 45) for i in range(2)] for h in range(2)]
    early_ref[...] = jnp.concatenate(
        [
            jnp.concatenate([turned(*whole[h], offset) for h in range(2)], axis=0)
            for offset in (0, 3, 1)
        ],
        axis=1,
    ).astype(early_ref.dtype)
    parts = []
    for side in range(2):
        for start, count in ((0, TOP), (TOP, 45 - TOP)):
            real, imag = (spread(columns[i][side][0], start, count)[:, 0:PAD] for i in range(2))
            parts.append(turned(real, imag, 2))
    late_ref[...] = jnp.concatenate(parts, axis=1).astype(late_ref.dtype)

    mid_r, mid_i = records[1][:, 0:128].T, records[1][:, 128:256].T
    within = lax.broadcasted_iota(jnp.int32, (WIDE, WIDE), 1) < 90
    real = jnp.where(within, mid_r[0:WIDE], 0.0)
    imag = jnp.where(within, mid_i[0:WIDE], 0.0)
    middle_ref[...] = jnp.concatenate(
        [jnp.concatenate([real, -imag], axis=1), jnp.concatenate([imag, real], axis=1)], axis=0
    ).astype(middle_ref.dtype)

    last_r, last_i = records[2][:, 0:128], records[2][:, 128:256]
    within = lax.broadcasted_iota(jnp.int32, (WIDE, 128), 0) < 90
    real = jnp.where(within, last_r, 0.0)
    imag = jnp.where(within, last_i, 0.0)
    zeros = jnp.zeros((32, 256), f32)
    last_ref[...] = jnp.concatenate(
        [
            jnp.concatenate([real, imag], axis=1),
            zeros,
            jnp.concatenate([-imag, real], axis=1),
            zeros,
        ],
        axis=0,
    ).astype(last_ref.dtype)

    row = lax.broadcasted_iota(jnp.int32, (WIDE, 128), 0)
    column = lax.broadcasted_iota(jnp.int32, (WIDE, 128), 1)
    one = jnp.where(row < 90, jnp.broadcast_to(mid_r[0:WIDE, 90:91], (WIDE, 128)), 1.0)
    two = jnp.where(column < 90, jnp.broadcast_to(last_r[90:91, :], (WIDE, 128)), 1.0)
    tables_ref[0] = one + two
    tables_ref[1] = one - two
    tables_ref[2] = 1.0 / (one * two)
    tables_ref[3] = jnp.broadcast_to(mid_i[0:WIDE, 90:91], (WIDE, 128)) + jnp.broadcast_to(
        last_i[90:91, :], (WIDE, 128)
    )
    zero = halves(lead_r[:, 90:91])[0]
    zero = jnp.where(lax.broadcasted_iota(jnp.int32, (PAD, 1), 0) < 45, zero, 1.0)
    scalars_ref[0] = jnp.broadcast_to(zero, (PAD, 128))
    scalars_ref[1] = jnp.broadcast_to(mult.astype(f32) / zero, (PAD, 128))


def rows_of(ref, cols, count):
    values = ref[:, :, cols]
    rows = values.shape[0] * values.shape[1]
    return jnp.pad(values.reshape(rows, values.shape[2]), ((0, count - rows), (0, 0)))


def early_kernel(lead_ref, own_ref, low_ref, high_ref, mine_ref, *far_refs):
    total = own_ref.shape[2]
    for start in range(0, total, CHUNK):
        cols = slice(start, min(start + CHUNK, total))
        product = jnp.dot(
            lead_ref[...],
            jnp.concatenate([rows_of(ref, cols, WIDE) for ref in (own_ref, low_ref, high_ref)], axis=0),
            preferred_element_type=jnp.float32,
        )
        mine_ref[:, cols] = product[0:WIDE].astype(mine_ref.dtype)
        for i, far_ref in enumerate(far_refs):
            rows = product[WIDE + 48 * i : WIDE + 48 * i + 48]
            far_ref[:, cols] = rows.astype(far_ref.dtype)


def interaction_kernel(*refs):
    count = 12
    operands, out_ref, buffers = refs[:count], refs[count], refs[count + 1 : 2 * count + 1]
    flat, windows, mid_real, mid_imag, rate_acc, couple_acc, done = refs[2 * count + 1 :]
    scalars_ref, middle_ref, last_ref, tables_ref, late_ref = buffers[:5]
    top_ref, bottom_ref, far_top_ref, far_bottom_ref, mine_ref = buffers[5:10]
    late, others = buffers[5:9], buffers[10:]
    total = mine_ref.shape[1]
    pieces = [slice(at, min(at + CHUNK, total)) for at in range(0, total, CHUNK)]
    whole = {}
    for i in range(5):
        whole[i] = pltpu.make_async_copy(operands[i], buffers[i], done.at[i, 0])
    parts = {}
    for k, cols in enumerate(pieces):
        for i in range(5, count):
            where = (slice(None),) * (len(operands[i].shape) - 1) + (cols,)
            parts[i, k] = pltpu.make_async_copy(
                operands[i].at[where], buffers[i].at[where], done.at[i, k]
            )
    whole[4].start()
    for i in range(5, count):
        parts[i, 0].start()
    whole[2].start()
    for k in range(1, len(pieces)):
        for i in range(5, count):
            parts[i, k].start()
    for i in (0, 1, 3):
        whole[i].start()

    flat[:, 8064:8320] = jnp.zeros((WIDE, 256), flat.dtype)
    zeros = jnp.zeros((PAD, 128), jnp.float32)
    for b in range(90, WIDE):
        mid_real[pl.ds(b, PAD, stride=WIDE), :] = zeros
        mid_imag[pl.ds(b, PAD, stride=WIDE), :] = zeros

    def window_of(b):
        tile, shift = divmod(90 * b, 128)
        pair = flat[:, tile * 128 : tile * 128 + 256]
        window = pair[:, shift : shift + 128]
        windows[b * PAD : (b + 1) * PAD, 0:128] = window[0:PAD]
        windows[b * PAD : (b + 1) * PAD, 128:256] = window[PAD:]

    def product_of(group):
        product = jnp.dot(
            windows[group * 480 : (group + 1) * 480, :],
            last_ref[...],
            preferred_element_type=jnp.float32,
        )
        for i in range(10):
            rows = pl.ds(group * 10 + i, PAD, stride=WIDE)
            mid_real[rows, :] = product[i * PAD : (i + 1) * PAD, 0:128]
            mid_imag[rows, :] = product[i * PAD : (i + 1) * PAD, 128:256]

    whole[4].wait()
    b = 0
    for k, cols in enumerate(pieces):
        for i in range(5, count):
            parts[i, k].wait()
        if k == 0:
            whole[2].wait()
        other = jnp.concatenate([ref[:, cols].astype(jnp.float32) for ref in others], axis=0)
        both = mine_ref[:, cols].astype(jnp.float32) + other
        both = both + jnp.dot(
            late_ref[...],
            jnp.concatenate([rows_of(ref, cols, PAD) for ref in late], axis=0),
            preferred_element_type=jnp.float32,
        )
        flat[:, cols] = both.astype(flat.dtype)
        ready = 8320 if cols.stop == total else cols.stop
        while b < 90 and 90 * b // 128 * 128 + 256 <= ready:
            window_of(b)
            b += 1
            if b % 10 == 0:
                product_of(b // 10 - 1)
    for i in (0, 1, 3):
        whole[i].wait()

    scaled = 0.5 / (smearing * smearing)
    def two_modes(s):
        low = pl.ds(s * WIDE, WIDE)
        high = pl.ds(s * WIDE + WIDE, WIDE)
        operand = jnp.concatenate(
            [
                jnp.concatenate([ref[low, :], ref[high, :]], axis=1).astype(jnp.bfloat16)
                for ref in (mid_real, mid_imag)
            ],
            axis=0,
        )
        value = jnp.dot(middle_ref[...], operand, preferred_element_type=jnp.float32)
        for i in range(2):
            real = value[0:WIDE, 128 * i : 128 * i + 128]
            imag = value[WIDE:, 128 * i : 128 * i + 128]
            freq = scalars_ref[0, pl.ds(s + i, 1), :]
            decays = freq - tables_ref[0]
            merges = freq + tables_ref[1]
            weight = (real * real + imag * imag) * (
                jnp.exp(-scaled * decays * decays) + jnp.exp(-scaled * merges * merges)
            )
            weight = weight * tables_ref[2] * scalars_ref[1, pl.ds(s + i, 1), :]
            at = pl.ds((s + i) * 8, 8)
            rate_acc[at, :] = jnp.sum(weight.reshape(WIDE // 8, 8, 128), axis=0)
            weight = weight * tables_ref[3]
            couple_acc[at, :] = jnp.sum(weight.reshape(WIDE // 8, 8, 128), axis=0)

    for i in range(24):
        two_modes(2 * i)

    sums = jnp.concatenate(
        [
            jnp.sum(rate_acc[...].reshape(PAD, 8, 128), axis=1),
            jnp.sum(couple_acc[...].reshape(PAD, 8, 128), axis=1),
        ],
        axis=0,
    )
    out_ref[:, 0:WIDE] = lax.dot_general(
        jnp.ones((8, 128), jnp.float32),
        sums,
        (((1,), (1,)), ((), ())),
        precision=lax.Precision.HIGHEST,
        preferred_element_type=jnp.float32,
    )[0:1]
    out_ref[:, WIDE:128] = jnp.zeros((1, 128 - WIDE), jnp.float32)


VMEM = pl.BlockSpec(memory_space=pltpu.VMEM)
SMEM = pl.BlockSpec(memory_space=pltpu.SMEM)
PARAMS = pltpu.CompilerParams(vmem_limit_bytes=56 << 20)


def ring(count, step):
    return [(i, (i + step) % count) for i in range(count)]


def body(
    force_third,
    phase_angle,
    eigenvectors,
    frequencies,
    deviation,
    send_rows,
    trip_table,
    irreducible,
    multiplicity,
    drive_term,
    boundary,
):
    f32, b16 = jnp.float32, jnp.bfloat16
    clus = lax.axis_index("clus")
    mode = lax.axis_index("mode")
    group = ("clus", "mode")

    with jax.named_scope("records"):
        extra = jnp.concatenate([frequencies, deviation], axis=1)[:, None, :]
        record = jnp.concatenate(
            [eigenvectors, extra, jnp.zeros((extra.shape[0], 5, 180), b16)], axis=1
        )
        share = lax.dynamic_slice_in_dim(record, 12 * (2 * clus + mode), 12, 1)
        chosen = pl.pallas_call(
            send_kernel,
            out_shape=jax.ShapeDtypeStruct((send_rows.shape[1],) + share.shape[1:], b16),
            in_specs=[SMEM, VMEM],
            out_specs=VMEM,
            compiler_params=PARAMS,
        )(send_rows, share)
        arrived = lax.all_to_all(chosen, "trip", 0, 0, tiled=True)
        angles = phase_angle.astype(f32)
        trig = jnp.stack([jnp.cos(angles), jnp.sin(angles)], axis=1).astype(b16)
        phases = jnp.pad(trig.reshape(4, 4).T[:, None, :], ((0, 0), (0, 15), (0, 176)))

    with jax.named_scope("force"):
        own = jnp.transpose(force_third, (1, 0, 2))
        low = lax.ppermute(own, "clus", ring(4, 1))
        high = lax.ppermute(own, "clus", ring(4, 3))

    with jax.named_scope("members"):
        picks = pl.pallas_call(
            pick_kernel,
            out_shape=jax.ShapeDtypeStruct((8, 4, 16, 180), b16),
            in_specs=[SMEM, VMEM, VMEM],
            out_specs=VMEM,
            compiler_params=PARAMS,
        )(trip_table, arrived, phases)
        members = lax.all_to_all(picks, group, 0, 0, tiled=True)

    with jax.named_scope("force_second"):
        low_top, high_bottom, _ = lax.optimization_barrier((low[:TOP], high[TOP:], members))
        top = lax.ppermute(low_top, "clus", ring(4, 1))
        bottom = lax.ppermute(high_bottom, "clus", ring(4, 3))

    with jax.named_scope("operands"):
        mult = lax.dynamic_index_in_dim(multiplicity, clus, 0, keepdims=False)
        where = jnp.stack([clus, mode, mult]).astype(jnp.int32)
        early, late, mid, last_all, tables, scalars = pl.pallas_call(
            operand_kernel,
            out_shape=(
                jax.ShapeDtypeStruct((2 * WIDE, 3 * WIDE), b16),
                jax.ShapeDtypeStruct((WIDE, 4 * PAD), b16),
                jax.ShapeDtypeStruct((2 * WIDE, 2 * WIDE), b16),
                jax.ShapeDtypeStruct((256, 256), b16),
                jax.ShapeDtypeStruct((4, WIDE, 128), f32),
                jax.ShapeDtypeStruct((2, PAD, 128), f32),
            ),
            in_specs=[SMEM, VMEM],
            out_specs=(VMEM,) * 6,
            compiler_params=PARAMS,
        )(where, members)

    with jax.named_scope("contract"):
        total = force_third.shape[2]
        swap = [(0, 1), (1, 0)]
        mine, *far = pl.pallas_call(
            early_kernel,
            out_shape=(jax.ShapeDtypeStruct((WIDE, total), b16),)
            + (jax.ShapeDtypeStruct((WIDE // 2, total), b16),) * 2,
            in_specs=[VMEM] * 4,
            out_specs=(VMEM,) * 3,
            compiler_params=PARAMS,
            cost_estimate=pl.CostEstimate(
                flops=2 * 192 * 288 * total, bytes_accessed=1200 * total, transcendentals=0
            ),
        )(early, own, low, high)
        other = [lax.ppermute(rows, "mode", swap) for rows in far]
        far_top = lax.ppermute(top, "mode", swap)
        far_bottom = lax.ppermute(bottom, "mode", swap)

    with jax.named_scope("interaction"):
        inputs = (scalars, mid, last_all, tables, late, top, bottom, far_top, far_bottom, mine, *other)
        sums = pl.pallas_call(
            interaction_kernel,
            out_shape=jax.ShapeDtypeStruct((1, 128), f32),
            in_specs=[pl.BlockSpec(memory_space=pl.ANY)] * len(inputs),
            out_specs=VMEM,
            scratch_shapes=[pltpu.VMEM(x.shape, x.dtype) for x in inputs]
            + [
                pltpu.VMEM((WIDE, 8320), b16),
                pltpu.VMEM((90 * PAD, 256), b16),
                pltpu.VMEM((PAD * WIDE, 128), f32),
                pltpu.VMEM((PAD * WIDE, 128), f32),
                pltpu.VMEM((8 * PAD, 128), f32),
                pltpu.VMEM((8 * PAD, 128), f32),
                pltpu.SemaphoreType.DMA((len(inputs), 4)),
            ],
            compiler_params=PARAMS,
        )(*inputs)
    with jax.named_scope("collect"):
        own_row = sums
        rows = [own_row] + [lax.ppermute(own_row, "clus", ring(4, step)) for step in (1, 2, 3)]
        points = jnp.arange(32, dtype=jnp.int32)
        partial = jnp.zeros((32, 128), f32)
        for step in range(4):
            point = lax.dynamic_index_in_dim(irreducible, (clus - step) % 4, 0, keepdims=False)
            partial = partial + jnp.where((points == point)[:, None], rows[step], 0.0)
        received = lax.all_to_all(partial[:, None, :], "trip", 0, 0, tiled=True)
        final = jnp.sum(received[:, 0, :], axis=0)[None, :]
        gamma_total = final[:, 0:45] + boundary
        return gamma_total, (drive_term + final[:, PAD : PAD + 45]) / gamma_total


def solution(mesh):
    return jax.shard_map(
        body,
        mesh=mesh,
        in_specs=(
            P("clus", "mode", None),
            P("clus", "trip"),
            P("trip", None, None),
            P("trip", None),
            P("trip", None),
            P("trip", None),
            P("trip", None),
            P("trip"),
            P("trip"),
            P("trip", "mode"),
            P("trip", "mode"),
        ),
        out_specs=(P("trip", "mode"), P("trip", "mode")),
        check_vma=False,
    )
```

```python
import jax
import jax.numpy as jnp
from jax import lax
from jax.experimental import pallas as pl
from jax.experimental.pallas import tpu as pltpu
from jax.sharding import PartitionSpec as P

smearing = 0.3
PAD = 48
WIDE = 96
CHUNK = 2048
TOP = 23


def send_kernel(rows_ref, share_ref, out_ref):
    for target in range(out_ref.shape[0]):
        out_ref[target] = share_ref[rows_ref[0, target]]


def pick_kernel(table_ref, arrived_ref, phase_ref, out_ref):
    for triplet in range(4):
        for member in range(3):
            block = arrived_ref[table_ref[triplet, member]]
            out_ref[2 * triplet, member, 0:12] = block
            out_ref[2 * triplet + 1, member, 0:12] = block
            fill = jnp.zeros((4, block.shape[1]), block.dtype)
            out_ref[2 * triplet, member, 12:16] = fill
            out_ref[2 * triplet + 1, member, 12:16] = fill
        out_ref[2 * triplet, 3] = phase_ref[triplet]
        out_ref[2 * triplet + 1, 3] = phase_ref[triplet]


def whole_record(members_ref, slot):
    parts = [members_ref[j, slot].astype(jnp.float32)[0:12] for j in range(8)]
    rows = jnp.concatenate(parts, axis=0)
    fill = jnp.zeros((WIDE, 38), jnp.float32)
    return jnp.concatenate([rows[:, 0:90], fill, rows[:, 90:180], fill], axis=1)


def operand_kernel(
    where_ref, members_ref, early_ref, late_ref, middle_ref, last_ref, tables_ref, scalars_ref
):
    rank, first, mult = where_ref[0], where_ref[1] == 0, where_ref[2]
    f32 = jnp.float32
    records = [whole_record(members_ref, member) for member in range(3)]
    lead_r, lead_i = records[0][:, 0:128].T, records[0][:, 128:256].T

    def halves(array):
        low, high = array[0:PAD], array[45 : 45 + PAD]
        return jnp.where(first, low, high), jnp.where(first, high, low)

    def sides(array):
        low, high = array[:, 0:PAD], array[:, 45 : 45 + PAD]
        return jnp.where(first, low, high), jnp.where(first, high, low)

    row = lax.broadcasted_iota(jnp.int32, (PAD, WIDE), 0)
    column = lax.broadcasted_iota(jnp.int32, (PAD, WIDE), 1)

    def spread(array, start, count):
        taken = (column // 2 + start == row) & (column < 2 * count)
        return jnp.dot(array, taken.astype(f32), preferred_element_type=f32)

    def turned(real, imag, offset):
        trig = members_ref[2 * ((rank + offset) & 3), 3].astype(f32)
        even = lax.broadcasted_iota(jnp.int32, (1, real.shape[1]), 1) % 2 == 0
        cosine = jnp.where(even, trig[0:1, 0:1], trig[0:1, 2:3])
        sine = jnp.where(even, trig[0:1, 1:2], trig[0:1, 3:4])
        return jnp.concatenate([cosine * real - sine * imag, cosine * imag + sine * real], axis=0)

    columns = []
    for array in (lead_r, lead_i):
        columns.append([halves(side) for side in sides(array)])
    whole = [[spread(columns[i][0][h], 0, 45) for i in range(2)] for h in range(2)]
    early_ref[...] = jnp.concatenate(
        [
            jnp.concatenate([turned(*whole[h], offset) for h in range(2)], axis=0)
            for offset in (0, 3, 1)
        ],
        axis=1,
    ).astype(early_ref.dtype)
    parts = []
    for side in range(2):
        for start, count in ((0, TOP), (TOP, 45 - TOP)):
            real, imag = (spread(columns[i][side][0], start, count)[:, 0:PAD] for i in range(2))
            parts.append(turned(real, imag, 2))
    late_ref[...] = jnp.concatenate(parts, axis=1).astype(late_ref.dtype)

    mid_r, mid_i = records[1][:, 0:128].T, records[1][:, 128:256].T
    within = lax.broadcasted_iota(jnp.int32, (WIDE, WIDE), 1) < 90
    real = jnp.where(within, mid_r[0:WIDE], 0.0)
    imag = jnp.where(within, mid_i[0:WIDE], 0.0)
    middle_ref[...] = jnp.concatenate(
        [jnp.concatenate([real, -imag], axis=1), jnp.concatenate([imag, real], axis=1)], axis=0
    ).astype(middle_ref.dtype)

    last_r, last_i = records[2][:, 0:128], records[2][:, 128:256]
    within = lax.broadcasted_iota(jnp.int32, (WIDE, 128), 0) < 90
    real = jnp.where(within, last_r, 0.0)
    imag = jnp.where(within, last_i, 0.0)
    zeros = jnp.zeros((32, 256), f32)
    last_ref[...] = jnp.concatenate(
        [
            jnp.concatenate([real, imag], axis=1),
            zeros,
            jnp.concatenate([-imag, real], axis=1),
            zeros,
        ],
        axis=0,
    ).astype(last_ref.dtype)

    row = lax.broadcasted_iota(jnp.int32, (WIDE, 128), 0)
    column = lax.broadcasted_iota(jnp.int32, (WIDE, 128), 1)
    one = jnp.where(row < 90, jnp.broadcast_to(mid_r[0:WIDE, 90:91], (WIDE, 128)), 1.0)
    two = jnp.where(column < 90, jnp.broadcast_to(last_r[90:91, :], (WIDE, 128)), 1.0)
    tables_ref[0] = one + two
    tables_ref[1] = one - two
    tables_ref[2] = 1.0 / (one * two)
    tables_ref[3] = jnp.broadcast_to(mid_i[0:WIDE, 90:91], (WIDE, 128)) + jnp.broadcast_to(
        last_i[90:91, :], (WIDE, 128)
    )
    zero = halves(lead_r[:, 90:91])[0]
    zero = jnp.where(lax.broadcasted_iota(jnp.int32, (PAD, 1), 0) < 45, zero, 1.0)
    scalars_ref[0] = jnp.broadcast_to(zero, (PAD, 128))
    scalars_ref[1] = jnp.broadcast_to(mult.astype(f32) / zero, (PAD, 128))


def rows_of(ref, cols, count):
    values = ref[:, :, cols]
    rows = values.shape[0] * values.shape[1]
    return jnp.pad(values.reshape(rows, values.shape[2]), ((0, count - rows), (0, 0)))


def halves_kernel(low_ref, high_ref, top_ref, bottom_ref, done):
    top = pltpu.make_async_copy(low_ref.at[0:TOP], top_ref, done.at[0])
    bottom = pltpu.make_async_copy(high_ref.at[TOP:45], bottom_ref, done.at[1])
    top.start()
    bottom.start()
    top.wait()
    bottom.wait()


def early_kernel(lead_ref, own_ref, low_ref, high_ref, mine_ref, *far_refs):
    total = own_ref.shape[2]
    for start in range(0, total, CHUNK):
        cols = slice(start, min(start + CHUNK, total))
        product = jnp.dot(
            lead_ref[...],
            jnp.concatenate([rows_of(ref, cols, WIDE) for ref in (own_ref, low_ref, high_ref)], axis=0),
            preferred_element_type=jnp.float32,
        )
        mine_ref[:, cols] = product[0:WIDE].astype(mine_ref.dtype)
        for i, far_ref in enumerate(far_refs):
            rows = product[WIDE + 48 * i : WIDE + 48 * i + 48]
            far_ref[:, cols] = rows.astype(far_ref.dtype)


def interaction_kernel(*refs):
    count = 12
    operands, out_ref, buffers = refs[:count], refs[count], refs[count + 1 : 2 * count + 1]
    flat, windows, mid_real, mid_imag, rate_acc, couple_acc, done = refs[2 * count + 1 :]
    scalars_ref, middle_ref, last_ref, tables_ref, late_ref = buffers[:5]
    top_ref, bottom_ref, far_top_ref, far_bottom_ref, mine_ref = buffers[5:10]
    late, others = buffers[5:9], buffers[10:]
    total = mine_ref.shape[1]
    pieces = [slice(at, min(at + CHUNK, total)) for at in range(0, total, CHUNK)]
    whole = {}
    for i in range(5):
        whole[i] = pltpu.make_async_copy(operands[i], buffers[i], done.at[i, 0])
    parts = {}
    for k, cols in enumerate(pieces):
        for i in range(5, count):
            where = (slice(None),) * (len(operands[i].shape) - 1) + (cols,)
            parts[i, k] = pltpu.make_async_copy(
                operands[i].at[where], buffers[i].at[where], done.at[i, k]
            )
    whole[4].start()
    for i in range(5, count):
        parts[i, 0].start()
    whole[2].start()
    for k in range(1, len(pieces)):
        for i in range(5, count):
            parts[i, k].start()
    for i in (0, 1, 3):
        whole[i].start()

    flat[:, 8064:8320] = jnp.zeros((WIDE, 256), flat.dtype)
    zeros = jnp.zeros((PAD, 128), jnp.float32)
    for b in range(90, WIDE):
        mid_real[pl.ds(b, PAD, stride=WIDE), :] = zeros
        mid_imag[pl.ds(b, PAD, stride=WIDE), :] = zeros

    def window_of(b):
        tile, shift = divmod(90 * b, 128)
        pair = flat[:, tile * 128 : tile * 128 + 256]
        window = pair[:, shift : shift + 128]
        windows[b * PAD : (b + 1) * PAD, 0:128] = window[0:PAD]
        windows[b * PAD : (b + 1) * PAD, 128:256] = window[PAD:]

    def product_of(group):
        product = jnp.dot(
            windows[group * 480 : (group + 1) * 480, :],
            last_ref[...],
            preferred_element_type=jnp.float32,
        )
        for i in range(10):
            rows = pl.ds(group * 10 + i, PAD, stride=WIDE)
            mid_real[rows, :] = product[i * PAD : (i + 1) * PAD, 0:128]
            mid_imag[rows, :] = product[i * PAD : (i + 1) * PAD, 128:256]

    whole[4].wait()
    b = 0
    for k, cols in enumerate(pieces):
        for i in range(5, count):
            parts[i, k].wait()
        if k == 0:
            whole[2].wait()
        other = jnp.concatenate([ref[:, cols].astype(jnp.float32) for ref in others], axis=0)
        both = mine_ref[:, cols].astype(jnp.float32) + other
        both = both + jnp.dot(
            late_ref[...],
            jnp.concatenate([rows_of(ref, cols, PAD) for ref in late], axis=0),
            preferred_element_type=jnp.float32,
        )
        flat[:, cols] = both.astype(flat.dtype)
        ready = 8320 if cols.stop == total else cols.stop
        while b < 90 and 90 * b // 128 * 128 + 256 <= ready:
            window_of(b)
            b += 1
            if b % 10 == 0:
                product_of(b // 10 - 1)
    for i in (0, 1, 3):
        whole[i].wait()

    scaled = 0.5 / (smearing * smearing)
    def two_modes(s):
        low = pl.ds(s * WIDE, WIDE)
        high = pl.ds(s * WIDE + WIDE, WIDE)
        operand = jnp.concatenate(
            [
                jnp.concatenate([ref[low, :], ref[high, :]], axis=1).astype(jnp.bfloat16)
                for ref in (mid_real, mid_imag)
            ],
            axis=0,
        )
        value = jnp.dot(middle_ref[...], operand, preferred_element_type=jnp.float32)
        for i in range(2):
            real = value[0:WIDE, 128 * i : 128 * i + 128]
            imag = value[WIDE:, 128 * i : 128 * i + 128]
            freq = scalars_ref[0, pl.ds(s + i, 1), :]
            decays = freq - tables_ref[0]
            merges = freq + tables_ref[1]
            weight = (real * real + imag * imag) * (
                jnp.exp(-scaled * decays * decays) + jnp.exp(-scaled * merges * merges)
            )
            weight = weight * tables_ref[2] * scalars_ref[1, pl.ds(s + i, 1), :]
            at = pl.ds((s + i) * 8, 8)
            rate_acc[at, :] = jnp.sum(weight.reshape(WIDE // 8, 8, 128), axis=0)
            weight = weight * tables_ref[3]
            couple_acc[at, :] = jnp.sum(weight.reshape(WIDE // 8, 8, 128), axis=0)

    for i in range(24):
        two_modes(2 * i)

    sums = jnp.concatenate(
        [
            jnp.sum(rate_acc[...].reshape(PAD, 8, 128), axis=1),
            jnp.sum(couple_acc[...].reshape(PAD, 8, 128), axis=1),
        ],
        axis=0,
    )
    out_ref[:, 0:WIDE] = lax.dot_general(
        jnp.ones((8, 128), jnp.float32),
        sums,
        (((1,), (1,)), ((), ())),
        precision=lax.Precision.HIGHEST,
        preferred_element_type=jnp.float32,
    )[0:1]
    out_ref[:, WIDE:128] = jnp.zeros((1, 128 - WIDE), jnp.float32)


VMEM = pl.BlockSpec(memory_space=pltpu.VMEM)
SMEM = pl.BlockSpec(memory_space=pltpu.SMEM)
PARAMS = pltpu.CompilerParams(vmem_limit_bytes=56 << 20)


def ring(count, step):
    return [(i, (i + step) % count) for i in range(count)]


def body(
    force_third,
    phase_angle,
    eigenvectors,
    frequencies,
    deviation,
    send_rows,
    trip_table,
    irreducible,
    multiplicity,
    drive_term,
    boundary,
):
    f32, b16 = jnp.float32, jnp.bfloat16
    clus = lax.axis_index("clus")
    mode = lax.axis_index("mode")
    group = ("clus", "mode")

    with jax.named_scope("records"):
        extra = jnp.concatenate([frequencies, deviation], axis=1)[:, None, :]
        record = jnp.concatenate(
            [eigenvectors, extra, jnp.zeros((extra.shape[0], 5, 180), b16)], axis=1
        )
        share = lax.dynamic_slice_in_dim(record, 12 * (2 * clus + mode), 12, 1)
        chosen = pl.pallas_call(
            send_kernel,
            out_shape=jax.ShapeDtypeStruct((send_rows.shape[1],) + share.shape[1:], b16),
            in_specs=[SMEM, VMEM],
            out_specs=VMEM,
            compiler_params=PARAMS,
        )(send_rows, share)
        arrived = lax.all_to_all(chosen, "trip", 0, 0, tiled=True)
        angles = phase_angle.astype(f32)
        trig = jnp.stack([jnp.cos(angles), jnp.sin(angles)], axis=1).astype(b16)
        phases = jnp.pad(trig.reshape(4, 4).T[:, None, :], ((0, 0), (0, 15), (0, 176)))

    with jax.named_scope("force"):
        own = jnp.transpose(force_third, (1, 0, 2))
        low = lax.ppermute(own, "clus", ring(4, 1))
        high = lax.ppermute(own, "clus", ring(4, 3))

    with jax.named_scope("members"):
        picks = pl.pallas_call(
            pick_kernel,
            out_shape=jax.ShapeDtypeStruct((8, 4, 16, 180), b16),
            in_specs=[SMEM, VMEM, VMEM],
            out_specs=VMEM,
            compiler_params=PARAMS,
        )(trip_table, arrived, phases)
        members = lax.all_to_all(picks, group, 0, 0, tiled=True)

    with jax.named_scope("force_second"):
        any_space = pl.BlockSpec(memory_space=pl.ANY)
        low_top, high_bottom = pl.pallas_call(
            halves_kernel,
            out_shape=(
                jax.ShapeDtypeStruct((TOP,) + low.shape[1:], b16),
                jax.ShapeDtypeStruct((45 - TOP,) + high.shape[1:], b16),
            ),
            in_specs=[any_space] * 2,
            out_specs=(any_space,) * 2,
            scratch_shapes=[pltpu.SemaphoreType.DMA((2,))],
            compiler_params=pltpu.CompilerParams(vmem_limit_bytes=4 << 20),
        )(low, high)
        low_top, high_bottom, _ = lax.optimization_barrier((low_top, high_bottom, members))
        top = lax.ppermute(low_top, "clus", ring(4, 1))
        bottom = lax.ppermute(high_bottom, "clus", ring(4, 3))

    with jax.named_scope("operands"):
        mult = lax.dynamic_index_in_dim(multiplicity, clus, 0, keepdims=False)
        where = jnp.stack([clus, mode, mult]).astype(jnp.int32)
        early, late, mid, last_all, tables, scalars = pl.pallas_call(
            operand_kernel,
            out_shape=(
                jax.ShapeDtypeStruct((2 * WIDE, 3 * WIDE), b16),
                jax.ShapeDtypeStruct((WIDE, 4 * PAD), b16),
                jax.ShapeDtypeStruct((2 * WIDE, 2 * WIDE), b16),
                jax.ShapeDtypeStruct((256, 256), b16),
                jax.ShapeDtypeStruct((4, WIDE, 128), f32),
                jax.ShapeDtypeStruct((2, PAD, 128), f32),
            ),
            in_specs=[SMEM, VMEM],
            out_specs=(VMEM,) * 6,
            compiler_params=PARAMS,
        )(where, members)

    with jax.named_scope("contract"):
        total = force_third.shape[2]
        swap = [(0, 1), (1, 0)]
        mine, *far = pl.pallas_call(
            early_kernel,
            out_shape=(jax.ShapeDtypeStruct((WIDE, total), b16),)
            + (jax.ShapeDtypeStruct((WIDE // 2, total), b16),) * 2,
            in_specs=[VMEM] * 4,
            out_specs=(VMEM,) * 3,
            compiler_params=PARAMS,
            cost_estimate=pl.CostEstimate(
                flops=2 * 192 * 288 * total, bytes_accessed=1200 * total, transcendentals=0
            ),
        )(early, own, low, high)
        other = [lax.ppermute(rows, "mode", swap) for rows in far]
        far_top = lax.ppermute(top, "mode", swap)
        far_bottom = lax.ppermute(bottom, "mode", swap)

    with jax.named_scope("masks"):
        points = jnp.arange(32, dtype=jnp.int32)
        masks = [
            points == lax.dynamic_index_in_dim(irreducible, (clus - step) % 4, 0, keepdims=False)
            for step in range(4)
        ]
        mine, *masks = lax.optimization_barrier((mine, *masks))

    with jax.named_scope("interaction"):
        inputs = (scalars, mid, last_all, tables, late, top, bottom, far_top, far_bottom, mine, *other)
        sums = pl.pallas_call(
            interaction_kernel,
            out_shape=jax.ShapeDtypeStruct((1, 128), f32),
            in_specs=[pl.BlockSpec(memory_space=pl.ANY)] * len(inputs),
            out_specs=VMEM,
            scratch_shapes=[pltpu.VMEM(x.shape, x.dtype) for x in inputs]
            + [
                pltpu.VMEM((WIDE, 8320), b16),
                pltpu.VMEM((90 * PAD, 256), b16),
                pltpu.VMEM((PAD * WIDE, 128), f32),
                pltpu.VMEM((PAD * WIDE, 128), f32),
                pltpu.VMEM((8 * PAD, 128), f32),
                pltpu.VMEM((8 * PAD, 128), f32),
                pltpu.SemaphoreType.DMA((len(inputs), 4)),
            ],
            compiler_params=PARAMS,
        )(*inputs)
    with jax.named_scope("collect"):
        own_row = sums
        rows = [own_row] + [lax.ppermute(own_row, "clus", ring(4, step)) for step in (1, 2, 3)]
        partial = jnp.zeros((32, 128), f32)
        for mask, row in zip(masks, rows):
            partial = partial + jnp.where(mask[:, None], row, 0.0)
        received = lax.all_to_all(partial[:, None, :], "trip", 0, 0, tiled=True)
        final = jnp.sum(received[:, 0, :], axis=0)[None, :]
        gamma_total = final[:, 0:45] + boundary
        return gamma_total, (drive_term + final[:, PAD : PAD + 45]) / gamma_total


def solution(mesh):
    return jax.shard_map(
        body,
        mesh=mesh,
        in_specs=(
            P("clus", "mode", None),
            P("clus", "trip"),
            P("trip", None, None),
            P("trip", None),
            P("trip", None),
            P("trip", None),
            P("trip", None),
            P("trip"),
            P("trip"),
            P("trip", "mode"),
            P("trip", "mode"),
        ),
        out_specs=(P("trip", "mode"), P("trip", "mode")),
        check_vma=False,
    )
```

```python
import jax
import jax.numpy as jnp
from jax import lax
from jax.experimental import pallas as pl
from jax.experimental.pallas import tpu as pltpu
from jax.sharding import PartitionSpec as P

smearing = 0.3
PAD = 48
WIDE = 96
CHUNK = 2048
TOP = 23


def send_kernel(rows_ref, share_ref, out_ref):
    for target in range(out_ref.shape[0]):
        out_ref[target] = share_ref[rows_ref[0, target]]


def pick_kernel(table_ref, arrived_ref, phase_ref, out_ref):
    for triplet in range(4):
        for member in range(3):
            block = arrived_ref[table_ref[triplet, member]]
            out_ref[2 * triplet, member, 0:12] = block
            out_ref[2 * triplet + 1, member, 0:12] = block
            fill = jnp.zeros((4, block.shape[1]), block.dtype)
            out_ref[2 * triplet, member, 12:16] = fill
            out_ref[2 * triplet + 1, member, 12:16] = fill
        out_ref[2 * triplet, 3] = phase_ref[triplet]
        out_ref[2 * triplet + 1, 3] = phase_ref[triplet]


def whole_record(members_ref, slot):
    parts = [members_ref[j, slot].astype(jnp.float32)[0:12] for j in range(8)]
    rows = jnp.concatenate(parts, axis=0)
    fill = jnp.zeros((WIDE, 38), jnp.float32)
    return jnp.concatenate([rows[:, 0:90], fill, rows[:, 90:180], fill], axis=1)


def operand_kernel(
    where_ref, members_ref, early_ref, late_ref, middle_ref, last_ref, tables_ref, scalars_ref
):
    rank, first, mult = where_ref[0], where_ref[1] == 0, where_ref[2]
    f32 = jnp.float32
    records = [whole_record(members_ref, member) for member in range(3)]
    lead_r, lead_i = records[0][:, 0:128].T, records[0][:, 128:256].T

    def halves(array):
        low, high = array[0:PAD], array[45 : 45 + PAD]
        return jnp.where(first, low, high), jnp.where(first, high, low)

    def sides(array):
        low, high = array[:, 0:PAD], array[:, 45 : 45 + PAD]
        return jnp.where(first, low, high), jnp.where(first, high, low)

    row = lax.broadcasted_iota(jnp.int32, (PAD, WIDE), 0)
    column = lax.broadcasted_iota(jnp.int32, (PAD, WIDE), 1)

    def spread(array, start, count):
        taken = (column // 2 + start == row) & (column < 2 * count)
        return jnp.dot(array, taken.astype(f32), preferred_element_type=f32)

    def turned(real, imag, offset):
        trig = members_ref[2 * ((rank + offset) & 3), 3].astype(f32)
        even = lax.broadcasted_iota(jnp.int32, (1, real.shape[1]), 1) % 2 == 0
        cosine = jnp.where(even, trig[0:1, 0:1], trig[0:1, 2:3])
        sine = jnp.where(even, trig[0:1, 1:2], trig[0:1, 3:4])
        return jnp.concatenate([cosine * real - sine * imag, cosine * imag + sine * real], axis=0)

    columns = []
    for array in (lead_r, lead_i):
        columns.append([halves(side) for side in sides(array)])
    whole = [[spread(columns[i][0][h], 0, 45) for i in range(2)] for h in range(2)]
    early_ref[...] = jnp.concatenate(
        [
            jnp.concatenate([turned(*whole[h], offset) for h in range(2)], axis=0)
            for offset in (0, 3, 1)
        ],
        axis=1,
    ).astype(early_ref.dtype)
    parts = []
    for side in range(2):
        for start, count in ((0, TOP), (TOP, 45 - TOP)):
            real, imag = (spread(columns[i][side][0], start, count)[:, 0:PAD] for i in range(2))
            parts.append(turned(real, imag, 2))
    late_ref[...] = jnp.concatenate(parts, axis=1).astype(late_ref.dtype)

    mid_r, mid_i = records[1][:, 0:128].T, records[1][:, 128:256].T
    within = lax.broadcasted_iota(jnp.int32, (WIDE, WIDE), 1) < 90
    real = jnp.where(within, mid_r[0:WIDE], 0.0)
    imag = jnp.where(within, mid_i[0:WIDE], 0.0)
    middle_ref[...] = jnp.concatenate(
        [jnp.concatenate([real, -imag], axis=1), jnp.concatenate([imag, real], axis=1)], axis=0
    ).astype(middle_ref.dtype)

    last_r, last_i = records[2][:, 0:128], records[2][:, 128:256]
    within = lax.broadcasted_iota(jnp.int32, (WIDE, 128), 0) < 90
    real = jnp.where(within, last_r, 0.0)
    imag = jnp.where(within, last_i, 0.0)
    zeros = jnp.zeros((32, 256), f32)
    last_ref[...] = jnp.concatenate(
        [
            jnp.concatenate([real, imag], axis=1),
            zeros,
            jnp.concatenate([-imag, real], axis=1),
            zeros,
        ],
        axis=0,
    ).astype(last_ref.dtype)

    row = lax.broadcasted_iota(jnp.int32, (WIDE, 128), 0)
    column = lax.broadcasted_iota(jnp.int32, (WIDE, 128), 1)
    one = jnp.where(row < 90, jnp.broadcast_to(mid_r[0:WIDE, 90:91], (WIDE, 128)), 1.0)
    two = jnp.where(column < 90, jnp.broadcast_to(last_r[90:91, :], (WIDE, 128)), 1.0)
    tables_ref[0] = one + two
    tables_ref[1] = one - two
    tables_ref[2] = 1.0 / (one * two)
    tables_ref[3] = jnp.broadcast_to(mid_i[0:WIDE, 90:91], (WIDE, 128)) + jnp.broadcast_to(
        last_i[90:91, :], (WIDE, 128)
    )
    zero = halves(lead_r[:, 90:91])[0]
    zero = jnp.where(lax.broadcasted_iota(jnp.int32, (PAD, 1), 0) < 45, zero, 1.0)
    scalars_ref[0] = jnp.broadcast_to(zero, (PAD, 128))
    scalars_ref[1] = jnp.broadcast_to(mult.astype(f32) / zero, (PAD, 128))


def rows_of(ref, cols, count):
    values = ref[:, :, cols]
    rows = values.shape[0] * values.shape[1]
    return jnp.pad(values.reshape(rows, values.shape[2]), ((0, count - rows), (0, 0)))


def early_kernel(lead_ref, own_ref, low_ref, high_ref, mine_ref, *far_refs):
    total = own_ref.shape[2]
    for start in range(0, total, CHUNK):
        cols = slice(start, min(start + CHUNK, total))
        product = jnp.dot(
            lead_ref[...],
            jnp.concatenate([rows_of(ref, cols, WIDE) for ref in (own_ref, low_ref, high_ref)], axis=0),
            preferred_element_type=jnp.float32,
        )
        mine_ref[:, cols] = product[0:WIDE].astype(mine_ref.dtype)
        for i, far_ref in enumerate(far_refs):
            rows = product[WIDE + 48 * i : WIDE + 48 * i + 48]
            far_ref[:, cols] = rows.astype(far_ref.dtype)


def interaction_kernel(*refs):
    count = 12
    operands, out_ref, buffers = refs[:count], refs[count], refs[count + 1 : 2 * count + 1]
    flat, windows, mid_real, mid_imag, rate_acc, couple_acc, done = refs[2 * count + 1 :]
    scalars_ref, middle_ref, last_ref, tables_ref, late_ref = buffers[:5]
    top_ref, bottom_ref, far_top_ref, far_bottom_ref, mine_ref = buffers[5:10]
    late, others = buffers[5:9], buffers[10:]
    total = mine_ref.shape[1]
    pieces = [slice(at, min(at + CHUNK, total)) for at in range(0, total, CHUNK)]
    whole = {}
    for i in range(5):
        whole[i] = pltpu.make_async_copy(operands[i], buffers[i], done.at[i, 0])
    parts = {}
    for k, cols in enumerate(pieces):
        for i in range(5, count):
            where = (slice(None),) * (len(operands[i].shape) - 1) + (cols,)
            parts[i, k] = pltpu.make_async_copy(
                operands[i].at[where], buffers[i].at[where], done.at[i, k]
            )
    whole[4].start()
    for i in range(5, count):
        parts[i, 0].start()
    whole[2].start()
    for k in range(1, len(pieces)):
        for i in range(5, count):
            parts[i, k].start()
    for i in (0, 1, 3):
        whole[i].start()

    flat[:, 8064:8320] = jnp.zeros((WIDE, 256), flat.dtype)
    zeros = jnp.zeros((PAD, 128), jnp.float32)
    for b in range(90, WIDE):
        mid_real[pl.ds(b, PAD, stride=WIDE), :] = zeros
        mid_imag[pl.ds(b, PAD, stride=WIDE), :] = zeros

    def window_of(b):
        tile, shift = divmod(90 * b, 128)
        pair = flat[:, tile * 128 : tile * 128 + 256]
        window = pair[:, shift : shift + 128]
        windows[b * PAD : (b + 1) * PAD, 0:128] = window[0:PAD]
        windows[b * PAD : (b + 1) * PAD, 128:256] = window[PAD:]

    def product_of(group):
        product = jnp.dot(
            windows[group * 480 : (group + 1) * 480, :],
            last_ref[...],
            preferred_element_type=jnp.float32,
        )
        for i in range(10):
            rows = pl.ds(group * 10 + i, PAD, stride=WIDE)
            mid_real[rows, :] = product[i * PAD : (i + 1) * PAD, 0:128]
            mid_imag[rows, :] = product[i * PAD : (i + 1) * PAD, 128:256]

    whole[4].wait()
    b = 0
    for k, cols in enumerate(pieces):
        for i in range(5, count):
            parts[i, k].wait()
        if k == 0:
            whole[2].wait()
        other = jnp.concatenate([ref[:, cols].astype(jnp.float32) for ref in others], axis=0)
        both = mine_ref[:, cols].astype(jnp.float32) + other
        both = both + jnp.dot(
            late_ref[...],
            jnp.concatenate([rows_of(ref, cols, PAD) for ref in late], axis=0),
            preferred_element_type=jnp.float32,
        )
        flat[:, cols] = both.astype(flat.dtype)
        ready = 8320 if cols.stop == total else cols.stop
        while b < 90 and 90 * b // 128 * 128 + 256 <= ready:
            window_of(b)
            b += 1
            if b % 10 == 0:
                product_of(b // 10 - 1)
    for i in (0, 1, 3):
        whole[i].wait()

    scaled = 0.5 / (smearing * smearing)
    def two_modes(s):
        low = pl.ds(s * WIDE, WIDE)
        high = pl.ds(s * WIDE + WIDE, WIDE)
        operand = jnp.concatenate(
            [
                jnp.concatenate([ref[low, :], ref[high, :]], axis=1).astype(jnp.bfloat16)
                for ref in (mid_real, mid_imag)
            ],
            axis=0,
        )
        value = jnp.dot(middle_ref[...], operand, preferred_element_type=jnp.float32)
        for i in range(2):
            real = value[0:WIDE, 128 * i : 128 * i + 128]
            imag = value[WIDE:, 128 * i : 128 * i + 128]
            freq = scalars_ref[0, pl.ds(s + i, 1), :]
            decays = freq - tables_ref[0]
            merges = freq + tables_ref[1]
            weight = (real * real + imag * imag) * (
                jnp.exp(-scaled * decays * decays) + jnp.exp(-scaled * merges * merges)
            )
            weight = weight * tables_ref[2] * scalars_ref[1, pl.ds(s + i, 1), :]
            at = pl.ds((s + i) * 8, 8)
            rate_acc[at, :] = jnp.sum(weight.reshape(WIDE // 8, 8, 128), axis=0)
            weight = weight * tables_ref[3]
            couple_acc[at, :] = jnp.sum(weight.reshape(WIDE // 8, 8, 128), axis=0)

    for i in range(24):
        two_modes(2 * i)

    sums = jnp.concatenate(
        [
            jnp.sum(rate_acc[...].reshape(PAD, 8, 128), axis=1),
            jnp.sum(couple_acc[...].reshape(PAD, 8, 128), axis=1),
        ],
        axis=0,
    )
    out_ref[:, 0:WIDE] = lax.dot_general(
        jnp.ones((8, 128), jnp.float32),
        sums,
        (((1,), (1,)), ((), ())),
        precision=lax.Precision.HIGHEST,
        preferred_element_type=jnp.float32,
    )[0:1]
    out_ref[:, WIDE:128] = jnp.zeros((1, 128 - WIDE), jnp.float32)


VMEM = pl.BlockSpec(memory_space=pltpu.VMEM)
SMEM = pl.BlockSpec(memory_space=pltpu.SMEM)
PARAMS = pltpu.CompilerParams(vmem_limit_bytes=56 << 20)


def ring(count, step):
    return [(i, (i + step) % count) for i in range(count)]


def body(
    force_third,
    phase_angle,
    eigenvectors,
    frequencies,
    deviation,
    send_rows,
    trip_table,
    irreducible,
    multiplicity,
    drive_term,
    boundary,
):
    f32, b16 = jnp.float32, jnp.bfloat16
    clus = lax.axis_index("clus")
    mode = lax.axis_index("mode")
    group = ("clus", "mode")

    with jax.named_scope("records"):
        extra = jnp.concatenate([frequencies, deviation], axis=1)[:, None, :]
        record = jnp.concatenate(
            [eigenvectors, extra, jnp.zeros((extra.shape[0], 5, 180), b16)], axis=1
        )
        share = lax.dynamic_slice_in_dim(record, 12 * (2 * clus + mode), 12, 1)
        chosen = pl.pallas_call(
            send_kernel,
            out_shape=jax.ShapeDtypeStruct((send_rows.shape[1],) + share.shape[1:], b16),
            in_specs=[SMEM, VMEM],
            out_specs=VMEM,
            compiler_params=PARAMS,
        )(send_rows, share)
        arrived = lax.all_to_all(chosen, "trip", 0, 0, tiled=True)
        angles = phase_angle.astype(f32)
        trig = jnp.stack([jnp.cos(angles), jnp.sin(angles)], axis=1).astype(b16)
        phases = jnp.pad(trig.reshape(4, 4).T[:, None, :], ((0, 0), (0, 15), (0, 176)))

    with jax.named_scope("force"):
        own = jnp.transpose(force_third, (1, 0, 2))
        low = lax.ppermute(own, "clus", ring(4, 1))
        high = lax.ppermute(own, "clus", ring(4, 3))

    with jax.named_scope("members"):
        picks = pl.pallas_call(
            pick_kernel,
            out_shape=jax.ShapeDtypeStruct((8, 4, 16, 180), b16),
            in_specs=[SMEM, VMEM, VMEM],
            out_specs=VMEM,
            compiler_params=PARAMS,
        )(trip_table, arrived, phases)
        members = lax.all_to_all(picks, group, 0, 0, tiled=True)

    with jax.named_scope("force_second"):
        low_top, high_bottom, _ = lax.optimization_barrier((low[:TOP], high[TOP:], members))
        top = lax.ppermute(low_top, "clus", ring(4, 1))
        bottom = lax.ppermute(high_bottom, "clus", ring(4, 3))

    with jax.named_scope("operands"):
        mult = lax.dynamic_index_in_dim(multiplicity, clus, 0, keepdims=False)
        where = jnp.stack([clus, mode, mult]).astype(jnp.int32)
        early, late, mid, last_all, tables, scalars = pl.pallas_call(
            operand_kernel,
            out_shape=(
                jax.ShapeDtypeStruct((2 * WIDE, 3 * WIDE), b16),
                jax.ShapeDtypeStruct((WIDE, 4 * PAD), b16),
                jax.ShapeDtypeStruct((2 * WIDE, 2 * WIDE), b16),
                jax.ShapeDtypeStruct((256, 256), b16),
                jax.ShapeDtypeStruct((4, WIDE, 128), f32),
                jax.ShapeDtypeStruct((2, PAD, 128), f32),
            ),
            in_specs=[SMEM, VMEM],
            out_specs=(VMEM,) * 6,
            compiler_params=PARAMS,
        )(where, members)

    with jax.named_scope("contract"):
        total = force_third.shape[2]
        swap = [(0, 1), (1, 0)]
        mine, *far = pl.pallas_call(
            early_kernel,
            out_shape=(jax.ShapeDtypeStruct((WIDE, total), b16),)
            + (jax.ShapeDtypeStruct((WIDE // 2, total), b16),) * 2,
            in_specs=[VMEM] * 4,
            out_specs=(VMEM,) * 3,
            compiler_params=PARAMS,
            cost_estimate=pl.CostEstimate(
                flops=2 * 192 * 288 * total, bytes_accessed=1200 * total, transcendentals=0
            ),
        )(early, own, low, high)
        other = [lax.ppermute(rows, "mode", swap) for rows in far]
        far_top = lax.ppermute(top, "mode", swap)
        far_bottom = lax.ppermute(bottom, "mode", swap)

    with jax.named_scope("interaction"):
        inputs = (scalars, mid, last_all, tables, late, top, bottom, far_top, far_bottom, mine, *other)
        sums = pl.pallas_call(
            interaction_kernel,
            out_shape=jax.ShapeDtypeStruct((1, 128), f32),
            in_specs=[pl.BlockSpec(memory_space=pl.ANY)] * len(inputs),
            out_specs=VMEM,
            scratch_shapes=[pltpu.VMEM(x.shape, x.dtype) for x in inputs]
            + [
                pltpu.VMEM((WIDE, 8320), b16),
                pltpu.VMEM((90 * PAD, 256), b16),
                pltpu.VMEM((PAD * WIDE, 128), f32),
                pltpu.VMEM((PAD * WIDE, 128), f32),
                pltpu.VMEM((8 * PAD, 128), f32),
                pltpu.VMEM((8 * PAD, 128), f32),
                pltpu.SemaphoreType.DMA((len(inputs), 4)),
            ],
            compiler_params=PARAMS,
        )(*inputs)
    with jax.named_scope("collect"):
        points = jnp.arange(32, dtype=jnp.int32)
        mine_is = points == lax.dynamic_index_in_dim(irreducible, clus, 0, keepdims=False)
        partial = jnp.where(mine_is[None, :, None], sums[None], 0.0)
        partial = jnp.broadcast_to(partial, (4, 32, 128)).reshape(128, 1, 128)
        received = lax.all_to_all(partial, ("clus", "trip"), 0, 0, tiled=True)
        final = jnp.sum(received[:, 0, :], axis=0)[None, :]
        gamma_total = final[:, 0:45] + boundary
        return gamma_total, (drive_term + final[:, PAD : PAD + 45]) / gamma_total


def solution(mesh):
    return jax.shard_map(
        body,
        mesh=mesh,
        in_specs=(
            P("clus", "mode", None),
            P("clus", "trip"),
            P("trip", None, None),
            P("trip", None),
            P("trip", None),
            P("trip", None),
            P("trip", None),
            P("trip"),
            P("trip"),
            P("trip", "mode"),
            P("trip", "mode"),
        ),
        out_specs=(P("trip", "mode"), P("trip", "mode")),
        check_vma=False,
    )
```
